32 devices in a mesh: mesh: 16 (over z, y, x), obs: 2 (over core).
Axes of the slice: x: 2, y: 2, z: 4, core: 2. Of those that a mesh axis runs over, the one named last changes fastest.
Arguments:
- probes: bfloat16 [64, 128, 512], P(None, 'mesh', 'obs'), may hold values from -6 to 6
- velocity: float32 [128, 512], P('mesh', 'obs'), may hold values from 0.5 to 2
- viscosity: float32 [128, 512], P('mesh', 'obs'), may hold values from 0.1 to 3
- friction: float32 [128, 512], P('mesh', 'obs'), may hold values from 0.5 to 4
- obs_block: int32 [16, 128], P('mesh', 'obs'), may hold values from 0 to 31
- obs_weight: float32 [16, 128, 128], P('mesh', 'obs'), may hold values from -0.5 to 0.5
- obs_prec: float32 [16, 128], P('mesh', 'obs'), may hold values from 0.05 to 0.5
- rank: int32 [1], replicated, may hold values from 1 to 64
Outputs:
- basis: float32 [64, 128, 512], P(None, 'mesh', 'obs')
- factor: float32 [64, 64], replicated
The draws below stay inside these ranges and needn't reach their ends.
All inputs are finite; a program needn't handle non-finite values.
Results may differ from the reference program's by a relative error of at most 0.0027.
Values may be sent and summed in bfloat16 or wider, within the bound.
No kernel may reach another device: no remote copies, remote signals or barrier semaphores. Data moves between devices by JAX's collectives and lax.ppermute only.
A program may use at most 64 MiB of HBM per device.

```python
import math
import jax
import jax.numpy as jnp
from jax import lax

P_SIZE = 64
BLOCK = 128
SLABS = 16
NX = 128
NZ = 512
OBS_SLAB = 128
NBLK = 32
CELLS = 65536


def plant(values, key, low, largest):
    dims = values.shape
    spot = [jax.random.randint(jax.random.fold_in(key, axis), (), 0, dims[axis]) for axis in range(len(dims))]
    values = values.at[tuple(spot)].set(low)
    longest = dims.index(max(dims))
    spot[longest] = (spot[longest] + 1) % dims[longest]
    return values.at[tuple(spot)].set(largest)


def level_of(own_key, extent, shards, low, top_value):
    level, own = 1.0, jax.random.fold_in(own_key, 6)
    for axis_at, parts in shards:
        heights = jnp.exp(jax.random.uniform(jax.random.fold_in(own, axis_at), (parts,), jnp.float32, low / len(shards), top_value / len(shards)))
        level = level * jnp.repeat(heights, extent[axis_at] // parts).reshape([-1 if axis == axis_at else 1 for axis in range(len(extent))])
    return level


def normal_values(rng, dims, spread, most, cuts=(), kind=jnp.bfloat16):
    loudness = level_of(rng, dims, cuts, -0.22, 0.18) if cuts else 1.0
    values = jax.random.normal(rng, dims, jnp.float32) * spread * loudness
    return jnp.minimum(jnp.maximum(values, -most), most).astype(kind)


def setup_inputs(seed: int = 0) -> dict:
    key_of = jax.random.split(jax.random.key(seed), 9)
    probes = normal_values(key_of[0], (P_SIZE, NX, NZ), 1.0, 6.0, ((1, 16), (2, 2)))
    velocity = jnp.clip(jnp.exp(math.log(2.0) - 1.3862944 * jax.random.uniform(key_of[1], (NX, NZ), jnp.float32) ** level_of(key_of[1], (NX, NZ), ((0, 16), (1, 2)), -0.2, 0.2)), 0.5, 2.0)
    viscosity = jnp.clip(jnp.exp(math.log(3.0) - 3.4011974 * jax.random.uniform(key_of[2], (NX, NZ), jnp.float32) ** level_of(key_of[2], (NX, NZ), ((0, 16), (1, 2)), -0.2, 0.2)), 0.1, 3.0)
    friction = jnp.clip(jnp.exp(math.log(4.0) - 2.0794415 * jax.random.uniform(key_of[3], (NX, NZ), jnp.float32) ** level_of(key_of[3], (NX, NZ), ((0, 16), (1, 2)), -0.2, 0.2)), 0.5, 4.0)
    obs_block = plant(jax.random.randint(key_of[4], (SLABS, OBS_SLAB), 0, NBLK), jax.random.fold_in(key_of[4], 1), 0, NBLK - 1).astype(jnp.int32)
    obs_weight = normal_values(key_of[5], (SLABS, OBS_SLAB, BLOCK), BLOCK ** -0.5, 0.5, ((0, 16), (1, 2)), jnp.float32)
    obs_prec = jnp.clip(jnp.exp(math.log(0.5) - 2.3025851 * jax.random.uniform(key_of[6], (SLABS, OBS_SLAB), jnp.float32) ** level_of(key_of[6], (SLABS, OBS_SLAB), ((0, 16), (1, 2)), -0.2, 0.2)), 0.05, 0.5)
    rank = jax.random.randint(key_of[7], (1,), 1, P_SIZE + 1).astype(jnp.int32)
    return dict(probes=probes, velocity=velocity, viscosity=viscosity, friction=friction, obs_block=obs_block, obs_weight=obs_weight, obs_prec=obs_prec, rank=rank)


PRIOR = 1.0

def apply_padded(padded, visc_pad, friction):
    height = padded.shape[1] - 2
    width = padded.shape[2] - 2
    centre = padded[:, 1:-1, 1:-1]
    visc_mid = visc_pad[1:-1, 1:-1]
    result = friction * centre
    for shift_row, shift_col in ((2, 1), (0, 1), (1, 2), (1, 0)):
        neighbor = padded[:, shift_row:shift_row + height, shift_col:shift_col + width]
        face_coef = 0.5 * (visc_mid + visc_pad[shift_row:shift_row + height, shift_col:shift_col + width])
        result = result + face_coef * (centre - neighbor)
    return result

def operate(field, viscosity, friction):
    padded = jnp.pad(field, ((0, 0), (1, 1), (1, 1)))
    visc_pad = jnp.pad(viscosity, 1)
    return apply_padded(padded, visc_pad, friction)

def reference(probes, velocity, viscosity, friction, obs_block, obs_weight, obs_prec, rank):
    omega = probes.astype(jnp.float32)
    tangent = operate(velocity * omega, viscosity, friction).astype(jnp.bfloat16)
    blocks = tangent.astype(jnp.float32).reshape(P_SIZE, SLABS, NBLK, BLOCK)
    picked = jnp.take_along_axis(blocks, obs_block[None, :, :, None], axis=2)
    misfit = obs_prec[None] * jnp.sum(picked * obs_weight[None], axis=-1)
    contrib = misfit[..., None] * obs_weight[None]
    slab_ids = jnp.broadcast_to(jnp.arange(SLABS, dtype=jnp.int32)[:, None], (SLABS, OBS_SLAB))
    source = jnp.zeros((P_SIZE, SLABS, NBLK, BLOCK), jnp.float32).at[:, slab_ids, obs_block].add(contrib)
    source = source.reshape(P_SIZE, NX, NZ)
    gradient = velocity * operate(source, viscosity, friction)
    sketch = (gradient + PRIOR * omega).reshape(P_SIZE, CELLS)
    gram = jnp.dot(sketch.astype(jnp.float32), sketch.T.astype(jnp.float32), precision=lax.Precision.HIGHEST, preferred_element_type=jnp.float32) / CELLS
    factor = jnp.linalg.cholesky(gram)
    solved = lax.linalg.triangular_solve(factor, sketch, left_side=True, lower=True)
    retained = (jnp.arange(P_SIZE, dtype=jnp.int32) < rank[0])[:, None]
    basis = jnp.where(retained, solved, 0.0).reshape(P_SIZE, NX, NZ)
    return (basis, factor)
```

```python
import functools

import jax
import jax.numpy as jnp
from jax import lax
from jax.experimental import pallas as pl
from jax.experimental.pallas import tpu as pltpu
from jax.sharding import PartitionSpec as P

LANES = 128
RIGHT = 16
PAD = 8
F32 = jnp.float32
BF16 = jnp.bfloat16


def split(x):
    high = x.astype(BF16)
    return high, (x - high.astype(F32)).astype(BF16)


def lane_of(shape):
    return lax.broadcasted_iota(jnp.int32, shape, 1)


def row_of(shape):
    return lax.broadcasted_iota(jnp.int32, shape, 0)


def dot(a, b, rhs_dim=0):
    return lax.dot_general(
        a, b, (((1,), (rhs_dim,)), ((), ())), preferred_element_type=F32
    )


def call(body, outs, args, scratch=(), flops=0, name=None):
    outs = [jax.ShapeDtypeStruct(shape, kind) for shape, kind in outs]
    return pl.pallas_call(
        body,
        out_shape=outs,
        scratch_shapes=list(scratch),
        compiler_params=pltpu.CompilerParams(vmem_limit_bytes=8 * 2**20),
        cost_estimate=pl.CostEstimate(
            flops=flops, bytes_accessed=2**20, transcendentals=0
        ),
        name=name,
    )(*args)


def shifted(x, left_edge, right_edge):
    lane = lane_of(x.shape)
    width = x.shape[1]
    left = jnp.where(lane == 0, left_edge, pltpu.roll(x, 1, 1))
    right = jnp.where(lane == width - 1, right_edge, pltpu.roll(x, width - 1, 1))
    return left, right


def operate_row(centre, above, below, left, right, visc, friction):
    own, *others = visc
    faces = [0.5 * (own + other) for other in others]
    result = (friction + faces[0] + faces[1] + faces[2] + faces[3]) * centre
    for face, value in zip(faces, (above, below, left, right)):
        result = result - face * value
    return result


def tangent_row(count, centre, above, below, left_edge, right_edge, friction):
    left, right = shifted(centre, left_edge, right_edge)
    visc = [x[count : count + 1] for x in (centre, above, below, left, right)]
    values = [x[:count] for x in (centre, above, below, left, right)]
    return operate_row(*values, visc, friction).astype(BF16)


def edge_columns(rows):
    height, width = rows[0].shape
    lane = lane_of((height, LANES))
    out = jnp.zeros((height, LANES), F32)
    for at, x in enumerate(rows):
        out = jnp.where(lane == at, x[:, :1], out)
        out = jnp.where(lane == RIGHT + at, x[:, width - 1 :], out)
    return out


def edges_from(left_ref, right_ref, rows, at):
    here, last = lax.axis_index("obs"), lax.axis_size("obs") - 1
    left = left_ref[rows, RIGHT + at : RIGHT + at + 1]
    right = right_ref[rows, at : at + 1]
    return jnp.where(here > 0, left, 0.0), jnp.where(here < last, right, 0.0)


def sources(tangents, grid_rows, observed, slab_columns):
    count, width = tangents[0].shape
    owned = width // LANES
    first = lax.axis_index("obs") * owned
    blocks = jnp.concatenate(
        [t[:, c * LANES : (c + 1) * LANES] for t in tangents for c in range(owned)], axis=0
    )
    doubled = jnp.concatenate([blocks, blocks], axis=1)
    total = None
    for at in range(0, len(observed), 2):
        pair = observed[at : at + 2]
        if len(pair) == 1:
            pair = pair + [tuple(jnp.zeros_like(x) for x in pair[0])]
        high = jnp.concatenate([x[0] for x in pair], axis=0)
        low = jnp.concatenate([x[1] for x in pair], axis=0)
        share = pair[0][0].shape[0]
        lane = lane_of((1, LANES))
        ids = jnp.where(lane < share, pair[0][2], pltpu.roll(pair[1][2], share, 1))
        ids = ids.astype(jnp.int32)
        precision = jnp.where(lane < share, pair[0][3], pltpu.roll(pair[1][3], share, 1))
        misfit = dot(doubled, jnp.concatenate([high, low], axis=1), 1)
        kept = []
        for i, row in enumerate(grid_rows):
            for c in range(owned):
                k = i * owned + c
                scale = jnp.where(ids == row * slab_columns + first + c, precision, 0.0)
                kept.append(misfit[k * count : (k + 1) * count] * scale)
        misfit_high, misfit_low = split(jnp.concatenate(kept, axis=0))
        both = dot(
            jnp.concatenate([misfit_high, misfit_low], axis=1),
            jnp.concatenate(
                [
                    jnp.concatenate([high, low], axis=1),
                    jnp.concatenate([high, jnp.zeros_like(low)], axis=1),
                ],
                axis=0,
            ),
        )
        part = both[:, :LANES] + both[:, LANES:]
        total = part if total is None else total + part
    return [
        jnp.concatenate(
            [total[(i * owned + c) * count : (i * owned + c + 1) * count] for c in range(owned)],
            axis=1,
        )
        for i in range(len(tangents))
    ]


def own_share(weight_ref, ids_ref, precision_ref):
    share = weight_ref.shape[1]
    out = jnp.zeros((PAD, LANES), F32)
    row, lane = row_of(out.shape), lane_of(out.shape)

    def wide(x):
        return jnp.concatenate([x, jnp.zeros((1, LANES - share), F32)], axis=1)

    out = jnp.where(row == 0, wide(ids_ref[...].astype(F32)), out)
    return jnp.where(row == 1, wide(precision_ref[...]), out)


def read_share(ref, at, share):
    weight = ref[at : at + share, :]
    high, low = split(weight)
    return high, low, ref[at + share : at + share + 1, :], ref[at + share + 1 : at + share + 2, :]


def edges_kernel(probes, velocity, viscosity, friction, weight, ids, precision, omega, up, down, turned, small):
    count, rows, width = probes.shape
    share = weight.shape[1]
    for c in range(width // LANES):
        lanes = slice(c * LANES, (c + 1) * LANES)
        turned[c] = probes[:, :, lanes].astype(F32).reshape(count * rows, LANES)
        for r in range(rows):
            omega[r * count : (r + 1) * count, lanes] = turned[c, pl.ds(r, count, stride=rows), :]
    meta = own_share(weight, ids, precision)
    weight_high, weight_low = split(weight[0])
    for out, near, next_near in ((up, 0, 1), (down, rows - 1, rows - 2)):
        out[:count, :] = omega[near * count : (near + 1) * count, :].astype(BF16)
        out[count : 2 * count, :] = omega[next_near * count : (next_near + 1) * count, :].astype(BF16)
        out[2 * count : 2 * count + share, :] = jnp.concatenate([weight_high, weight_low], axis=1)
        small[...] = jnp.zeros_like(small)
        at = 0
        for ref, r in (
            (velocity, near),
            (velocity, next_near),
            (viscosity, near),
            (viscosity, next_near),
            (friction, near),
        ):
            value = ref[r : r + 1, :]
            high = value.astype(BF16).astype(F32)
            small[at : at + 1, :] = high
            small[at + 1 : at + 2, :] = value - high
            at += 2
        small[at : at + 1, :LANES] = meta[0:1]
        high = meta[1:2].astype(BF16).astype(F32)
        small[at + 1 : at + 2, :LANES] = high
        small[at + 2 : at + 3, :LANES] = meta[1:2] - high
        out[2 * count + share :, :] = small[...].astype(BF16)


def forced_kernel(omega, velocity, viscosity, weight, ids, precision, forced, sent):
    rows, width = velocity.shape
    count = omega.shape[0] // rows
    share = weight.shape[1]
    blocks = []
    first = row_of((PAD, width)) == 0
    for r in range(rows):
        block = jnp.concatenate(
            [
                velocity[r : r + 1, :] * omega[r * count : (r + 1) * count, :],
                jnp.where(first, viscosity[r : r + 1, :], 0.0),
            ],
            axis=0,
        )
        forced[r] = block
        blocks.append(block)
    sent[: count + PAD, :] = edge_columns(blocks)
    sent[count + PAD : count + PAD + share, :] = weight[0]
    sent[count + PAD + share :, :] = own_share(weight, ids, precision)


def shares_of(refs, at, share):
    return [read_share(ref, at, share) for ref in refs]


def inner_kernel(slab_columns, share, forced, friction, from_left, from_right, *rest):
    *observed, out = rest
    rows, height, width = forced.shape
    count = height - PAD
    tangents = []
    inner = range(1, rows - 1)
    for r in inner:
        edges = edges_from(from_left, from_right, slice(0, height), r)
        tangents.append(
            tangent_row(count, forced[r], forced[r - 1], forced[r + 1], *edges, friction[r : r + 1, :])
        )
    result = sources(tangents, inner, shares_of(observed, height, share), slab_columns)
    for i, x in enumerate(result):
        out[i * count : (i + 1) * count, :] = x


def received(ref, count, share):
    small = ref[2 * count + share :, :].astype(F32)
    parts = [small[i : i + 1] + small[i + 1 : i + 2] for i in range(0, 10, 2)]
    return parts, small[10:11, :LANES], small[11:12, :LANES] + small[12:13, :LANES]


def far_kernel(count, share, from_up, from_down, near, sent):
    blocks = []
    edge = lax.axis_index("mesh"), lax.axis_size("mesh") - 1
    width = from_up.shape[1]
    first = row_of((PAD, width)) == 0
    at = count + PAD
    for i, (ref, inside) in enumerate(((from_up, edge[0] > 0), (from_down, edge[0] < edge[1]))):
        (velocity, _, viscosity, _, _), ids, precision = received(ref, count, share)
        block = jnp.concatenate(
            [velocity * ref[:count, :].astype(F32), jnp.where(first, viscosity, 0.0)], axis=0
        )
        block = jnp.where(inside, block, 0.0)
        near[i] = block
        blocks.append(block)
        both = ref[2 * count : 2 * count + share, :].astype(F32)
        sent[at : at + share, :] = both[:, :LANES] + both[:, LANES:]
        row = row_of((PAD, LANES))
        sent[at + share : at + share + PAD, :] = jnp.where(
            row == 0, ids, jnp.where(row == 1, precision, 0.0)
        )
        at += share + PAD
    sent[: count + PAD, :] = edge_columns(blocks)


def outer_kernel(slab_columns, share, forced, near, friction, from_left, from_right, inner, *rest):
    *observed, out, sent = rest
    rows, height, width = forced.shape
    count = height - PAD
    tangents = []
    outer = (0, rows - 1)
    for r in outer:
        edges = edges_from(from_left, from_right, slice(0, height), r)
        above = near[0] if r == 0 else forced[r - 1]
        below = near[1] if r == rows - 1 else forced[r + 1]
        tangents.append(tangent_row(count, forced[r], above, below, *edges, friction[r : r + 1, :]))
    first, last = sources(tangents, outer, shares_of(observed, height, share), slab_columns)
    out[:count, :] = first
    out[count:, :] = last
    middle = [inner[i * count : (i + 1) * count, :] for i in range(rows - 2)]
    sent[...] = edge_columns([first, *middle, last])


def halo_kernel(slab_columns, share, forced, near, from_up, from_down, from_left, from_right, *rest):
    *observed, out = rest
    rows, height, width = forced.shape
    count = height - PAD
    here, last = lax.axis_index("mesh"), lax.axis_size("mesh") - 1
    for i, ref in enumerate((from_up, from_down)):
        (_, velocity, _, viscosity, friction), _, _ = received(ref, count, share)
        far = jnp.concatenate(
            [
                velocity * ref[count : 2 * count, :].astype(F32),
                jnp.broadcast_to(viscosity, (PAD, width)),
            ],
            axis=0,
        )
        own = forced[rows - 1 if i else 0]
        above, below = (own, far) if i else (far, own)
        edges = edges_from(from_left, from_right, slice(0, height), i)
        tangent = tangent_row(count, near[i], above, below, *edges, friction)
        at = height + i * (share + PAD)
        (source,) = sources(
            [tangent], (0 if i else rows - 1,), shares_of(observed, at, share), slab_columns
        )
        inside = here < last if i else here > 0
        out[i * count : (i + 1) * count, :] = jnp.where(inside, source, 0.0)


def packed(gram):
    half = gram.shape[0] // 2
    top, bottom = gram[:half], gram[half:]
    row, lane = row_of(top.shape), lane_of(top.shape) % (2 * half)
    mixed = jnp.where((lane >= half) & (row >= lane - half), pltpu.roll(top, half, 1), bottom)
    quarter = half // 2
    body = jnp.where(lane_of((quarter, LANES)) < 2 * half, mixed[:quarter], mixed[quarter:])
    diagonal = jnp.sum(jnp.where(row == lane - half, bottom, 0.0), axis=0, keepdims=True)
    return body, diagonal


def unpacked(body, diagonal):
    quarter = body.shape[0]
    half, size = 2 * quarter, 4 * quarter
    lane = lane_of(body.shape)
    turned = pltpu.roll(body, size, 1)
    mixed = jnp.concatenate(
        [jnp.where(lane < size, body, turned), jnp.where(lane < size, turned, body)], axis=0
    )
    row, lane = row_of(mixed.shape), lane_of(mixed.shape)
    top = pltpu.roll(mixed, LANES - half, 1)
    lower = jnp.concatenate(
        [
            jnp.where(row > lane, top, 0.0),
            jnp.where((lane < half) | ((lane < size) & (row < lane - half)), mixed, 0.0),
        ],
        axis=0,
    )
    spread = jnp.concatenate(
        [
            jnp.where(row == lane, top, 0.0),
            jnp.where(row == lane - half, diagonal, 0.0),
        ],
        axis=0,
    )
    square = jnp.concatenate([lower, jnp.zeros((LANES - size, LANES), F32)], axis=0)
    return lower + square.T[:size] + spread


def sketch_kernel(
    cells, forced, near, omega, velocity, friction, visc_left, visc_right,
    from_left, from_right, inner, outer, halo, sketch, gram, gram_diagonal,
):
    rows, height, width = forced.shape
    count = height - PAD
    values = [halo[:count, :], outer[:count, :]]
    values += [inner[i * count : (i + 1) * count, :] for i in range(rows - 2)]
    values += [outer[count:, :], halo[count:, :]]
    viscs = [near[0, count : count + 1, :]]
    viscs += [forced[r, count : count + 1, :] for r in range(rows)]
    viscs += [near[1, count : count + 1, :]]
    total = jnp.zeros((2 * count, 2 * count), F32)
    for r in range(rows):
        centre, visc = values[r + 1], viscs[r + 1]
        left, right = shifted(centre, *edges_from(from_left, from_right, slice(0, count), r))
        visc_side = shifted(
            visc, *edges_from(visc_left, visc_right, slice(count, count + 1), r)
        )
        gradient = velocity[r : r + 1, :] * operate_row(
            centre, values[r], values[r + 2], left, right,
            [visc, viscs[r], viscs[r + 2], *visc_side],
            friction[r : r + 1, :],
        )
        value = gradient + omega[r * count : (r + 1) * count, :]
        sketch[r * count : (r + 1) * count, :] = value
        parts = jnp.concatenate(split(value), axis=0)
        total = total + dot(parts, parts, 1)
    total = total + pltpu.roll(total, count, 1)
    total = (total[:count] + total[count:]) / cells
    body, diagonal = packed(total)
    gram[...] = body
    gram_diagonal[...] = jnp.broadcast_to(diagonal, gram_diagonal.shape)


def spread_kernel(body, other_body, diagonal, other_diagonal, out):
    total = body[...] + other_body[...]
    last = diagonal[0:1, :] + other_diagonal[0:1, :]
    for i in range(total.shape[0]):
        row = total[i : i + 1, :]
        for d in range(out.shape[0]):
            out[d, :, i * LANES : (i + 1) * LANES] = row
    for d in range(out.shape[0]):
        out[d, :, total.shape[0] * LANES :] = last


def factorize(matrix):
    size = matrix.shape[0]
    row = row_of((8, LANES))
    tiles = [matrix[8 * t : 8 * t + 8] for t in range(size // 8)]
    for j in range(size):
        t, s = divmod(j, 8)
        pivot_row = jnp.broadcast_to(tiles[t][s : s + 1], (8, LANES))
        pivot = jnp.broadcast_to(pivot_row[:, j : j + 1], (8, LANES))
        scaled = pivot_row / pivot
        for q in range(t, size // 8):
            column = jnp.broadcast_to(tiles[q][:, j : j + 1], (8, LANES))
            if q == t:
                column = jnp.where(row > s, column, 0.0)
            tiles[q] = tiles[q] - column * scaled
    out = []
    for t, tile in enumerate(tiles):
        diagonal = jnp.sum(
            jnp.where(lane_of((8, LANES)) == row + 8 * t, tile, 0.0), axis=1, keepdims=True
        )
        out.append(tile * lax.rsqrt(diagonal))
    return jnp.concatenate(out, axis=0)


def basis_kernel(rank, gathered, sketch, basis, factor, turned):
    count = factor.shape[0]
    parts = gathered.shape[2] // LANES - 1
    total = gathered[0]
    for d in range(1, gathered.shape[0]):
        total = total + gathered[d]
    row = row_of((parts, LANES))
    body = jnp.zeros((parts, LANES), F32)
    for i in range(parts):
        body = jnp.where(row == i, total[:, i * LANES : (i + 1) * LANES], body)
    matrix = unpacked(body, total[:, parts * LANES :])
    row, lane = row_of(matrix.shape), lane_of(matrix.shape)
    matrix = jnp.where(lane == row + count, 1.0, matrix)
    done = factorize(matrix)
    upper = jnp.where((lane < count) & (lane >= row), done, 0.0)
    square = jnp.concatenate([upper, jnp.zeros((LANES - count, LANES), F32)], axis=0)
    factor[...] = square.T[:count, :count]
    inverse = pltpu.roll(done, count, 1)
    inverse = jnp.where((lane <= row) & (row < rank[0]), inverse, 0.0)
    high = inverse.astype(BF16).astype(F32)
    high, low = (x + pltpu.roll(x, count, 1) for x in (high, inverse - high))
    left = jnp.concatenate([high, low], axis=1).astype(BF16)
    rows = sketch.shape[0] // count
    width = sketch.shape[1]
    for r in range(rows):
        parts = split(sketch[r * count : (r + 1) * count, :])
        value = dot(left, jnp.concatenate([*parts, *parts], axis=0))
        for c in range(width // LANES):
            turned[c, pl.ds(r, count, stride=rows), :] = value[:, c * LANES : (c + 1) * LANES]
    for c in range(width // LANES):
        basis[:, :, c * LANES : (c + 1) * LANES] = turned[c].reshape(count, rows, LANES)


def ring(x, axis, step):
    size = lax.axis_size(axis)
    return lax.ppermute(x, axis, [(i, (i + step) % size) for i in range(size)])


def both_sides(x):
    other = ring(x, "obs", 1)
    return other, (other if lax.axis_size("obs") == 2 else ring(x, "obs", -1))


def all_shares(x, sides):
    size = lax.axis_size("obs")
    if size == 2:
        return [x, sides[0]]
    gathered = lax.all_gather(x, "obs")
    return [gathered[i] for i in range(size)]


def per_device(probes, velocity, viscosity, friction, obs_block, obs_weight, obs_prec, rank):
    count, rows, width = probes.shape
    share = obs_weight.shape[1]
    mesh_size, obs_size = lax.axis_size("mesh"), lax.axis_size("obs")
    slab_columns = width * obs_size // LANES
    cells = rows * width * mesh_size * obs_size
    height = count + PAD

    payload = (2 * count + share + 16, width)
    omega, up, down = call(
        edges_kernel,
        [((rows * count, width), F32), (payload, BF16), (payload, BF16)],
        (probes, velocity, viscosity, friction, obs_weight, obs_block, obs_prec),
        [pltpu.VMEM((width // LANES, rows * count, LANES), F32), pltpu.VMEM((16, width), F32)],
        name="edges",
    )
    from_up, from_down = ring(down, "mesh", 1), ring(up, "mesh", -1)

    forced, sent = call(
        forced_kernel,
        [((rows, height, width), F32), ((height + share + PAD, LANES), F32)],
        (omega, velocity, viscosity, obs_weight, obs_block, obs_prec),
        name="forced",
    )
    sides = both_sides(sent)
    observed = all_shares(sent, sides)
    (inner,) = call(
        functools.partial(inner_kernel, slab_columns, share),
        [(((rows - 2) * count, width), F32)],
        (forced, friction, *sides, *observed),
        name="inner",
    )
    near, far_sent = call(
        functools.partial(far_kernel, count, share),
        [((2, height, width), F32), ((height + 2 * (share + PAD), LANES), F32)],
        (from_up, from_down),
        name="far",
    )
    far_sides = both_sides(far_sent)
    far_observed = all_shares(far_sent, far_sides)
    outer, source_sent = call(
        functools.partial(outer_kernel, slab_columns, share),
        [((2 * count, width), F32), ((count, LANES), F32)],
        (forced, near, friction, *sides, inner, *observed),
        name="outer",
    )
    source_sides = both_sides(source_sent)
    (halo,) = call(
        functools.partial(halo_kernel, slab_columns, share),
        [((2 * count, width), F32)],
        (forced, near, from_up, from_down, *far_sides, *far_observed),
        name="halo",
    )
    sketch, gram, gram_diagonal = call(
        functools.partial(sketch_kernel, cells),
        [((rows * count, width), F32), ((16, LANES), F32), ((8, LANES), F32)],
        (forced, near, omega, velocity, friction, *sides, *source_sides, inner, outer, halo),
        name="sketch",
    )
    gram = jnp.concatenate([gram, gram_diagonal], axis=0)
    if obs_size == 2:
        other = ring(gram, "obs", 1)
    else:
        other = lax.psum(gram, "obs") - gram
    (pieces,) = call(
        spread_kernel,
        [((mesh_size, 1, 17 * LANES), F32)],
        (gram[:16], other[:16], gram[16:], other[16:]),
        name="spread",
    )
    gathered = lax.all_to_all(pieces, "mesh", 0, 0, tiled=True)
    basis, factor = pl.pallas_call(
        basis_kernel,
        out_shape=[
            jax.ShapeDtypeStruct((count, rows, width), F32),
            jax.ShapeDtypeStruct((count, count), F32),
        ],
        in_specs=[
            pl.BlockSpec(memory_space=pltpu.SMEM),
            pl.BlockSpec(memory_space=pltpu.VMEM),
            pl.BlockSpec(memory_space=pltpu.VMEM),
        ],
        scratch_shapes=[pltpu.VMEM((width // LANES, rows * count, LANES), F32)],
        compiler_params=pltpu.CompilerParams(vmem_limit_bytes=8 * 2**20),
        name="basis",
    )(rank, gathered, sketch)
    return basis, factor


def solution(mesh):
    in_specs = (
        P(None, "mesh", "obs"),
        P("mesh", "obs"),
        P("mesh", "obs"),
        P("mesh", "obs"),
        P("mesh", "obs"),
        P("mesh", "obs", None),
        P("mesh", "obs"),
        P(),
    )
    out_specs = (P(None, "mesh", "obs"), P())
    return jax.shard_map(
        per_device, mesh=mesh, in_specs=in_specs, out_specs=out_specs, check_vma=False
    )
```

```python
import functools

import jax
import jax.numpy as jnp
from jax import lax
from jax.experimental import pallas as pl
from jax.experimental.pallas import tpu as pltpu
from jax.sharding import PartitionSpec as P

LANES = 128
RIGHT = 16
PAD = 8
F32 = jnp.float32
BF16 = jnp.bfloat16


def split(x):
    high = x.astype(BF16)
    return high, (x - high.astype(F32)).astype(BF16)


def lane_of(shape):
    return lax.broadcasted_iota(jnp.int32, shape, 1)


def row_of(shape):
    return lax.broadcasted_iota(jnp.int32, shape, 0)


def dot(a, b, rhs_dim=0):
    return lax.dot_general(
        a, b, (((1,), (rhs_dim,)), ((), ())), preferred_element_type=F32
    )


def call(body, outs, args, scratch=(), flops=0, space=pltpu.VMEM, name=None):
    if space != pltpu.VMEM:
        args = [pltpu.with_memory_space_constraint(x, space) for x in args]
    outs = [jax.ShapeDtypeStruct(shape, kind) for shape, kind in outs]
    return pl.pallas_call(
        body,
        out_shape=outs,
        in_specs=[pl.BlockSpec(memory_space=space)] * len(args),
        scratch_shapes=list(scratch),
        compiler_params=pltpu.CompilerParams(vmem_limit_bytes=8 * 2**20),
        cost_estimate=pl.CostEstimate(
            flops=flops, bytes_accessed=2**20, transcendentals=0
        ),
        name=name,
    )(*args)


def shifted(x, left_edge, right_edge):
    lane = lane_of(x.shape)
    width = x.shape[1]
    left = jnp.where(lane == 0, left_edge, pltpu.roll(x, 1, 1))
    right = jnp.where(lane == width - 1, right_edge, pltpu.roll(x, width - 1, 1))
    return left, right


def operate_row(centre, above, below, left, right, visc, friction):
    own, *others = visc
    faces = [0.5 * (own + other) for other in others]
    result = (friction + faces[0] + faces[1] + faces[2] + faces[3]) * centre
    for face, value in zip(faces, (above, below, left, right)):
        result = result - face * value
    return result


def tangent_row(count, centre, above, below, left_edge, right_edge, friction):
    left, right = shifted(centre, left_edge, right_edge)
    visc = [x[count : count + 1] for x in (centre, above, below, left, right)]
    values = [x[:count] for x in (centre, above, below, left, right)]
    return operate_row(*values, visc, friction).astype(BF16)


def edge_columns(rows):
    height, width = rows[0].shape
    lane = lane_of((height, LANES))
    out = jnp.zeros((height, LANES), F32)
    for at, x in enumerate(rows):
        out = jnp.where(lane == at, x[:, :1], out)
        out = jnp.where(lane == RIGHT + at, x[:, width - 1 :], out)
    return out


def edges_from(left_ref, right_ref, rows, at):
    here, last = lax.axis_index("obs"), lax.axis_size("obs") - 1
    left = left_ref[rows, RIGHT + at : RIGHT + at + 1]
    right = right_ref[rows, at : at + 1]
    return jnp.where(here > 0, left, 0.0), jnp.where(here < last, right, 0.0)


def sources(tangents, grid_rows, observed, slab_columns):
    count, width = tangents[0].shape
    owned = width // LANES
    first = lax.axis_index("obs") * owned
    blocks = jnp.concatenate(
        [t[:, c * LANES : (c + 1) * LANES] for t in tangents for c in range(owned)], axis=0
    )
    doubled = jnp.concatenate([blocks, blocks], axis=1)
    total = None
    for at in range(0, len(observed), 2):
        pair = observed[at : at + 2]
        if len(pair) == 1:
            pair = pair + [tuple(jnp.zeros_like(x) for x in pair[0])]
        high = jnp.concatenate([x[0] for x in pair], axis=0)
        low = jnp.concatenate([x[1] for x in pair], axis=0)
        share = pair[0][0].shape[0]
        lane = lane_of((1, LANES))
        ids = jnp.where(lane < share, pair[0][2], pltpu.roll(pair[1][2], share, 1))
        ids = ids.astype(jnp.int32)
        precision = jnp.where(lane < share, pair[0][3], pltpu.roll(pair[1][3], share, 1))
        misfit = dot(doubled, jnp.concatenate([high, low], axis=1), 1)
        kept = []
        for i, row in enumerate(grid_rows):
            for c in range(owned):
                k = i * owned + c
                scale = jnp.where(ids == row * slab_columns + first + c, precision, 0.0)
                kept.append(misfit[k * count : (k + 1) * count] * scale)
        misfit_high, misfit_low = split(jnp.concatenate(kept, axis=0))
        both = dot(
            jnp.concatenate([misfit_high, misfit_low], axis=1),
            jnp.concatenate(
                [
                    jnp.concatenate([high, low], axis=1),
                    jnp.concatenate([high, jnp.zeros_like(low)], axis=1),
                ],
                axis=0,
            ),
        )
        part = both[:, :LANES] + both[:, LANES:]
        total = part if total is None else total + part
    return [
        jnp.concatenate(
            [total[(i * owned + c) * count : (i * owned + c + 1) * count] for c in range(owned)],
            axis=1,
        )
        for i in range(len(tangents))
    ]


def share_rows(ids, precision):
    out = jnp.zeros((PAD, LANES), F32)
    row = row_of(out.shape)

    def wide(x):
        return jnp.concatenate([x, jnp.zeros((1, LANES - x.shape[1]), F32)], axis=1)

    return jnp.where(row == 0, wide(ids), jnp.where(row == 1, wide(precision), out))


def read_share(ref, at, share):
    weight = ref[at : at + share, :]
    high, low = split(weight)
    return high, low, ref[at + share : at + share + 1, :], ref[at + share + 1 : at + share + 2, :]


def edges_kernel(
    probes, velocity, viscosity, friction, weight, ids, precision,
    omega, up, down, grid, owned, staged, staged_ids, staged_precision, turned, small, sems,
):
    count, rows, width = probes.shape
    share = weight.shape[1]
    copies = [
        pltpu.make_async_copy(source, target, sems.at[i])
        for i, (source, target) in enumerate(
            (
                (probes, staged),
                (velocity, grid.at[0]),
                (viscosity, grid.at[1]),
                (friction, grid.at[2]),
                (weight.at[0], owned.at[:share]),
                (ids, staged_ids),
                (precision, staged_precision),
            )
        )
    ]
    for copy in copies:
        copy.start()
    for copy in copies:
        copy.wait()
    owned[share:, :] = share_rows(staged_ids[...].astype(F32), staged_precision[...])
    for c in range(width // LANES):
        lanes = slice(c * LANES, (c + 1) * LANES)
        turned[c] = staged[:, :, lanes].astype(F32).reshape(count * rows, LANES)
        for r in range(rows):
            omega[r * count : (r + 1) * count, lanes] = turned[c, pl.ds(r, count, stride=rows), :]
    weights = jnp.concatenate(split(owned[:share, :]), axis=1)
    for out, near, next_near in ((up, 0, 1), (down, rows - 1, rows - 2)):
        out[:count, :] = omega[near * count : (near + 1) * count, :].astype(BF16)
        out[count : 2 * count, :] = omega[next_near * count : (next_near + 1) * count, :].astype(BF16)
        out[2 * count : 2 * count + share, :] = weights
        small[...] = jnp.zeros_like(small)
        at = 0
        for field, r in ((0, near), (0, next_near), (1, near), (1, next_near), (2, near)):
            value = grid[field, r : r + 1, :]
            high = value.astype(BF16).astype(F32)
            small[at : at + 1, :] = high
            small[at + 1 : at + 2, :] = value - high
            at += 2
        small[at : at + 1, :LANES] = owned[share : share + 1, :]
        value = owned[share + 1 : share + 2, :]
        high = value.astype(BF16).astype(F32)
        small[at + 1 : at + 2, :LANES] = high
        small[at + 2 : at + 3, :LANES] = value - high
        out[2 * count + share :, :] = small[...].astype(BF16)


def forced_kernel(omega, grid, owned, forced, sent):
    _, rows, width = grid.shape
    count = omega.shape[0] // rows
    blocks = []
    first = row_of((PAD, width)) == 0
    for r in range(rows):
        block = jnp.concatenate(
            [
                grid[0, r : r + 1, :] * omega[r * count : (r + 1) * count, :],
                jnp.where(first, grid[1, r : r + 1, :], 0.0),
            ],
            axis=0,
        )
        forced[r] = block
        blocks.append(block)
    sent[: count + PAD, :] = edge_columns(blocks)
    sent[count + PAD :, :] = owned[...]


def shares_of(refs, at, share):
    return [read_share(ref, at, share) for ref in refs]


def inner_kernel(slab_columns, share, forced, grid, from_left, from_right, *rest):
    *observed, out = rest
    rows, height, width = forced.shape
    count = height - PAD
    tangents = []
    inner = range(1, rows - 1)
    for r in inner:
        edges = edges_from(from_left, from_right, slice(0, height), r)
        tangents.append(
            tangent_row(count, forced[r], forced[r - 1], forced[r + 1], *edges, grid[2, r : r + 1, :])
        )
    result = sources(tangents, inner, shares_of(observed, height, share), slab_columns)
    for i, x in enumerate(result):
        out[i * count : (i + 1) * count, :] = x


def received(ref, count, share):
    small = ref[2 * count + share :, :].astype(F32)
    parts = [small[i : i + 1] + small[i + 1 : i + 2] for i in range(0, 10, 2)]
    return parts, small[10:11, :LANES], small[11:12, :LANES] + small[12:13, :LANES]


def far_kernel(count, share, from_up, from_down, inner, near, sent):
    blocks = []
    edge = lax.axis_index("mesh"), lax.axis_size("mesh") - 1
    width = from_up.shape[1]
    first = row_of((PAD, width)) == 0
    at = count + PAD
    for i, (ref, inside) in enumerate(((from_up, edge[0] > 0), (from_down, edge[0] < edge[1]))):
        (velocity, _, viscosity, _, _), ids, precision = received(ref, count, share)
        block = jnp.concatenate(
            [velocity * ref[:count, :].astype(F32), jnp.where(first, viscosity, 0.0)], axis=0
        )
        block = jnp.where(inside, block, 0.0)
        near[i] = block
        blocks.append(block)
        both = ref[2 * count : 2 * count + share, :].astype(F32)
        sent[at : at + share, :] = both[:, :LANES] + both[:, LANES:]
        row = row_of((PAD, LANES))
        sent[at + share : at + share + PAD, :] = jnp.where(
            row == 0, ids, jnp.where(row == 1, precision, 0.0)
        )
        at += share + PAD
    sent[: count + PAD, :] = edge_columns(blocks)


def outer_kernel(slab_columns, share, forced, near, grid, from_left, from_right, inner, *rest):
    *observed, out, sent = rest
    rows, height, width = forced.shape
    count = height - PAD
    tangents = []
    outer = (0, rows - 1)
    for r in outer:
        edges = edges_from(from_left, from_right, slice(0, height), r)
        above = near[0] if r == 0 else forced[r - 1]
        below = near[1] if r == rows - 1 else forced[r + 1]
        tangents.append(tangent_row(count, forced[r], above, below, *edges, grid[2, r : r + 1, :]))
    first, last = sources(tangents, outer, shares_of(observed, height, share), slab_columns)
    out[:count, :] = first
    out[count:, :] = last
    middle = [inner[i * count : (i + 1) * count, :] for i in range(rows - 2)]
    sent[...] = edge_columns([first, *middle, last])


def halo_kernel(slab_columns, share, forced, near, from_up, from_down, from_left, from_right, *rest):
    *observed, out = rest
    rows, height, width = forced.shape
    count = height - PAD
    here, last = lax.axis_index("mesh"), lax.axis_size("mesh") - 1
    for i, ref in enumerate((from_up, from_down)):
        (_, velocity, _, viscosity, friction), _, _ = received(ref, count, share)
        far = jnp.concatenate(
            [
                velocity * ref[count : 2 * count, :].astype(F32),
                jnp.broadcast_to(viscosity, (PAD, width)),
            ],
            axis=0,
        )
        own = forced[rows - 1 if i else 0]
        above, below = (own, far) if i else (far, own)
        edges = edges_from(from_left, from_right, slice(0, height), i)
        tangent = tangent_row(count, near[i], above, below, *edges, friction)
        at = height + i * (share + PAD)
        (source,) = sources(
            [tangent], (0 if i else rows - 1,), shares_of(observed, at, share), slab_columns
        )
        inside = here < last if i else here > 0
        out[i * count : (i + 1) * count, :] = jnp.where(inside, source, 0.0)


def packed(gram):
    half = gram.shape[0] // 2
    top, bottom = gram[:half], gram[half:]
    row, lane = row_of(top.shape), lane_of(top.shape) % (2 * half)
    mixed = jnp.where((lane >= half) & (row >= lane - half), pltpu.roll(top, half, 1), bottom)
    quarter = half // 2
    body = jnp.where(lane_of((quarter, LANES)) < 2 * half, mixed[:quarter], mixed[quarter:])
    diagonal = jnp.sum(jnp.where(row == lane - half, bottom, 0.0), axis=0, keepdims=True)
    return body, diagonal


def unpacked(body, diagonal):
    quarter = body.shape[0]
    half, size = 2 * quarter, 4 * quarter
    lane = lane_of(body.shape)
    turned = pltpu.roll(body, size, 1)
    mixed = jnp.concatenate(
        [jnp.where(lane < size, body, turned), jnp.where(lane < size, turned, body)], axis=0
    )
    row, lane = row_of(mixed.shape), lane_of(mixed.shape)
    top = pltpu.roll(mixed, LANES - half, 1)
    lower = jnp.concatenate(
        [
            jnp.where(row > lane, top, 0.0),
            jnp.where((lane < half) | ((lane < size) & (row < lane - half)), mixed, 0.0),
        ],
        axis=0,
    )
    spread = jnp.concatenate(
        [
            jnp.where(row == lane, top, 0.0),
            jnp.where(row == lane - half, diagonal, 0.0),
        ],
        axis=0,
    )
    square = jnp.concatenate([lower, jnp.zeros((LANES - size, LANES), F32)], axis=0)
    return lower + square.T[:size] + spread


def sketch_kernel(
    cells, forced, near, omega, grid, visc_left, visc_right,
    from_left, from_right, inner, outer, halo, sketch, gram,
):
    rows, height, width = forced.shape
    count = height - PAD
    values = [halo[:count, :], outer[:count, :]]
    values += [inner[i * count : (i + 1) * count, :] for i in range(rows - 2)]
    values += [outer[count:, :], halo[count:, :]]
    viscs = [near[0, count : count + 1, :]]
    viscs += [forced[r, count : count + 1, :] for r in range(rows)]
    viscs += [near[1, count : count + 1, :]]
    total = jnp.zeros((2 * count, 2 * count), F32)
    for r in range(rows):
        centre, visc = values[r + 1], viscs[r + 1]
        left, right = shifted(centre, *edges_from(from_left, from_right, slice(0, count), r))
        visc_side = shifted(
            visc, *edges_from(visc_left, visc_right, slice(count, count + 1), r)
        )
        gradient = grid[0, r : r + 1, :] * operate_row(
            centre, values[r], values[r + 2], left, right,
            [visc, viscs[r], viscs[r + 2], *visc_side],
            grid[2, r : r + 1, :],
        )
        value = gradient + omega[r * count : (r + 1) * count, :]
        sketch[r * count : (r + 1) * count, :] = value
        parts = jnp.concatenate(split(value), axis=0)
        total = total + dot(parts, parts, 1)
    total = total + pltpu.roll(total, count, 1)
    total = (total[:count] + total[count:]) / cells
    body, diagonal = packed(total)
    for i in range(body.shape[0]):
        gram[:, i * LANES : (i + 1) * LANES] = body[i : i + 1, :]
    gram[:, body.shape[0] * LANES :] = diagonal


def factorize(matrix):
    size = matrix.shape[0]
    row = row_of((8, LANES))
    tiles = [matrix[t : t + 8] for t in range(0, size, 8)]
    whole = functools.partial(jnp.broadcast_to, shape=(8, LANES))
    for t in range(size // 8):
        later = range(t + 1, size // 8)
        columns = {
            q: [whole(tiles[q][:, j : j + 1]) for j in range(8 * t, 8 * t + 8)]
            for q in (t, *later)
        }
        square = [
            [whole(columns[t][c][d : d + 1]) if d >= c else None for d in range(8)] for c in range(8)
        ]
        rows = [whole(tiles[t][c : c + 1]) for c in range(8)]
        for c in range(8):
            root = lax.rsqrt(square[c][c])
            rows[c] = rows[c] * root
            left = [square[c][d] * root if d > c else None for d in range(8)]
            for d in range(c + 1, 8):
                for e in range(d, 8):
                    square[d][e] = square[d][e] - left[d] * left[e]
                rows[d] = rows[d] - left[d] * rows[c]
            for q in later:
                columns[q][c] = columns[q][c] * root
                for d in range(c + 1, 8):
                    columns[q][d] = columns[q][d] - left[d] * columns[q][c]
                tiles[q] = tiles[q] - columns[q][c] * rows[c]
        tiles[t] = rows[0]
        for c in range(1, 8):
            tiles[t] = jnp.where(row == c, rows[c], tiles[t])
    return jnp.concatenate(tiles, axis=0)


def basis_kernel(rank, gram, sketch, basis, factor, turned):
    count = factor.shape[0]
    parts = gram.shape[1] // LANES - 1
    row = row_of((parts, LANES))
    body = jnp.zeros((parts, LANES), F32)
    for i in range(parts):
        body = jnp.where(row == i, gram[:, i * LANES : (i + 1) * LANES], body)
    matrix = unpacked(body, gram[:, parts * LANES :])
    row, lane = row_of(matrix.shape), lane_of(matrix.shape)
    matrix = jnp.where(lane == row + count, 1.0, matrix)
    done = factorize(matrix)
    upper = jnp.where((lane < count) & (lane >= row), done, 0.0)
    square = jnp.concatenate([upper, jnp.zeros((LANES - count, LANES), F32)], axis=0)
    factor[...] = square.T[:count, :count]
    inverse = pltpu.roll(done, count, 1)
    inverse = jnp.where((lane <= row) & (row < rank[0]), inverse, 0.0)
    high = inverse.astype(BF16).astype(F32)
    high, low = (x + pltpu.roll(x, count, 1) for x in (high, inverse - high))
    left = jnp.concatenate([high, low], axis=1).astype(BF16)
    rows = sketch.shape[0] // count
    width = sketch.shape[1]
    for r in range(rows):
        parts = split(sketch[r * count : (r + 1) * count, :])
        value = dot(left, jnp.concatenate([*parts, *parts], axis=0))
        for c in range(width // LANES):
            turned[c, pl.ds(r, count, stride=rows), :] = value[:, c * LANES : (c + 1) * LANES]
    for c in range(width // LANES):
        basis[:, :, c * LANES : (c + 1) * LANES] = turned[c].reshape(count, rows, LANES)


def ring(x, axis, step):
    size = lax.axis_size(axis)
    return lax.ppermute(x, axis, [(i, (i + step) % size) for i in range(size)])


def both_sides(x):
    other = ring(x, "obs", 1)
    return other, (other if lax.axis_size("obs") == 2 else ring(x, "obs", -1))


def all_shares(x, sides):
    size = lax.axis_size("obs")
    if size == 2:
        return [x, sides[0]]
    gathered = lax.all_gather(x, "obs")
    return [gathered[i] for i in range(size)]


def per_device(probes, velocity, viscosity, friction, obs_block, obs_weight, obs_prec, rank):
    count, rows, width = probes.shape
    share = obs_weight.shape[1]
    mesh_size, obs_size = lax.axis_size("mesh"), lax.axis_size("obs")
    slab_columns = width * obs_size // LANES
    cells = rows * width * mesh_size * obs_size
    height = count + PAD

    payload = (2 * count + share + 16, width)
    omega, up, down, grid, owned = call(
        edges_kernel,
        [
            ((rows * count, width), F32),
            (payload, BF16),
            (payload, BF16),
            ((3, rows, width), F32),
            ((share + PAD, LANES), F32),
        ],
        (probes, velocity, viscosity, friction, obs_weight, obs_block, obs_prec),
        [
            pltpu.VMEM(probes.shape, probes.dtype),
            pltpu.VMEM(obs_block.shape, obs_block.dtype),
            pltpu.VMEM(obs_prec.shape, F32),
            pltpu.VMEM((width // LANES, rows * count, LANES), F32),
            pltpu.VMEM((16, width), F32),
            pltpu.SemaphoreType.DMA((7,)),
        ],
        space=pltpu.HBM,
        name="edges",
    )
    from_up, from_down = ring(down, "mesh", 1), ring(up, "mesh", -1)

    forced, sent = call(
        forced_kernel,
        [((rows, height, width), F32), ((height + share + PAD, LANES), F32)],
        (omega, grid, owned),
        name="forced",
    )
    sides = both_sides(sent)
    observed = all_shares(sent, sides)
    (inner,) = call(
        functools.partial(inner_kernel, slab_columns, share),
        [(((rows - 2) * count, width), F32)],
        (forced, grid, *sides, *observed),
        name="inner",
    )
    near, far_sent = call(
        functools.partial(far_kernel, count, share),
        [((2, height, width), F32), ((height + 2 * (share + PAD), LANES), F32)],
        (from_up, from_down, inner),
        name="far",
    )
    far_sides = both_sides(far_sent)
    far_observed = all_shares(far_sent, far_sides)
    outer, source_sent = call(
        functools.partial(outer_kernel, slab_columns, share),
        [((2 * count, width), F32), ((count, LANES), F32)],
        (forced, near, grid, *sides, inner, *observed),
        name="outer",
    )
    source_sides = both_sides(source_sent)
    (halo,) = call(
        functools.partial(halo_kernel, slab_columns, share),
        [((2 * count, width), F32)],
        (forced, near, from_up, from_down, *far_sides, *far_observed),
        name="halo",
    )
    sketch, gram = call(
        functools.partial(sketch_kernel, cells),
        [((rows * count, width), F32), ((1, 17 * LANES), F32)],
        (forced, near, omega, grid, *sides, *source_sides, inner, outer, halo),
        name="sketch",
    )
    gram = gram + ring(gram, "obs", 1) if obs_size == 2 else lax.psum(gram, "obs")
    pieces = jnp.broadcast_to(gram, (mesh_size, *gram.shape))
    gram = jnp.sum(lax.all_to_all(pieces, "mesh", 0, 0, tiled=True), axis=0)
    basis, factor = pl.pallas_call(
        basis_kernel,
        out_shape=[
            jax.ShapeDtypeStruct((count, rows, width), F32),
            jax.ShapeDtypeStruct((count, count), F32),
        ],
        in_specs=[
            pl.BlockSpec(memory_space=pltpu.SMEM),
            pl.BlockSpec(memory_space=pltpu.VMEM),
            pl.BlockSpec(memory_space=pltpu.VMEM),
        ],
        scratch_shapes=[pltpu.VMEM((width // LANES, rows * count, LANES), F32)],
        compiler_params=pltpu.CompilerParams(vmem_limit_bytes=8 * 2**20),
        name="basis",
    )(rank, gram, sketch)
    return basis, factor


def solution(mesh):
    in_specs = (
        P(None, "mesh", "obs"),
        P("mesh", "obs"),
        P("mesh", "obs"),
        P("mesh", "obs"),
        P("mesh", "obs"),
        P("mesh", "obs", None),
        P("mesh", "obs"),
        P(),
    )
    out_specs = (P(None, "mesh", "obs"), P())
    return jax.shard_map(
        per_device, mesh=mesh, in_specs=in_specs, out_specs=out_specs, check_vma=False
    )
```

```python
import functools

import jax
import jax.numpy as jnp
from jax import lax
from jax.experimental import pallas as pl
from jax.experimental.pallas import tpu as pltpu
from jax.sharding import PartitionSpec as P

LANES = 128
RIGHT = 16
PAD = 8
F32 = jnp.float32
BF16 = jnp.bfloat16


def split(x):
    high = x.astype(BF16)
    return high, (x - high.astype(F32)).astype(BF16)


def lane_of(shape):
    return lax.broadcasted_iota(jnp.int32, shape, 1)


def row_of(shape):
    return lax.broadcasted_iota(jnp.int32, shape, 0)


def dot(a, b, rhs_dim=0):
    return lax.dot_general(
        a, b, (((1,), (rhs_dim,)), ((), ())), preferred_element_type=F32
    )


def call(body, outs, args, scratch=(), flops=0, space=pltpu.VMEM, name=None):
    if space != pltpu.VMEM:
        args = [pltpu.with_memory_space_constraint(x, space) for x in args]
    outs = [jax.ShapeDtypeStruct(shape, kind) for shape, kind in outs]
    return pl.pallas_call(
        body,
        out_shape=outs,
        in_specs=[pl.BlockSpec(memory_space=space)] * len(args),
        scratch_shapes=list(scratch),
        compiler_params=pltpu.CompilerParams(vmem_limit_bytes=8 * 2**20),
        cost_estimate=pl.CostEstimate(
            flops=flops, bytes_accessed=2**20, transcendentals=0
        ),
        name=name,
    )(*args)


def shifted(x, left_edge, right_edge):
    lane = lane_of(x.shape)
    width = x.shape[1]
    left = jnp.where(lane == 0, left_edge, pltpu.roll(x, 1, 1))
    right = jnp.where(lane == width - 1, right_edge, pltpu.roll(x, width - 1, 1))
    return left, right


def operate_row(centre, above, below, left, right, visc, friction):
    own, *others = visc
    faces = [0.5 * (own + other) for other in others]
    result = (friction + faces[0] + faces[1] + faces[2] + faces[3]) * centre
    for face, value in zip(faces, (above, below, left, right)):
        result = result - face * value
    return result


def tangent_row(count, centre, above, below, left_edge, right_edge, friction):
    left, right = shifted(centre, left_edge, right_edge)
    visc = [x[count : count + 1] for x in (centre, above, below, left, right)]
    values = [x[:count] for x in (centre, above, below, left, right)]
    return operate_row(*values, visc, friction).astype(BF16)


def edge_columns(rows):
    height, width = rows[0].shape
    lane = lane_of((height, LANES))
    out = jnp.zeros((height, LANES), F32)
    for at, x in enumerate(rows):
        out = jnp.where(lane == at, x[:, :1], out)
        out = jnp.where(lane == RIGHT + at, x[:, width - 1 :], out)
    return out


def edges_from(left_ref, right_ref, rows, at):
    here, last = lax.axis_index("obs"), lax.axis_size("obs") - 1
    left = left_ref[rows, RIGHT + at : RIGHT + at + 1]
    right = right_ref[rows, at : at + 1]
    return jnp.where(here > 0, left, 0.0), jnp.where(here < last, right, 0.0)


def sources(tangents, grid_rows, observed, slab_columns):
    count, width = tangents[0].shape
    owned = width // LANES
    first = lax.axis_index("obs") * owned
    blocks = jnp.concatenate(
        [t[:, c * LANES : (c + 1) * LANES] for t in tangents for c in range(owned)], axis=0
    )
    doubled = jnp.concatenate([blocks, blocks], axis=1)
    total = None
    for at in range(0, len(observed), 2):
        pair = observed[at : at + 2]
        if len(pair) == 1:
            pair = pair + [tuple(jnp.zeros_like(x) for x in pair[0])]
        high = jnp.concatenate([x[0] for x in pair], axis=0)
        low = jnp.concatenate([x[1] for x in pair], axis=0)
        share = pair[0][0].shape[0]
        lane = lane_of((1, LANES))
        ids = jnp.where(lane < share, pair[0][2], pltpu.roll(pair[1][2], share, 1))
        ids = ids.astype(jnp.int32)
        precision = jnp.where(lane < share, pair[0][3], pltpu.roll(pair[1][3], share, 1))
        misfit = dot(doubled, jnp.concatenate([high, low], axis=1), 1)
        kept = []
        for i, row in enumerate(grid_rows):
            for c in range(owned):
                k = i * owned + c
                scale = jnp.where(ids == row * slab_columns + first + c, precision, 0.0)
                kept.append(misfit[k * count : (k + 1) * count] * scale)
        misfit_high, misfit_low = split(jnp.concatenate(kept, axis=0))
        both = dot(
            jnp.concatenate([misfit_high, misfit_low], axis=1),
            jnp.concatenate(
                [
                    jnp.concatenate([high, low], axis=1),
                    jnp.concatenate([high, jnp.zeros_like(low)], axis=1),
                ],
                axis=0,
            ),
        )
        part = both[:, :LANES] + both[:, LANES:]
        total = part if total is None else total + part
    return [
        jnp.concatenate(
            [total[(i * owned + c) * count : (i * owned + c + 1) * count] for c in range(owned)],
            axis=1,
        )
        for i in range(len(tangents))
    ]


def share_rows(ids, precision):
    out = jnp.zeros((PAD, LANES), F32)
    row = row_of(out.shape)

    def wide(x):
        return jnp.concatenate([x, jnp.zeros((1, LANES - x.shape[1]), F32)], axis=1)

    return jnp.where(row == 0, wide(ids), jnp.where(row == 1, wide(precision), out))


def read_share(ref, at, share):
    weight = ref[at : at + share, :]
    high, low = split(weight)
    return high, low, ref[at + share : at + share + 1, :], ref[at + share + 1 : at + share + 2, :]


def edges_kernel(
    probes, velocity, viscosity, friction, weight, ids, precision,
    omega, first, second, grid, owned, staged, staged_ids, staged_precision, turned, small, sems,
):
    count, rows, width = probes.shape
    share = weight.shape[1]
    copies = [
        pltpu.make_async_copy(source, target, sems.at[i])
        for i, (source, target) in enumerate(
            (
                (probes, staged),
                (velocity, grid.at[0]),
                (viscosity, grid.at[1]),
                (friction, grid.at[2]),
                (weight.at[0], owned.at[:share]),
                (ids, staged_ids),
                (precision, staged_precision),
            )
        )
    ]
    for copy in copies:
        copy.start()
    for copy in copies:
        copy.wait()
    owned[share:, :] = share_rows(staged_ids[...].astype(F32), staged_precision[...])
    for c in range(width // LANES):
        lanes = slice(c * LANES, (c + 1) * LANES)
        turned[c] = staged[:, :, lanes].astype(F32).reshape(count * rows, LANES)
        for r in range(rows):
            omega[r * count : (r + 1) * count, lanes] = turned[c, pl.ds(r, count, stride=rows), :]
    half = share // 2
    weights = owned[:share, :].astype(BF16)
    weights = jnp.concatenate([weights[:half], weights[half:]], axis=1)
    even = lax.axis_index("mesh") % 2 == 0
    for out, below in ((first, even), (second, jnp.logical_not(even))):
        near = jnp.where(below, rows - 1, 0)
        beyond = jnp.where(below, rows - 2, 1)
        for i, r in enumerate((near, beyond)):
            at = pl.multiple_of(r * count, count)
            out[i * count : (i + 1) * count, :] = omega[pl.ds(at, count), :].astype(BF16)
        out[2 * count : 2 * count + half, :] = weights
        small[...] = jnp.zeros_like(small)
        at = 0
        for field, r in ((0, near), (0, beyond), (1, near), (1, beyond), (2, near)):
            value = grid[field, pl.ds(r, 1), :]
            high = value.astype(BF16).astype(F32)
            small[at : at + 1, :] = high
            small[at + 1 : at + 2, :] = value - high
            at += 2
        small[at : at + 1, :LANES] = owned[share : share + 1, :]
        value = owned[share + 1 : share + 2, :]
        high = value.astype(BF16).astype(F32)
        small[at + 1 : at + 2, :LANES] = high
        small[at + 2 : at + 3, :LANES] = value - high
        out[2 * count + half :, :] = small[...].astype(BF16)


def forced_kernel(omega, grid, owned, forced, sent):
    _, rows, width = grid.shape
    count = omega.shape[0] // rows
    blocks = []
    first = row_of((PAD, width)) == 0
    for r in range(rows):
        block = jnp.concatenate(
            [
                grid[0, r : r + 1, :] * omega[r * count : (r + 1) * count, :],
                jnp.where(first, grid[1, r : r + 1, :], 0.0),
            ],
            axis=0,
        )
        forced[r] = block
        blocks.append(block)
    sent[: count + PAD, :] = edge_columns(blocks)
    sent[count + PAD :, :] = owned[...]


def shares_of(refs, at, share):
    return [read_share(ref, at, share) for ref in refs]


def inner_kernel(slab_columns, share, forced, grid, from_left, from_right, *rest):
    *observed, out = rest
    rows, height, width = forced.shape
    count = height - PAD
    tangents = []
    inner = range(1, rows - 1)
    for r in inner:
        edges = edges_from(from_left, from_right, slice(0, height), r)
        tangents.append(
            tangent_row(count, forced[r], forced[r - 1], forced[r + 1], *edges, grid[2, r : r + 1, :])
        )
    result = sources(tangents, inner, shares_of(observed, height, share), slab_columns)
    for i, x in enumerate(result):
        out[i * count : (i + 1) * count, :] = x


def arrival(first, second, below):
    even = lax.axis_index("mesh") % 2 == 0
    return jnp.where(even if below else jnp.logical_not(even), first[...], second[...])


def received(x, count, share):
    small = x[2 * count + share // 2 :].astype(F32)
    parts = [small[i : i + 1] + small[i + 1 : i + 2] for i in range(0, 10, 2)]
    return parts, small[10:11, :LANES], small[11:12, :LANES] + small[12:13, :LANES]


def far_kernel(count, share, first, second, inner, near, sent):
    blocks = []
    here, last = lax.axis_index("mesh"), lax.axis_size("mesh") - 1
    width = first.shape[1]
    top = row_of((PAD, width)) == 0
    at = count + PAD
    for i, inside in enumerate((here > 0, here < last)):
        x = arrival(first, second, i == 1)
        (velocity, _, viscosity, _, _), ids, precision = received(x, count, share)
        block = jnp.concatenate(
            [velocity * x[:count].astype(F32), jnp.where(top, viscosity, 0.0)], axis=0
        )
        block = jnp.where(inside, block, 0.0)
        near[i] = block
        blocks.append(block)
        weight = x[2 * count : 2 * count + share // 2].astype(F32)
        sent[at : at + share // 2, :] = weight[:, :LANES]
        sent[at + share // 2 : at + share, :] = weight[:, LANES:]
        row = row_of((PAD, LANES))
        sent[at + share : at + share + PAD, :] = jnp.where(
            row == 0, ids, jnp.where(row == 1, precision, 0.0)
        )
        at += share + PAD
    sent[: count + PAD, :] = edge_columns(blocks)


def outer_kernel(slab_columns, share, forced, near, grid, from_left, from_right, inner, *rest):
    *observed, out, sent = rest
    rows, height, width = forced.shape
    count = height - PAD
    tangents = []
    outer = (0, rows - 1)
    for r in outer:
        edges = edges_from(from_left, from_right, slice(0, height), r)
        above = near[0] if r == 0 else forced[r - 1]
        below = near[1] if r == rows - 1 else forced[r + 1]
        tangents.append(tangent_row(count, forced[r], above, below, *edges, grid[2, r : r + 1, :]))
    first, last = sources(tangents, outer, shares_of(observed, height, share), slab_columns)
    out[:count, :] = first
    out[count:, :] = last
    middle = [inner[i * count : (i + 1) * count, :] for i in range(rows - 2)]
    sent[...] = edge_columns([first, *middle, last])


def halo_kernel(slab_columns, share, forced, near, first, second, from_left, from_right, *rest):
    *observed, out = rest
    rows, height, width = forced.shape
    count = height - PAD
    here, last = lax.axis_index("mesh"), lax.axis_size("mesh") - 1
    for i in range(2):
        x = arrival(first, second, i == 1)
        (_, velocity, _, viscosity, friction), _, _ = received(x, count, share)
        far = jnp.concatenate(
            [
                velocity * x[count : 2 * count].astype(F32),
                jnp.broadcast_to(viscosity, (PAD, width)),
            ],
            axis=0,
        )
        own = forced[rows - 1 if i else 0]
        above, below = (own, far) if i else (far, own)
        edges = edges_from(from_left, from_right, slice(0, height), i)
        tangent = tangent_row(count, near[i], above, below, *edges, friction)
        at = height + i * (share + PAD)
        (source,) = sources(
            [tangent], (0 if i else rows - 1,), shares_of(observed, at, share), slab_columns
        )
        inside = here < last if i else here > 0
        out[i * count : (i + 1) * count, :] = jnp.where(inside, source, 0.0)


def packed(gram):
    half = gram.shape[0] // 2
    top, bottom = gram[:half], gram[half:]
    row, lane = row_of(top.shape), lane_of(top.shape) % (2 * half)
    mixed = jnp.where((lane >= half) & (row >= lane - half), pltpu.roll(top, half, 1), bottom)
    quarter = half // 2
    body = jnp.where(lane_of((quarter, LANES)) < 2 * half, mixed[:quarter], mixed[quarter:])
    diagonal = jnp.sum(jnp.where(row == lane - half, bottom, 0.0), axis=0, keepdims=True)
    return body, diagonal


def unpacked(body, diagonal):
    quarter = body.shape[0]
    half, size = 2 * quarter, 4 * quarter
    lane = lane_of(body.shape)
    turned = pltpu.roll(body, size, 1)
    mixed = jnp.concatenate(
        [jnp.where(lane < size, body, turned), jnp.where(lane < size, turned, body)], axis=0
    )
    row, lane = row_of(mixed.shape), lane_of(mixed.shape)
    top = pltpu.roll(mixed, LANES - half, 1)
    lower = jnp.concatenate(
        [
            jnp.where(row > lane, top, 0.0),
            jnp.where((lane < half) | ((lane < size) & (row < lane - half)), mixed, 0.0),
        ],
        axis=0,
    )
    spread = jnp.concatenate(
        [
            jnp.where(row == lane, top, 0.0),
            jnp.where(row == lane - half, diagonal, 0.0),
        ],
        axis=0,
    )
    square = jnp.concatenate([lower, jnp.zeros((LANES - size, LANES), F32)], axis=0)
    return lower + square.T[:size] + spread


def sketch_kernel(
    cells, forced, near, omega, grid, visc_left, visc_right,
    from_left, from_right, inner, outer, halo, sketch, gram,
):
    rows, height, width = forced.shape
    count = height - PAD
    values = [halo[:count, :], outer[:count, :]]
    values += [inner[i * count : (i + 1) * count, :] for i in range(rows - 2)]
    values += [outer[count:, :], halo[count:, :]]
    viscs = [near[0, count : count + 1, :]]
    viscs += [forced[r, count : count + 1, :] for r in range(rows)]
    viscs += [near[1, count : count + 1, :]]
    total = jnp.zeros((2 * count, 2 * count), F32)
    for r in range(rows):
        centre, visc = values[r + 1], viscs[r + 1]
        left, right = shifted(centre, *edges_from(from_left, from_right, slice(0, count), r))
        visc_side = shifted(
            visc, *edges_from(visc_left, visc_right, slice(count, count + 1), r)
        )
        gradient = grid[0, r : r + 1, :] * operate_row(
            centre, values[r], values[r + 2], left, right,
            [visc, viscs[r], viscs[r + 2], *visc_side],
            grid[2, r : r + 1, :],
        )
        value = gradient + omega[r * count : (r + 1) * count, :]
        sketch[r * count : (r + 1) * count, :] = value
        parts = jnp.concatenate(split(value), axis=0)
        total = total + dot(parts, parts, 1)
    total = total + pltpu.roll(total, count, 1)
    total = (total[:count] + total[count:]) / cells
    body, diagonal = packed(total)
    for i in range(body.shape[0]):
        gram[:, i * LANES : (i + 1) * LANES] = body[i : i + 1, :]
    gram[:, body.shape[0] * LANES :] = diagonal


def factorize(matrix):
    size = matrix.shape[0]
    row = row_of((8, LANES))
    tiles = [matrix[t : t + 8] for t in range(0, size, 8)]
    whole = functools.partial(jnp.broadcast_to, shape=(8, LANES))
    for t in range(size // 8):
        later = range(t + 1, size // 8)
        columns = {
            q: [whole(tiles[q][:, j : j + 1]) for j in range(8 * t, 8 * t + 8)]
            for q in (t, *later)
        }
        square = [
            [whole(columns[t][c][d : d + 1]) if d >= c else None for d in range(8)] for c in range(8)
        ]
        rows = [whole(tiles[t][c : c + 1]) for c in range(8)]
        for c in range(8):
            root = lax.rsqrt(square[c][c])
            rows[c] = rows[c] * root
            left = [square[c][d] * root if d > c else None for d in range(8)]
            for d in range(c + 1, 8):
                for e in range(d, 8):
                    square[d][e] = square[d][e] - left[d] * left[e]
                rows[d] = rows[d] - left[d] * rows[c]
            for q in later:
                columns[q][c] = columns[q][c] * root
                for d in range(c + 1, 8):
                    columns[q][d] = columns[q][d] - left[d] * columns[q][c]
                tiles[q] = tiles[q] - columns[q][c] * rows[c]
        tiles[t] = rows[0]
        for c in range(1, 8):
            tiles[t] = jnp.where(row == c, rows[c], tiles[t])
    return jnp.concatenate(tiles, axis=0)


def basis_kernel(rank, gram, sketch, basis, factor, turned):
    count = factor.shape[0]
    parts = gram.shape[1] // LANES - 1
    row = row_of((parts, LANES))
    body = jnp.zeros((parts, LANES), F32)
    for i in range(parts):
        body = jnp.where(row == i, gram[:, i * LANES : (i + 1) * LANES], body)
    matrix = unpacked(body, gram[:, parts * LANES :])
    row, lane = row_of(matrix.shape), lane_of(matrix.shape)
    matrix = jnp.where(lane == row + count, 1.0, matrix)
    done = factorize(matrix)
    upper = jnp.where((lane < count) & (lane >= row), done, 0.0)
    square = jnp.concatenate([upper, jnp.zeros((LANES - count, LANES), F32)], axis=0)
    factor[...] = square.T[:count, :count]
    inverse = pltpu.roll(done, count, 1)
    inverse = jnp.where((lane <= row) & (row < rank[0]), inverse, 0.0)
    high = inverse.astype(BF16).astype(F32)
    high, low = (x + pltpu.roll(x, count, 1) for x in (high, inverse - high))
    left = jnp.concatenate([high, low], axis=1).astype(BF16)
    rows = sketch.shape[0] // count
    width = sketch.shape[1]
    for r in range(rows):
        parts = split(sketch[r * count : (r + 1) * count, :])
        value = dot(left, jnp.concatenate([*parts, *parts], axis=0))
        for c in range(width // LANES):
            turned[c, pl.ds(r, count, stride=rows), :] = value[:, c * LANES : (c + 1) * LANES]
    for c in range(width // LANES):
        basis[:, :, c * LANES : (c + 1) * LANES] = turned[c].reshape(count, rows, LANES)


def ring(x, axis, step):
    size = lax.axis_size(axis)
    return lax.ppermute(x, axis, [(i, (i + step) % size) for i in range(size)])


def exchanged(x, odd):
    rows, columns = lax.axis_size("mesh"), lax.axis_size("obs")
    pairs = []
    for i in range(rows):
        partner = i + 1 if i % 2 == odd else i - 1
        for c in range(columns):
            target = partner * columns + c if 0 <= partner < rows else i * columns + (c ^ 1)
            pairs.append((i * columns + c, target))
    return lax.ppermute(x, ("mesh", "obs"), pairs)


def summed(x):
    rows, columns = lax.axis_size("mesh"), lax.axis_size("obs")
    x = x + ring(x, "obs", 1) if columns == 2 else lax.psum(x, "obs")
    step = 1
    while step < rows:
        offsets = (step, 2 * step, 3 * step) if step == 1 else (step, 3 * step, 2 * step)
        if rows % (4 * step):
            offsets = (step,)
        pieces = [
            lax.ppermute(
                x,
                ("mesh", "obs"),
                [
                    (i * columns + c, (i ^ offset) * columns + (c ^ 1))
                    for i in range(rows)
                    for c in range(columns)
                ],
            )
            for offset in offsets
        ]
        for piece in pieces:
            x = x + piece
        step = step * (len(offsets) + 1)
    return x


def both_sides(x):
    other = ring(x, "obs", 1)
    return other, (other if lax.axis_size("obs") == 2 else ring(x, "obs", -1))


def all_shares(x, sides):
    size = lax.axis_size("obs")
    if size == 2:
        return [x, sides[0]]
    gathered = lax.all_gather(x, "obs")
    return [gathered[i] for i in range(size)]


def per_device(probes, velocity, viscosity, friction, obs_block, obs_weight, obs_prec, rank):
    count, rows, width = probes.shape
    share = obs_weight.shape[1]
    mesh_size, obs_size = lax.axis_size("mesh"), lax.axis_size("obs")
    slab_columns = width * obs_size // LANES
    cells = rows * width * mesh_size * obs_size
    height = count + PAD

    payload = (2 * count + share // 2 + 16, width)
    omega, first, second, grid, owned = call(
        edges_kernel,
        [
            ((rows * count, width), F32),
            (payload, BF16),
            (payload, BF16),
            ((3, rows, width), F32),
            ((share + PAD, LANES), F32),
        ],
        (probes, velocity, viscosity, friction, obs_weight, obs_block, obs_prec),
        [
            pltpu.VMEM(probes.shape, probes.dtype),
            pltpu.VMEM(obs_block.shape, obs_block.dtype),
            pltpu.VMEM(obs_prec.shape, F32),
            pltpu.VMEM((width // LANES, rows * count, LANES), F32),
            pltpu.VMEM((16, width), F32),
            pltpu.SemaphoreType.DMA((7,)),
        ],
        space=pltpu.HBM,
        name="edges",
    )
    arrived = exchanged(first, 0), exchanged(second, 1)

    forced, sent = call(
        forced_kernel,
        [((rows, height, width), F32), ((height + share + PAD, LANES), F32)],
        (omega, grid, owned),
        name="forced",
    )
    sides = both_sides(sent)
    observed = all_shares(sent, sides)
    (inner,) = call(
        functools.partial(inner_kernel, slab_columns, share),
        [(((rows - 2) * count, width), F32)],
        (forced, grid, *sides, *observed),
        name="inner",
    )
    near, far_sent = call(
        functools.partial(far_kernel, count, share),
        [((2, height, width), F32), ((height + 2 * (share + PAD), LANES), F32)],
        (*arrived, inner),
        name="far",
    )
    far_sides = both_sides(far_sent)
    far_observed = all_shares(far_sent, far_sides)
    outer, source_sent = call(
        functools.partial(outer_kernel, slab_columns, share),
        [((2 * count, width), F32), ((count, LANES), F32)],
        (forced, near, grid, *sides, inner, *observed),
        name="outer",
    )
    source_sides = both_sides(source_sent)
    (halo,) = call(
        functools.partial(halo_kernel, slab_columns, share),
        [((2 * count, width), F32)],
        (forced, near, *arrived, *far_sides, *far_observed),
        name="halo",
    )
    sketch, gram = call(
        functools.partial(sketch_kernel, cells),
        [((rows * count, width), F32), ((1, 17 * LANES), F32)],
        (forced, near, omega, grid, *sides, *source_sides, inner, outer, halo),
        name="sketch",
    )
    gram = summed(gram)
    basis, factor = pl.pallas_call(
        basis_kernel,
        out_shape=[
            jax.ShapeDtypeStruct((count, rows, width), F32),
            jax.ShapeDtypeStruct((count, count), F32),
        ],
        in_specs=[
            pl.BlockSpec(memory_space=pltpu.SMEM),
            pl.BlockSpec(memory_space=pltpu.VMEM),
            pl.BlockSpec(memory_space=pltpu.VMEM),
        ],
        scratch_shapes=[pltpu.VMEM((width // LANES, rows * count, LANES), F32)],
        compiler_params=pltpu.CompilerParams(vmem_limit_bytes=8 * 2**20),
        name="basis",
    )(rank, gram, sketch)
    return basis, factor


def solution(mesh):
    in_specs = (
        P(None, "mesh", "obs"),
        P("mesh", "obs"),
        P("mesh", "obs"),
        P("mesh", "obs"),
        P("mesh", "obs"),
        P("mesh", "obs", None),
        P("mesh", "obs"),
        P(),
    )
    out_specs = (P(None, "mesh", "obs"), P())
    return jax.shard_map(
        per_device, mesh=mesh, in_specs=in_specs, out_specs=out_specs, check_vma=False
    )
```

```python
import functools

import jax
import jax.numpy as jnp
from jax import lax
from jax.experimental import pallas as pl
from jax.experimental.pallas import tpu as pltpu
from jax.sharding import PartitionSpec as P

LANES = 128
RIGHT = 16
PAD = 8
F32 = jnp.float32
BF16 = jnp.bfloat16


def split(x):
    high = x.astype(BF16)
    return high, (x - high.astype(F32)).astype(BF16)


def lane_of(shape):
    return lax.broadcasted_iota(jnp.int32, shape, 1)


def row_of(shape):
    return lax.broadcasted_iota(jnp.int32, shape, 0)


def dot(a, b, rhs_dim=0):
    return lax.dot_general(
        a, b, (((1,), (rhs_dim,)), ((), ())), preferred_element_type=F32
    )


def call(body, outs, args, scratch=(), flops=0, space=pltpu.VMEM, name=None):
    if space != pltpu.VMEM:
        args = [pltpu.with_memory_space_constraint(x, space) for x in args]
    outs = [jax.ShapeDtypeStruct(shape, kind) for shape, kind in outs]
    return pl.pallas_call(
        body,
        out_shape=outs,
        in_specs=[pl.BlockSpec(memory_space=space)] * len(args),
        scratch_shapes=list(scratch),
        compiler_params=pltpu.CompilerParams(vmem_limit_bytes=8 * 2**20),
        cost_estimate=pl.CostEstimate(
            flops=flops, bytes_accessed=2**20, transcendentals=0
        ),
        name=name,
    )(*args)


def shifted(x, left_edge, right_edge):
    lane = lane_of(x.shape)
    width = x.shape[1]
    left = jnp.where(lane == 0, left_edge, pltpu.roll(x, 1, 1))
    right = jnp.where(lane == width - 1, right_edge, pltpu.roll(x, width - 1, 1))
    return left, right


def operate_row(centre, above, below, left, right, visc, friction):
    own, *others = visc
    faces = [0.5 * (own + other) for other in others]
    result = (friction + faces[0] + faces[1] + faces[2] + faces[3]) * centre
    for face, value in zip(faces, (above, below, left, right)):
        result = result - face * value
    return result


def tangent_row(count, centre, above, below, left_edge, right_edge, friction):
    left, right = shifted(centre, left_edge, right_edge)
    visc = [x[count : count + 1] for x in (centre, above, below, left, right)]
    values = [x[:count] for x in (centre, above, below, left, right)]
    return operate_row(*values, visc, friction).astype(BF16)


def edge_columns(rows):
    height, width = rows[0].shape
    lane = lane_of((height, LANES))
    out = jnp.zeros((height, LANES), F32)
    for at, x in enumerate(rows):
        out = jnp.where(lane == at, x[:, :1], out)
        out = jnp.where(lane == RIGHT + at, x[:, width - 1 :], out)
    return out


def edges_from(left_ref, right_ref, rows, at):
    here, last = lax.axis_index("obs"), lax.axis_size("obs") - 1
    left = left_ref[rows, RIGHT + at : RIGHT + at + 1]
    right = right_ref[rows, at : at + 1]
    return jnp.where(here > 0, left, 0.0), jnp.where(here < last, right, 0.0)


def sources(tangents, grid_rows, observed, slab_columns):
    count, width = tangents[0].shape
    owned = width // LANES
    first = lax.axis_index("obs") * owned
    blocks = jnp.concatenate(
        [t[:, c * LANES : (c + 1) * LANES] for t in tangents for c in range(owned)], axis=0
    )
    doubled = jnp.concatenate([blocks, blocks], axis=1)
    total = None
    for at in range(0, len(observed), 2):
        pair = observed[at : at + 2]
        if len(pair) == 1:
            pair = pair + [tuple(jnp.zeros_like(x) for x in pair[0])]
        high = jnp.concatenate([x[0] for x in pair], axis=0)
        low = jnp.concatenate([x[1] for x in pair], axis=0)
        share = pair[0][0].shape[0]
        lane = lane_of((1, LANES))
        ids = jnp.where(lane < share, pair[0][2], pltpu.roll(pair[1][2], share, 1))
        ids = ids.astype(jnp.int32)
        precision = jnp.where(lane < share, pair[0][3], pltpu.roll(pair[1][3], share, 1))
        misfit = dot(doubled, jnp.concatenate([high, low], axis=1), 1)
        kept = []
        for i, row in enumerate(grid_rows):
            for c in range(owned):
                k = i * owned + c
                scale = jnp.where(ids == row * slab_columns + first + c, precision, 0.0)
                kept.append(misfit[k * count : (k + 1) * count] * scale)
        misfit_high, misfit_low = split(jnp.concatenate(kept, axis=0))
        both = dot(
            jnp.concatenate([misfit_high, misfit_low], axis=1),
            jnp.concatenate(
                [
                    jnp.concatenate([high, low], axis=1),
                    jnp.concatenate([high, jnp.zeros_like(low)], axis=1),
                ],
                axis=0,
            ),
        )
        part = both[:, :LANES] + both[:, LANES:]
        total = part if total is None else total + part
    return [
        jnp.concatenate(
            [total[(i * owned + c) * count : (i * owned + c + 1) * count] for c in range(owned)],
            axis=1,
        )
        for i in range(len(tangents))
    ]


def share_rows(ids, precision):
    out = jnp.zeros((PAD, LANES), F32)
    row = row_of(out.shape)

    def wide(x):
        return jnp.concatenate([x, jnp.zeros((1, LANES - x.shape[1]), F32)], axis=1)

    return jnp.where(row == 0, wide(ids), jnp.where(row == 1, wide(precision), out))


def read_share(ref, at, share):
    high, low = split(ref[at : at + share, :])
    return high, low, ref[at + share : at + share + 1, :], ref[at + share + 1 : at + share + 2, :]


def probe_row(turned, r, rows):
    parts, cells, _ = turned.shape
    return jnp.concatenate(
        [turned[c, pl.ds(r, cells // rows, stride=rows), :] for c in range(parts)], axis=1
    )


def edges_kernel(
    probes, velocity, viscosity, friction, weight, ids, precision,
    turned, first, second, grid, owned, staged, staged_ids, staged_precision, small, sems,
):
    count, rows, width = probes.shape
    share = weight.shape[1]
    copies = [
        pltpu.make_async_copy(source, target, sems.at[i])
        for i, (source, target) in enumerate(
            (
                (probes, staged),
                (velocity, grid.at[0]),
                (viscosity, grid.at[1]),
                (friction, grid.at[2]),
                (weight.at[0], owned.at[:share]),
                (ids, staged_ids),
                (precision, staged_precision),
            )
        )
    ]
    for copy in copies:
        copy.start()
    for copy in copies:
        copy.wait()
    owned[share:, :] = share_rows(staged_ids[...].astype(F32), staged_precision[...])
    for c in range(width // LANES):
        lanes = slice(c * LANES, (c + 1) * LANES)
        turned[c] = staged[:, :, lanes].astype(F32).reshape(count * rows, LANES)
    half = share // 2
    weights = owned[:share, :].astype(BF16)
    weights = jnp.concatenate([weights[:half], weights[half:]], axis=1)
    even = lax.axis_index("mesh") % 2 == 0
    for out, below in ((first, even), (second, jnp.logical_not(even))):
        near = jnp.where(below, rows - 1, 0)
        beyond = jnp.where(below, rows - 2, 1)
        for i, r in enumerate((near, beyond)):
            out[i * count : (i + 1) * count, :] = probe_row(turned, r, rows).astype(BF16)
        out[2 * count : 2 * count + half, :] = weights
        small[...] = jnp.zeros_like(small)
        at = 0
        for field, r in ((0, near), (0, beyond), (1, near), (1, beyond), (2, near)):
            value = grid[field, pl.ds(r, 1), :]
            high = value.astype(BF16).astype(F32)
            small[at : at + 1, :] = high
            small[at + 1 : at + 2, :] = value - high
            at += 2
        small[at : at + 1, :LANES] = owned[share : share + 1, :]
        value = owned[share + 1 : share + 2, :]
        high = value.astype(BF16).astype(F32)
        small[at + 1 : at + 2, :LANES] = high
        small[at + 2 : at + 3, :LANES] = value - high
        out[2 * count + half :, :] = small[...].astype(BF16)


def forced_kernel(omega, grid, owned, forced, sent):
    _, rows, width = grid.shape
    count = omega.shape[1] // rows
    blocks = []
    first = row_of((PAD, width)) == 0
    for r in range(rows):
        block = jnp.concatenate(
            [
                grid[0, r : r + 1, :] * probe_row(omega, r, rows),
                jnp.where(first, grid[1, r : r + 1, :], 0.0),
            ],
            axis=0,
        )
        forced[r] = block
        blocks.append(block)
    sent[: count + PAD, :] = edge_columns(blocks)
    sent[count + PAD :, :] = owned[...]


def shares_of(refs, at, share):
    return [read_share(ref, at, share) for ref in refs]


def inner_kernel(slab_columns, share, forced, grid, from_left, from_right, *rest):
    *observed, out = rest
    rows, height, width = forced.shape
    count = height - PAD
    tangents = []
    inner = range(1, rows - 1)
    for r in inner:
        edges = edges_from(from_left, from_right, slice(0, height), r)
        tangents.append(
            tangent_row(count, forced[r], forced[r - 1], forced[r + 1], *edges, grid[2, r : r + 1, :])
        )
    result = sources(tangents, inner, shares_of(observed, height, share), slab_columns)
    for i, x in enumerate(result):
        out[i * count : (i + 1) * count, :] = x


def arrival(first, second, below):
    even = lax.axis_index("mesh") % 2 == 0
    return jnp.where(even if below else jnp.logical_not(even), first[...], second[...])


def received(x, count, share):
    small = x[2 * count + share // 2 :].astype(F32)
    parts = [small[i : i + 1] + small[i + 1 : i + 2] for i in range(0, 10, 2)]
    return parts, small[10:11, :LANES], small[11:12, :LANES] + small[12:13, :LANES]


def far_kernel(count, share, first, second, early, near, sent):
    blocks = []
    here, last = lax.axis_index("mesh"), lax.axis_size("mesh") - 1
    width = first.shape[1]
    top = row_of((PAD, width)) == 0
    at = count + PAD
    for i, inside in enumerate((here > 0, here < last)):
        x = arrival(first, second, i == 1)
        (velocity, _, viscosity, _, _), ids, precision = received(x, count, share)
        block = jnp.concatenate(
            [velocity * x[:count].astype(F32), jnp.where(top, viscosity, 0.0)], axis=0
        )
        block = jnp.where(inside, block, 0.0)
        near[i] = block
        blocks.append(block)
        weight = x[2 * count : 2 * count + share // 2].astype(F32)
        sent[at : at + share // 2, :] = weight[:, :LANES]
        sent[at + share // 2 : at + share, :] = weight[:, LANES:]
        row = row_of((PAD, LANES))
        sent[at + share : at + share + PAD, :] = jnp.where(
            row == 0, ids, jnp.where(row == 1, precision, 0.0)
        )
        at += share + PAD
    sent[: count + PAD, :] = edge_columns(blocks)


def outer_kernel(slab_columns, share, forced, near, grid, from_left, from_right, inner, *rest):
    *observed, out, sent = rest
    rows, height, width = forced.shape
    count = height - PAD
    tangents = []
    outer = (0, rows - 1)
    for r in outer:
        edges = edges_from(from_left, from_right, slice(0, height), r)
        above = near[0] if r == 0 else forced[r - 1]
        below = near[1] if r == rows - 1 else forced[r + 1]
        tangents.append(tangent_row(count, forced[r], above, below, *edges, grid[2, r : r + 1, :]))
    first, last = sources(tangents, outer, shares_of(observed, height, share), slab_columns)
    out[:count, :] = first
    out[count:, :] = last
    middle = [inner[i * count : (i + 1) * count, :] for i in range(rows - 2)]
    sent[...] = edge_columns([first, *middle, last])


def halo_kernel(slab_columns, share, forced, near, first, second, from_left, from_right, *rest):
    *observed, out = rest
    rows, height, width = forced.shape
    count = height - PAD
    here, last = lax.axis_index("mesh"), lax.axis_size("mesh") - 1
    for i in range(2):
        x = arrival(first, second, i == 1)
        (_, velocity, _, viscosity, friction), _, _ = received(x, count, share)
        far = jnp.concatenate(
            [
                velocity * x[count : 2 * count].astype(F32),
                jnp.broadcast_to(viscosity, (PAD, width)),
            ],
            axis=0,
        )
        own = forced[rows - 1 if i else 0]
        above, below = (own, far) if i else (far, own)
        edges = edges_from(from_left, from_right, slice(0, height), i)
        tangent = tangent_row(count, near[i], above, below, *edges, friction)
        at = height + i * (share + PAD)
        (source,) = sources(
            [tangent], (0 if i else rows - 1,), shares_of(observed, at, share), slab_columns
        )
        inside = here < last if i else here > 0
        out[i * count : (i + 1) * count, :] = jnp.where(inside, source, 0.0)


def packed(gram):
    half = gram.shape[0] // 2
    top, bottom = gram[:half], gram[half:]
    row, lane = row_of(top.shape), lane_of(top.shape) % (2 * half)
    mixed = jnp.where((lane >= half) & (row >= lane - half), pltpu.roll(top, half, 1), bottom)
    quarter = half // 2
    body = jnp.where(lane_of((quarter, LANES)) < 2 * half, mixed[:quarter], mixed[quarter:])
    diagonal = jnp.sum(jnp.where(row == lane - half, bottom, 0.0), axis=0, keepdims=True)
    return body, diagonal


def unpacked(body, diagonal):
    quarter = body.shape[0]
    half, size = 2 * quarter, 4 * quarter
    lane = lane_of(body.shape)
    turned = pltpu.roll(body, size, 1)
    mixed = jnp.concatenate(
        [jnp.where(lane < size, body, turned), jnp.where(lane < size, turned, body)], axis=0
    )
    row, lane = row_of(mixed.shape), lane_of(mixed.shape)
    top = pltpu.roll(mixed, LANES - half, 1)
    lower = jnp.concatenate(
        [
            jnp.where(row > lane, top, 0.0),
            jnp.where((lane < half) | ((lane < size) & (row < lane - half)), mixed, 0.0),
        ],
        axis=0,
    )
    spread = jnp.concatenate(
        [
            jnp.where(row == lane, top, 0.0),
            jnp.where(row == lane - half, diagonal, 0.0),
        ],
        axis=0,
    )
    square = jnp.concatenate([lower, jnp.zeros((LANES - size, LANES), F32)], axis=0)
    return lower + square.T[:size] + spread


def sketch_rows(rows, forced, omega, grid, sources, viscs, edges, visc_edges, parts):
    total = None
    for r in rows:
        left, right = shifted(sources[r], *edges[r])
        visc_side = shifted(viscs[r], *edges_from(*visc_edges, r))
        gradient = grid[0, r : r + 1, :] * operate_row(
            sources[r], sources[r - 1], sources[r + 1], left, right,
            [viscs[r], viscs[r - 1], viscs[r + 1], *visc_side],
            grid[2, r : r + 1, :],
        )
        value = jnp.concatenate(split(gradient + probe_row(omega, r, grid.shape[1])), axis=0)
        parts(r)[...] = value
        more = dot(value, value, 1)
        total = more if total is None else total + more
    return total


def sketch_kernel(
    cells, forced, near, omega, grid, visc_left, visc_right, from_left, from_right,
    inner, outer, halo, parts, gram,
):
    rows, height, width = forced.shape
    count = height - PAD
    sources = {r: inner[(r - 1) * count : r * count, :] for r in range(1, rows - 1)}
    viscs = {r: forced[r, count : count + 1, :] for r in range(rows)}
    for i, (r, beyond) in enumerate(((0, -1), (rows - 1, rows))):
        sources[r] = outer[i * count : (i + 1) * count, :]
        sources[beyond] = halo[i * count : (i + 1) * count, :]
        viscs[beyond] = near[i, count : count + 1, :]
    edges = {r: edges_from(from_left, from_right, slice(0, count), r) for r in range(rows)}
    total = sketch_rows(
        range(rows), forced, omega, grid, sources, viscs, edges,
        (visc_left, visc_right, slice(count, count + 1)), parts.at.__getitem__,
    )
    total = total + pltpu.roll(total, count, 1)
    total = (total[:count] + total[count:]) / cells
    body, diagonal = packed(total)
    for i in range(body.shape[0]):
        gram[:, i * LANES : (i + 1) * LANES] = body[i : i + 1, :]
    gram[:, body.shape[0] * LANES :] = diagonal


def factorize(matrix):
    size = matrix.shape[0]
    row = row_of((8, LANES))
    tiles = [matrix[t : t + 8] for t in range(0, size, 8)]
    last = size // 8 - 1

    def whole(x):
        return jnp.broadcast_to(x, (8, LANES))

    def columns_of(q, t):
        return [whole(tiles[q][:, j : j + 1]) for j in range(8 * t, 8 * t + 8)]

    def upper(block):
        return [[whole(block[c][d : d + 1]) if d >= c else None for d in range(8)] for c in range(8)]

    square = upper(columns_of(0, 0))
    columns = {q: columns_of(q, 0) for q in range(1, last + 1)}
    for t in range(last + 1):
        later = range(t + 1, last + 1)
        rows = [whole(tiles[t][c : c + 1]) for c in range(8)]
        block = columns_of(t + 1, t + 1) if t < last else None
        for c in range(8):
            root = lax.rsqrt(square[c][c])
            rows[c] = rows[c] * root
            left = [square[c][d] * root if d > c else None for d in range(8)]
            for d in range(c + 1, 8):
                for e in range(d, 8):
                    square[d][e] = square[d][e] - left[d] * left[e]
                rows[d] = rows[d] - left[d] * rows[c]
            for q in later:
                columns[q][c] = columns[q][c] * root
                for d in range(c + 1, 8):
                    columns[q][d] = columns[q][d] - left[d] * columns[q][c]
        tiles[t] = rows[0]
        for c in range(1, 8):
            tiles[t] = jnp.where(row == c, rows[c], tiles[t])
        if t < last:
            for column in columns[t + 1]:
                block = [block[e] - column * whole(column[e : e + 1]) for e in range(8)]
            square = upper(block)
            for q in later:
                for c in range(8):
                    tiles[q] = tiles[q] - columns[q][c] * rows[c]
            columns = {q: columns_of(q, t + 1) for q in range(t + 2, last + 1)}
    return jnp.concatenate(tiles, axis=0)


def basis_kernel(rank, gram, parts, basis, factor, turned, lower, sems):
    count = factor.shape[0]
    lines = gram.shape[1] // LANES - 1
    row = row_of((lines, LANES))
    body = jnp.zeros((lines, LANES), F32)
    for i in range(lines):
        body = jnp.where(row == i, gram[:, i * LANES : (i + 1) * LANES], body)
    matrix = unpacked(body, gram[:, lines * LANES :])
    row, lane = row_of(matrix.shape), lane_of(matrix.shape)
    matrix = jnp.where(lane == row + count, 1.0, matrix)
    done = factorize(matrix)
    inverse = pltpu.roll(done, count, 1)
    inverse = jnp.where((lane <= row) & (row < rank[0]), inverse, 0.0)
    high = inverse.astype(BF16).astype(F32)
    high, low = (x + pltpu.roll(x, count, 1) for x in (high, inverse - high))
    left = jnp.concatenate([high, low], axis=1).astype(BF16)
    rows = parts.shape[0]
    copies = [pltpu.make_async_copy(lower, factor, sems.at[turned.shape[0]])]
    for c in range(turned.shape[0]):
        lanes = slice(c * LANES, (c + 1) * LANES)
        for r in range(rows):
            part = parts[r, :, lanes]
            value = dot(left, jnp.concatenate([part, part], axis=0))
            turned[c, pl.ds(r, count, stride=rows), :] = value
        copy = pltpu.make_async_copy(turned.at[c], basis.at[:, lanes], sems.at[c])
        copy.start()
        copies.append(copy)
        if c == 0:
            upper = jnp.where((lane < count) & (lane >= row), done, 0.0)
            square = jnp.concatenate([upper, jnp.zeros((LANES - count, LANES), F32)], axis=0)
            lower[...] = square.T[:count, :count]
            copies[0].start()
    for copy in copies:
        copy.wait()


def ring(x, axis, step):
    size = lax.axis_size(axis)
    return lax.ppermute(x, axis, [(i, (i + step) % size) for i in range(size)])


def exchanged(x, odd):
    rows, columns = lax.axis_size("mesh"), lax.axis_size("obs")
    pairs = []
    for i in range(rows):
        partner = i + 1 if i % 2 == odd else i - 1
        for c in range(columns):
            target = partner * columns + c if 0 <= partner < rows else i * columns + (c ^ 1)
            pairs.append((i * columns + c, target))
    return lax.ppermute(x, ("mesh", "obs"), pairs)


def summed(x):
    rows, columns = lax.axis_size("mesh"), lax.axis_size("obs")
    x = x + ring(x, "obs", 1) if columns == 2 else lax.psum(x, "obs")
    step = 1
    while step < rows:
        offsets = (step, 2 * step, 3 * step) if step == 1 else (step, 3 * step, 2 * step)
        if rows % (4 * step):
            offsets = (step,)
        pieces = [
            lax.ppermute(
                x,
                ("mesh", "obs"),
                [
                    (i * columns + c, (i ^ offset) * columns + (c ^ 1))
                    for i in range(rows)
                    for c in range(columns)
                ],
            )
            for offset in offsets
        ]
        for piece in pieces:
            x = x + piece
        step = step * (len(offsets) + 1)
    return x


def both_sides(x):
    other = ring(x, "obs", 1)
    return other, (other if lax.axis_size("obs") == 2 else ring(x, "obs", -1))


def all_shares(x, sides):
    size = lax.axis_size("obs")
    if size == 2:
        return [x, sides[0]]
    gathered = lax.all_gather(x, "obs")
    here = lax.axis_index("obs")
    return [lax.dynamic_index_in_dim(gathered, (here + i) % size, 0, False) for i in range(size)]


def per_device(probes, velocity, viscosity, friction, obs_block, obs_weight, obs_prec, rank):
    count, rows, width = probes.shape
    share = obs_weight.shape[1]
    mesh_size, obs_size = lax.axis_size("mesh"), lax.axis_size("obs")
    slab_columns = width * obs_size // LANES
    cells = rows * width * mesh_size * obs_size
    height = count + PAD

    payload = (2 * count + share // 2 + 16, width)
    turned = (width // LANES, rows * count, LANES)
    omega, first, second, grid, owned = call(
        edges_kernel,
        [
            (turned, F32),
            (payload, BF16),
            (payload, BF16),
            ((3, rows, width), F32),
            ((share + PAD, LANES), F32),
        ],
        (probes, velocity, viscosity, friction, obs_weight, obs_block, obs_prec),
        [
            pltpu.VMEM(probes.shape, probes.dtype),
            pltpu.VMEM(obs_block.shape, obs_block.dtype),
            pltpu.VMEM(obs_prec.shape, F32),
            pltpu.VMEM((16, width), F32),
            pltpu.SemaphoreType.DMA((7,)),
        ],
        space=pltpu.HBM,
        name="edges",
    )
    arrived = exchanged(first, 0), exchanged(second, 1)

    forced, sent = call(
        forced_kernel,
        [((rows, height, width), F32), ((height + share + PAD, LANES), F32)],
        (omega, grid, owned),
        name="forced",
    )
    sides = both_sides(sent)
    observed = all_shares(sent, sides)
    (inner,) = call(
        functools.partial(inner_kernel, slab_columns, share),
        [(((rows - 2) * count, width), F32)],
        (forced, grid, *sides, *observed),
        name="inner",
    )
    near, far_sent = call(
        functools.partial(far_kernel, count, share),
        [((2, height, width), F32), ((height + 2 * (share + PAD), LANES), F32)],
        (*arrived, inner),
        name="far",
    )
    far_sides = both_sides(far_sent)
    far_observed = all_shares(far_sent, far_sides)
    outer, source_sent = call(
        functools.partial(outer_kernel, slab_columns, share),
        [((2 * count, width), F32), ((count, LANES), F32)],
        (forced, near, grid, *sides, inner, *observed),
        name="outer",
    )
    source_sides = both_sides(source_sent)
    (halo,) = call(
        functools.partial(halo_kernel, slab_columns, share),
        [((2 * count, width), F32)],
        (forced, near, *arrived, *far_sides, *far_observed),
        name="halo",
    )
    parts, gram = call(
        functools.partial(sketch_kernel, cells),
        [((rows, 2 * count, width), BF16), ((1, 17 * LANES), F32)],
        (forced, near, omega, grid, *sides, *source_sides, inner, outer, halo),
        name="sketch",
    )
    gram = summed(gram)
    basis, factor = pl.pallas_call(
        basis_kernel,
        out_shape=[
            jax.ShapeDtypeStruct((count * rows, width), F32),
            jax.ShapeDtypeStruct((count, count), F32),
        ],
        in_specs=[pl.BlockSpec(memory_space=pltpu.SMEM)] + [pl.BlockSpec(memory_space=pltpu.VMEM)] * 2,
        out_specs=[pl.BlockSpec(memory_space=pl.ANY)] * 2,
        scratch_shapes=[
            pltpu.VMEM(turned, F32),
            pltpu.VMEM((count, count), F32),
            pltpu.SemaphoreType.DMA((width // LANES + 1,)),
        ],
        compiler_params=pltpu.CompilerParams(vmem_limit_bytes=8 * 2**20),
        name="basis",
    )(rank, gram, parts)
    return basis.reshape(count, rows, width), factor


def solution(mesh):
    in_specs = (
        P(None, "mesh", "obs"),
        P("mesh", "obs"),
        P("mesh", "obs"),
        P("mesh", "obs"),
        P("mesh", "obs"),
        P("mesh", "obs", None),
        P("mesh", "obs"),
        P(),
    )
    out_specs = (P(None, "mesh", "obs"), P())
    return jax.shard_map(
        per_device, mesh=mesh, in_specs=in_specs, out_specs=out_specs, check_vma=False
    )
```

```python
import functools

import jax
import jax.numpy as jnp
from jax import lax
from jax.experimental import pallas as pl
from jax.experimental.pallas import tpu as pltpu
from jax.sharding import PartitionSpec as P

LANES = 128
RIGHT = 16
PAD = 8
F32 = jnp.float32
BF16 = jnp.bfloat16


def split(x):
    high = x.astype(BF16)
    return high, (x - high.astype(F32)).astype(BF16)


def lane_of(shape):
    return lax.broadcasted_iota(jnp.int32, shape, 1)


def row_of(shape):
    return lax.broadcasted_iota(jnp.int32, shape, 0)


def dot(a, b, rhs_dim=0):
    return lax.dot_general(
        a, b, (((1,), (rhs_dim,)), ((), ())), preferred_element_type=F32
    )


def call(body, outs, args, scratch=(), flops=0, space=pltpu.VMEM, name=None):
    if space != pltpu.VMEM:
        args = [pltpu.with_memory_space_constraint(x, space) for x in args]
    outs = [jax.ShapeDtypeStruct(shape, kind) for shape, kind in outs]
    return pl.pallas_call(
        body,
        out_shape=outs,
        in_specs=[pl.BlockSpec(memory_space=space)] * len(args),
        scratch_shapes=list(scratch),
        compiler_params=pltpu.CompilerParams(vmem_limit_bytes=8 * 2**20),
        cost_estimate=pl.CostEstimate(
            flops=flops, bytes_accessed=2**20, transcendentals=0
        ),
        name=name,
    )(*args)


def shifted(x, left_edge, right_edge):
    width = x.shape[1]
    lane = lane_of((x.shape[0], LANES))
    left, right = pltpu.roll(x, 1, 1), pltpu.roll(x, width - 1, 1)
    first = jnp.where(lane == 0, left_edge, left[:, :LANES])
    last = jnp.where(lane == LANES - 1, right_edge, right[:, width - LANES :])
    return (
        jnp.concatenate([first, left[:, LANES:]], axis=1),
        jnp.concatenate([right[:, : width - LANES], last], axis=1),
    )


def operate_row(centre, above, below, left, right, visc, friction):
    own, *others = visc
    faces = [0.5 * (own + other) for other in others]
    result = (friction + faces[0] + faces[1] + faces[2] + faces[3]) * centre
    for face, value in zip(faces, (above, below, left, right)):
        result = result - face * value
    return result


def forced_row(count, centre, above, below, left_edge, right_edge, friction):
    left, right = shifted(centre, left_edge, right_edge)
    visc = [x[count : count + 1] for x in (centre, above, below, left, right)]
    values = [x[:count] for x in (centre, above, below, left, right)]
    return operate_row(*values, visc, friction)


def tangent_row(*args):
    return forced_row(*args).astype(BF16)


def with_edges(count, result, centre, left_edge, right_edge):
    width = centre.shape[1]
    lane = lane_of((count, LANES))
    tiles = [result[:, at : at + LANES] for at in range(0, width, LANES)]
    for at, edge, place in ((0, left_edge, 0), (-1, right_edge, LANES - 1)):
        x = centre[:, :LANES] if at == 0 else centre[:, width - LANES :]
        visc = edge[count : count + 1]
        face = 0.5 * (x[count : count + 1] + visc)
        tiles[at] = tiles[at] + jnp.where(lane == place, (0.5 * visc) * x[:count] - face * edge[:count], 0.0)
    return jnp.concatenate(tiles, axis=1)


def edge_columns(rows, out=None):
    for at, x in rows.items():
        height, width = x.shape
        lane = lane_of((height, LANES))
        out = jnp.zeros((height, LANES), F32) if out is None else out
        out = jnp.where(lane == at, x[:, :1], out)
        out = jnp.where(lane == RIGHT + at, x[:, width - 1 :], out)
    return out


def edges_from(left_ref, right_ref, rows, at):
    here, last = lax.axis_index("obs"), lax.axis_size("obs") - 1
    left = left_ref[rows, RIGHT + at : RIGHT + at + 1]
    right = right_ref[rows, at : at + 1]
    return jnp.where(here > 0, left, 0.0), jnp.where(here < last, right, 0.0)


def sources(tangents, grid_rows, observed, slab_columns):
    count, width = tangents[0].shape
    owned = width // LANES
    first = lax.axis_index("obs") * owned
    blocks = jnp.concatenate(
        [t[:, c * LANES : (c + 1) * LANES] for t in tangents for c in range(owned)], axis=0
    )
    doubled = jnp.concatenate([blocks, blocks], axis=1)
    total = None
    for at in range(0, len(observed), 2):
        pair = observed[at : at + 2]
        if len(pair) == 1:
            pair = pair + [tuple(jnp.zeros_like(x) for x in pair[0])]
        high = jnp.concatenate([x[0] for x in pair], axis=0)
        share = pair[0][0].shape[0]
        lane = lane_of((1, LANES))
        ids = jnp.where(lane < share, pair[0][2], pltpu.roll(pair[1][2], share, 1))
        ids = ids.astype(jnp.int32)
        precision = jnp.where(lane < share, pair[0][3], pltpu.roll(pair[1][3], share, 1))
        low = jnp.concatenate([x[1] for x in pair], axis=0)
        misfit = dot(doubled, jnp.concatenate([high, low], axis=1), 1)
        kept = []
        for i, row in enumerate(grid_rows):
            for c in range(owned):
                k = i * owned + c
                scale = jnp.where(ids == row * slab_columns + first + c, precision, 0.0)
                kept.append(misfit[k * count : (k + 1) * count] * scale)
        misfit_high, misfit_low = split(jnp.concatenate(kept, axis=0))
        halves = jnp.concatenate([misfit_high, misfit_low], axis=1)
        both = dot(
            halves,
            jnp.concatenate(
                [
                    jnp.concatenate([high, low], axis=1),
                    jnp.concatenate([high, jnp.zeros_like(low)], axis=1),
                ],
                axis=0,
            ),
        )
        part = both[:, :LANES] + both[:, LANES:]
        total = part if total is None else total + part
    return [
        jnp.concatenate(
            [total[(i * owned + c) * count : (i * owned + c + 1) * count] for c in range(owned)],
            axis=1,
        )
        for i in range(len(tangents))
    ]


def share_rows(ids, precision):
    out = jnp.zeros((PAD, LANES), F32)
    row = row_of(out.shape)

    def wide(x):
        return jnp.concatenate([x, jnp.zeros((1, LANES - x.shape[1]), F32)], axis=1)

    return jnp.where(row == 0, wide(ids), jnp.where(row == 1, wide(precision), out))


def read_share(ref, at, share):
    high, low = split(ref[at : at + share, :])
    return high, low, ref[at + share : at + share + 1, :], ref[at + share + 1 : at + share + 2, :]


def probe_row(turned, r, rows):
    parts, cells, _ = turned.shape
    return jnp.concatenate(
        [turned[c, pl.ds(r, cells // rows, stride=rows), :] for c in range(parts)], axis=1
    )


def edges_kernel(
    probes, velocity, viscosity, friction, weight, ids, precision,
    turned, first, second, grid, owned, staged, staged_ids, staged_precision, small, sems,
):
    count, rows, width = probes.shape
    share = weight.shape[1]
    copies = [
        pltpu.make_async_copy(source, target, sems.at[i])
        for i, (source, target) in enumerate(
            (
                (probes, staged),
                (velocity, grid.at[0]),
                (viscosity, grid.at[1]),
                (friction, grid.at[2]),
                (weight.at[0], owned.at[:share]),
                (ids, staged_ids),
                (precision, staged_precision),
            )
        )
    ]
    for copy in copies:
        copy.start()
    for copy in copies[1:]:
        copy.wait()
    owned[share:, :] = share_rows(staged_ids[...].astype(F32), staged_precision[...])
    half = share // 2
    weights = owned[:share, :].astype(BF16)
    weights = jnp.concatenate([weights[:half], weights[half:]], axis=1)
    even = lax.axis_index("mesh") % 2 == 0
    sides = []
    for out, below in ((first, even), (second, jnp.logical_not(even))):
        near = jnp.where(below, rows - 1, 0)
        beyond = jnp.where(below, rows - 2, 1)
        sides.append((out, near, beyond))
        out[2 * count : 2 * count + half, :] = weights
        small[...] = jnp.zeros_like(small)
        at = 0
        for field, r in ((0, near), (0, beyond), (1, near), (1, beyond), (2, near)):
            value = grid[field, pl.ds(r, 1), :]
            high = value.astype(BF16).astype(F32)
            small[at : at + 1, :] = high
            small[at + 1 : at + 2, :] = value - high
            at += 2
        small[at : at + 1, :LANES] = owned[share : share + 1, :]
        value = owned[share + 1 : share + 2, :]
        high = value.astype(BF16).astype(F32)
        small[at + 1 : at + 2, :LANES] = high
        small[at + 2 : at + 3, :LANES] = value - high
        out[2 * count + half :, :] = small[...].astype(BF16)
    copies[0].wait()
    for c in range(width // LANES):
        lanes = slice(c * LANES, (c + 1) * LANES)
        turned[c] = staged[:, :, lanes].astype(F32).reshape(count * rows, LANES)
    for out, *picked in sides:
        for i, r in enumerate(picked):
            out[i * count : (i + 1) * count, :] = probe_row(turned, r, rows).astype(BF16)


def forced_kernel(omega, grid, owned, forced, sent):
    _, rows, width = grid.shape
    count = omega.shape[1] // rows
    blocks = []
    first = row_of((PAD, width)) == 0
    for r in range(rows):
        block = jnp.concatenate(
            [
                grid[0, r : r + 1, :] * probe_row(omega, r, rows),
                jnp.where(first, grid[1, r : r + 1, :], 0.0),
            ],
            axis=0,
        )
        forced[r] = block
        blocks.append(block)
    sent[: count + PAD, :] = edge_columns(dict(enumerate(blocks)))
    sent[count + PAD :, :] = owned[...]


def shares_of(refs, at, share):
    return [read_share(ref, at, share) for ref in refs]


def inner_kernel(slab_columns, share, forced, grid, from_left, from_right, *rest):
    *observed, out, edge_sources = rest
    rows, height, width = forced.shape
    count = height - PAD
    tangents = []
    inner = range(1, rows - 1)
    for r in inner:
        edges = edges_from(from_left, from_right, slice(0, height), r)
        tangents.append(
            tangent_row(count, forced[r], forced[r - 1], forced[r + 1], *edges, grid[2, r : r + 1, :])
        )
    result = sources(tangents, inner, shares_of(observed, height, share), slab_columns)
    for i, x in enumerate(result):
        out[i * count : (i + 1) * count, :] = x
    edge_sources[...] = edge_columns(dict(zip(inner, result)))


def arrival(first, second, below):
    even = lax.axis_index("mesh") % 2 == 0
    return jnp.where(even if below else jnp.logical_not(even), first[...], second[...])


def received(x, count, share):
    small = x[2 * count + share // 2 :].astype(F32)
    parts = [small[i : i + 1] + small[i + 1 : i + 2] for i in range(0, 10, 2)]
    return parts, small[10:11, :LANES], small[11:12, :LANES] + small[12:13, :LANES]


def far_kernel(count, share, first, second, early, near, sent):
    blocks = []
    here, last = lax.axis_index("mesh"), lax.axis_size("mesh") - 1
    width = first.shape[1]
    top = row_of((PAD, width)) == 0
    at = count + PAD
    for i, inside in enumerate((here > 0, here < last)):
        x = arrival(first, second, i == 1)
        (velocity, _, viscosity, _, _), ids, precision = received(x, count, share)
        block = jnp.concatenate(
            [velocity * x[:count].astype(F32), jnp.where(top, viscosity, 0.0)], axis=0
        )
        block = jnp.where(inside, block, 0.0)
        near[i] = block
        blocks.append(block)
        weight = x[2 * count : 2 * count + share // 2].astype(F32)
        sent[at : at + share // 2, :] = weight[:, :LANES]
        sent[at + share // 2 : at + share, :] = weight[:, LANES:]
        row = row_of((PAD, LANES))
        sent[at + share : at + share + PAD, :] = jnp.where(
            row == 0, ids, jnp.where(row == 1, precision, 0.0)
        )
        at += share + PAD
    sent[: count + PAD, :] = edge_columns(dict(enumerate(blocks)))


def outer_kernel(
    slab_columns, share, forced, near, grid, from_left, from_right, inner_edges, first_in, second_in, *rest
):
    *observed, out, sent, beside = rest
    rows, height, width = forced.shape
    count = height - PAD
    tangents = []
    outer = (0, rows - 1)
    for r in outer:
        edges = edges_from(from_left, from_right, slice(0, height), r)
        above = near[0] if r == 0 else forced[r - 1]
        below = near[1] if r == rows - 1 else forced[r + 1]
        tangents.append(tangent_row(count, forced[r], above, below, *edges, grid[2, r : r + 1, :]))
    first, last = sources(tangents, outer, shares_of(observed, height, share), slab_columns)
    out[:count, :] = first
    out[count:, :] = last
    sent[...] = edge_columns({0: first, rows - 1: last}, inner_edges[...])
    for i in range(2):
        x = arrival(first_in, second_in, i == 1)
        (_, velocity, _, viscosity, friction), _, _ = received(x, count, share)
        far = jnp.concatenate(
            [
                velocity * x[count : 2 * count].astype(F32),
                jnp.broadcast_to(viscosity, (PAD, width)),
            ],
            axis=0,
        )
        own = forced[rows - 1 if i else 0]
        above, below = (own, far) if i else (far, own)
        beside[i * count : (i + 1) * count, :] = forced_row(count, near[i], above, below, 0.0, 0.0, friction)


def halo_kernel(slab_columns, share, rows, near, beside, from_left, from_right, *rest):
    *observed, out = rest
    _, height, width = near.shape
    count = height - PAD
    here, last = lax.axis_index("mesh"), lax.axis_size("mesh") - 1
    for i in range(2):
        edges = edges_from(from_left, from_right, slice(0, height), i)
        tangent = with_edges(count, beside[i * count : (i + 1) * count, :], near[i], *edges)
        at = height + i * (share + PAD)
        (source,) = sources(
            [tangent.astype(BF16)], (0 if i else rows - 1,), shares_of(observed, at, share), slab_columns
        )
        inside = here < last if i else here > 0
        out[i * count : (i + 1) * count, :] = jnp.where(inside, source, 0.0)


def packed(gram):
    half = gram.shape[0] // 2
    top, bottom = gram[:half], gram[half:]
    row, lane = row_of(top.shape), lane_of(top.shape) % (2 * half)
    mixed = jnp.where((lane >= half) & (row >= lane - half), pltpu.roll(top, half, 1), bottom)
    quarter = half // 2
    body = jnp.where(lane_of((quarter, LANES)) < 2 * half, mixed[:quarter], mixed[quarter:])
    diagonal = jnp.sum(jnp.where(row == lane - half, bottom, 0.0), axis=0, keepdims=True)
    return body, diagonal


def unpacked(body, diagonal):
    quarter = body.shape[0]
    half, size = 2 * quarter, 4 * quarter
    lane = lane_of(body.shape)
    turned = pltpu.roll(body, size, 1)
    mixed = jnp.concatenate(
        [jnp.where(lane < size, body, turned), jnp.where(lane < size, turned, body)], axis=0
    )
    row, lane = row_of(mixed.shape), lane_of(mixed.shape)
    top = pltpu.roll(mixed, LANES - half, 1)
    lower = jnp.concatenate(
        [
            jnp.where(row > lane, top, 0.0),
            jnp.where((lane < half) | ((lane < size) & (row < lane - half)), mixed, 0.0),
        ],
        axis=0,
    )
    spread = jnp.concatenate(
        [
            jnp.where(row == lane, top, 0.0),
            jnp.where(row == lane - half, diagonal, 0.0),
        ],
        axis=0,
    )
    square = jnp.concatenate([lower, jnp.zeros((LANES - size, LANES), F32)], axis=0)
    return lower + square.T[:size] + spread


def sketch_row(r, omega, grid, sources, viscs, edges, visc_edges):
    source, above, below = sources
    left, right = shifted(source, *edges)
    gradient = grid[0, r : r + 1, :] * operate_row(
        source, above, below, left, right,
        [*viscs, *shifted(viscs[0], *visc_edges)],
        grid[2, r : r + 1, :],
    )
    return gradient + probe_row(omega, r, grid.shape[1])


def middle_kernel(forced, omega, grid, visc_left, visc_right, inner, out):
    rows, height, width = forced.shape
    count = height - PAD
    none = jnp.zeros((count, width), F32)
    for r in range(1, rows - 1):
        sources = [
            inner[(i - 1) * count : i * count, :] if 0 < i < rows - 1 else none for i in (r, r - 1, r + 1)
        ]
        out[(r - 1) * count : r * count, :] = sketch_row(
            r, omega, grid, sources,
            [forced[i, count : count + 1, :] for i in (r, r - 1, r + 1)],
            (0.0, 0.0),
            edges_from(visc_left, visc_right, slice(count, count + 1), r),
        )


def sketch_kernel(
    cells, forced, near, omega, grid, visc_left, visc_right, from_left, from_right,
    inner, outer, halo, middle, parts, gram,
):
    rows, height, width = forced.shape
    count = height - PAD
    lane = lane_of((count, LANES))
    total = jnp.zeros((2 * count, 2 * count), F32)
    for r in range(rows):
        edges = edges_from(from_left, from_right, slice(0, count), r)
        visc_edges = edges_from(visc_left, visc_right, slice(count, count + 1), r)
        own = forced[r, count : count + 1, :]
        if 0 < r < rows - 1:
            value = middle[(r - 1) * count : r * count, :]
            for beyond, source in ((0, outer[:count, :]), (rows - 1, outer[count:, :])):
                if abs(r - beyond) == 1:
                    face = 0.5 * (own + forced[beyond, count : count + 1, :])
                    value = value - (grid[0, r : r + 1, :] * face) * source
            tiles = [value[:, at : at + LANES] for at in range(0, width, LANES)]
            for at, edge, visc, place in ((0, edges[0], visc_edges[0], 0), (-1, edges[1], visc_edges[1], LANES - 1)):
                lanes = slice(0, LANES) if at == 0 else slice(width - LANES, width)
                face = grid[0, r : r + 1, lanes] * (0.5 * (own[:, lanes] + visc))
                tiles[at] = tiles[at] - jnp.where(lane == place, face * edge, 0.0)
            value = jnp.concatenate(tiles, axis=1)
        else:
            i = min(r, 1)
            mine, beside = (outer[i * count : (i + 1) * count, :], halo[i * count : (i + 1) * count, :])
            next_row = 1 if r == 0 else r - 1
            inside = inner[(next_row - 1) * count : next_row * count, :]
            sources = (mine, inside, beside) if i else (mine, beside, inside)
            viscs = forced[next_row, count : count + 1, :], near[i, count : count + 1, :]
            value = sketch_row(
                r, omega, grid, sources, (own, *(viscs if i else viscs[::-1])), edges, visc_edges
            )
        value = jnp.concatenate(split(value), axis=0)
        parts[r] = value
        total = total + dot(value, value, 1)
    total = total + pltpu.roll(total, count, 1)
    total = (total[:count] + total[count:]) / cells
    body, diagonal = packed(total)
    for i in range(body.shape[0]):
        gram[:, i * LANES : (i + 1) * LANES] = body[i : i + 1, :]
    gram[:, body.shape[0] * LANES :] = diagonal


def factorize(matrix):
    size = matrix.shape[0]
    row = row_of((8, LANES))
    tiles = [matrix[t : t + 8] for t in range(0, size, 8)]
    last = size // 8 - 1

    def whole(x):
        return jnp.broadcast_to(x, (8, LANES))

    def columns_of(q, t):
        return [whole(tiles[q][:, j : j + 1]) for j in range(8 * t, 8 * t + 8)]

    def upper(block):
        return [[whole(block[c][d : d + 1]) if d >= c else None for d in range(8)] for c in range(8)]

    square = upper(columns_of(0, 0))
    columns = {q: columns_of(q, 0) for q in range(1, last + 1)}
    for t in range(last + 1):
        later = range(t + 1, last + 1)
        rows = [whole(tiles[t][c : c + 1]) for c in range(8)]
        block = columns_of(t + 1, t + 1) if t < last else None
        for c in range(8):
            root = lax.rsqrt(square[c][c])
            rows[c] = rows[c] * root
            left = [square[c][d] * root if d > c else None for d in range(8)]
            for d in range(c + 1, 8):
                for e in range(d, 8):
                    square[d][e] = square[d][e] - left[d] * left[e]
                rows[d] = rows[d] - left[d] * rows[c]
            for q in later:
                columns[q][c] = columns[q][c] * root
                for d in range(c + 1, 8):
                    columns[q][d] = columns[q][d] - left[d] * columns[q][c]
        tiles[t] = rows[0]
        for c in range(1, 8):
            tiles[t] = jnp.where(row == c, rows[c], tiles[t])
        if t < last:
            for column in columns[t + 1]:
                block = [block[e] - column * whole(column[e : e + 1]) for e in range(8)]
            square = upper(block)
            for q in later:
                for c in range(8):
                    tiles[q] = tiles[q] - columns[q][c] * rows[c]
            columns = {q: columns_of(q, t + 1) for q in range(t + 2, last + 1)}
    return jnp.concatenate(tiles, axis=0)


def basis_kernel(rank, gram, parts, basis, factor, turned, lower, sems):
    count = factor.shape[0]
    lines = gram.shape[1] // LANES - 1
    row = row_of((lines, LANES))
    body = jnp.zeros((lines, LANES), F32)
    for i in range(lines):
        body = jnp.where(row == i, gram[:, i * LANES : (i + 1) * LANES], body)
    matrix = unpacked(body, gram[:, lines * LANES :])
    row, lane = row_of(matrix.shape), lane_of(matrix.shape)
    matrix = jnp.where(lane == row + count, 1.0, matrix)
    done = factorize(matrix)
    inverse = pltpu.roll(done, count, 1)
    inverse = jnp.where((lane <= row) & (row < rank[0]), inverse, 0.0)
    high = inverse.astype(BF16).astype(F32)
    high, low = (x + pltpu.roll(x, count, 1) for x in (high, inverse - high))
    left = jnp.concatenate([high, low], axis=1).astype(BF16)
    rows = parts.shape[0]
    copies = [pltpu.make_async_copy(lower, factor, sems.at[turned.shape[0]])]
    for c in range(turned.shape[0]):
        lanes = slice(c * LANES, (c + 1) * LANES)
        for r in range(rows):
            part = parts[r, :, lanes]
            value = dot(left, jnp.concatenate([part, part], axis=0))
            turned[c, pl.ds(r, count, stride=rows), :] = value
        copy = pltpu.make_async_copy(turned.at[c], basis.at[:, lanes], sems.at[c])
        copy.start()
        copies.append(copy)
        if c == 0:
            upper = jnp.where((lane < count) & (lane >= row), done, 0.0)
            square = jnp.concatenate([upper, jnp.zeros((LANES - count, LANES), F32)], axis=0)
            lower[...] = square.T[:count, :count]
            copies[0].start()
    for copy in copies:
        copy.wait()


def ring(x, axis, step):
    size = lax.axis_size(axis)
    return lax.ppermute(x, axis, [(i, (i + step) % size) for i in range(size)])


def exchanged(x, odd):
    rows, columns = lax.axis_size("mesh"), lax.axis_size("obs")
    pairs = []
    for i in range(rows):
        partner = i + 1 if i % 2 == odd else i - 1
        for c in range(columns):
            target = partner * columns + c if 0 <= partner < rows else i * columns + (c ^ 1)
            pairs.append((i * columns + c, target))
    return lax.ppermute(x, ("mesh", "obs"), pairs)


def summed(x):
    rows, columns = lax.axis_size("mesh"), lax.axis_size("obs")
    x = x + ring(x, "obs", 1) if columns == 2 else lax.psum(x, "obs")
    step = 1
    while step < rows:
        offsets = (step, 2 * step, 3 * step) if step == 1 else (step, 3 * step, 2 * step)
        if rows % (4 * step):
            offsets = (step,)
        pieces = [
            lax.ppermute(
                x,
                ("mesh", "obs"),
                [
                    (i * columns + c, (i ^ offset) * columns + (c ^ 1))
                    for i in range(rows)
                    for c in range(columns)
                ],
            )
            for offset in offsets
        ]
        for piece in pieces:
            x = x + piece
        step = step * (len(offsets) + 1)
    return x


def both_sides(x):
    other = ring(x, "obs", 1)
    return other, (other if lax.axis_size("obs") == 2 else ring(x, "obs", -1))


def all_shares(x, sides):
    size = lax.axis_size("obs")
    if size == 2:
        return [x, sides[0]]
    gathered = lax.all_gather(x, "obs")
    here = lax.axis_index("obs")
    return [lax.dynamic_index_in_dim(gathered, (here + i) % size, 0, False) for i in range(size)]


def per_device(probes, velocity, viscosity, friction, obs_block, obs_weight, obs_prec, rank):
    count, rows, width = probes.shape
    share = obs_weight.shape[1]
    mesh_size, obs_size = lax.axis_size("mesh"), lax.axis_size("obs")
    slab_columns = width * obs_size // LANES
    cells = rows * width * mesh_size * obs_size
    height = count + PAD

    payload = (2 * count + share // 2 + 16, width)
    turned = (width // LANES, rows * count, LANES)
    omega, first, second, grid, owned = call(
        edges_kernel,
        [
            (turned, F32),
            (payload, BF16),
            (payload, BF16),
            ((3, rows, width), F32),
            ((share + PAD, LANES), F32),
        ],
        (probes, velocity, viscosity, friction, obs_weight, obs_block, obs_prec),
        [
            pltpu.VMEM(probes.shape, probes.dtype),
            pltpu.VMEM(obs_block.shape, obs_block.dtype),
            pltpu.VMEM(obs_prec.shape, F32),
            pltpu.VMEM((16, width), F32),
            pltpu.SemaphoreType.DMA((7,)),
        ],
        space=pltpu.HBM,
        name="edges",
    )
    arrived = exchanged(first, 0), exchanged(second, 1)

    forced, sent = call(
        forced_kernel,
        [((rows, height, width), F32), ((height + share + PAD, LANES), F32)],
        (omega, grid, owned),
        name="forced",
    )
    sides = both_sides(sent)
    observed = all_shares(sent, sides)
    inner, inner_edges = call(
        functools.partial(inner_kernel, slab_columns, share),
        [(((rows - 2) * count, width), F32), ((count, LANES), F32)],
        (forced, grid, *sides, *observed),
        name="inner",
    )
    (middle,) = call(
        middle_kernel,
        [(((rows - 2) * count, width), F32)],
        (forced, omega, grid, *sides, inner),
        name="middle",
    )
    near, far_sent = call(
        functools.partial(far_kernel, count, share),
        [((2, height, width), F32), ((height + 2 * (share + PAD), LANES), F32)],
        (*arrived, middle),
        name="far",
    )
    far_sides = both_sides(far_sent)
    far_observed = all_shares(far_sent, far_sides)
    outer, source_sent, beside = call(
        functools.partial(outer_kernel, slab_columns, share),
        [((2 * count, width), F32), ((count, LANES), F32), ((2 * count, width), F32)],
        (forced, near, grid, *sides, inner_edges, *arrived, *observed),
        name="outer",
    )
    source_sides = both_sides(source_sent)
    (halo,) = call(
        functools.partial(halo_kernel, slab_columns, share, rows),
        [((2 * count, width), F32)],
        (near, beside, *far_sides, *far_observed),
        name="halo",
    )
    parts, gram = call(
        functools.partial(sketch_kernel, cells),
        [((rows, 2 * count, width), BF16), ((1, 17 * LANES), F32)],
        (forced, near, omega, grid, *sides, *source_sides, inner, outer, halo, middle),
        name="sketch",
    )
    gram = summed(gram)
    basis, factor = pl.pallas_call(
        basis_kernel,
        out_shape=[
            jax.ShapeDtypeStruct((count * rows, width), F32),
            jax.ShapeDtypeStruct((count, count), F32),
        ],
        in_specs=[pl.BlockSpec(memory_space=pltpu.SMEM)] + [pl.BlockSpec(memory_space=pltpu.VMEM)] * 2,
        out_specs=[pl.BlockSpec(memory_space=pl.ANY)] * 2,
        scratch_shapes=[
            pltpu.VMEM(turned, F32),
            pltpu.VMEM((count, count), F32),
            pltpu.SemaphoreType.DMA((width // LANES + 1,)),
        ],
        compiler_params=pltpu.CompilerParams(vmem_limit_bytes=8 * 2**20),
        name="basis",
    )(rank, gram, parts)
    return basis.reshape(count, rows, width), factor


def solution(mesh):
    in_specs = (
        P(None, "mesh", "obs"),
        P("mesh", "obs"),
        P("mesh", "obs"),
        P("mesh", "obs"),
        P("mesh", "obs"),
        P("mesh", "obs", None),
        P("mesh", "obs"),
        P(),
    )
    out_specs = (P(None, "mesh", "obs"), P())
    return jax.shard_map(
        per_device, mesh=mesh, in_specs=in_specs, out_specs=out_specs, check_vma=False
    )
```

```python
import functools

import jax
import jax.numpy as jnp
from jax import lax
from jax.experimental import pallas as pl
from jax.experimental.pallas import tpu as pltpu
from jax.sharding import PartitionSpec as P

LANES = 128
RIGHT = 16
PAD = 8
F32 = jnp.float32
BF16 = jnp.bfloat16


def split(x):
    high = x.astype(BF16)
    return high, (x - high.astype(F32)).astype(BF16)


def lane_of(shape):
    return lax.broadcasted_iota(jnp.int32, shape, 1)


def row_of(shape):
    return lax.broadcasted_iota(jnp.int32, shape, 0)


def dot(a, b, rhs_dim=0):
    return lax.dot_general(
        a, b, (((1,), (rhs_dim,)), ((), ())), preferred_element_type=F32
    )


def call(body, outs, args, scratch=(), flops=0, space=pltpu.VMEM, name=None):
    if space != pltpu.VMEM:
        args = [pltpu.with_memory_space_constraint(x, space) for x in args]
    outs = [jax.ShapeDtypeStruct(shape, kind) for shape, kind in outs]
    return pl.pallas_call(
        body,
        out_shape=outs,
        in_specs=[pl.BlockSpec(memory_space=space)] * len(args),
        scratch_shapes=list(scratch),
        compiler_params=pltpu.CompilerParams(vmem_limit_bytes=8 * 2**20),
        cost_estimate=pl.CostEstimate(
            flops=flops, bytes_accessed=2**20, transcendentals=0
        ),
        name=name,
    )(*args)


def shifted(x, left_edge, right_edge):
    width = x.shape[1]
    lane = lane_of((x.shape[0], LANES))
    left, right = pltpu.roll(x, 1, 1), pltpu.roll(x, width - 1, 1)
    first = jnp.where(lane == 0, left_edge, left[:, :LANES])
    last = jnp.where(lane == LANES - 1, right_edge, right[:, width - LANES :])
    return (
        jnp.concatenate([first, left[:, LANES:]], axis=1),
        jnp.concatenate([right[:, : width - LANES], last], axis=1),
    )


def operate_row(centre, above, below, left, right, visc, friction):
    own, *others = visc
    faces = [0.5 * (own + other) for other in others]
    result = (friction + faces[0] + faces[1] + faces[2] + faces[3]) * centre
    for face, value in zip(faces, (above, below, left, right)):
        result = result - face * value
    return result


def forced_row(count, centre, above, below, left_edge, right_edge, friction):
    left, right = shifted(centre, left_edge, right_edge)
    visc = [x[count : count + 1] for x in (centre, above, below, left, right)]
    values = [x[:count] for x in (centre, above, below, left, right)]
    return operate_row(*values, visc, friction)


def tangent_row(*args):
    return forced_row(*args).astype(BF16)


def with_edges(count, result, centre, left_edge, right_edge):
    width = centre.shape[1]
    lane = lane_of((count, LANES))
    tiles = [result[:, at : at + LANES] for at in range(0, width, LANES)]
    for at, edge, place in ((0, left_edge, 0), (-1, right_edge, LANES - 1)):
        x = centre[:, :LANES] if at == 0 else centre[:, width - LANES :]
        visc = edge[count : count + 1]
        face = 0.5 * (x[count : count + 1] + visc)
        tiles[at] = tiles[at] + jnp.where(lane == place, (0.5 * visc) * x[:count] - face * edge[:count], 0.0)
    return jnp.concatenate(tiles, axis=1)


def edge_columns(rows, out=None):
    for at, x in rows.items():
        height, width = x.shape
        lane = lane_of((height, LANES))
        out = jnp.zeros((height, LANES), F32) if out is None else out
        out = jnp.where(lane == at, x[:, :1], out)
        out = jnp.where(lane == RIGHT + at, x[:, width - 1 :], out)
    return out


def edges_from(left_ref, right_ref, rows, at):
    here, last = lax.axis_index("obs"), lax.axis_size("obs") - 1
    left = left_ref[rows, RIGHT + at : RIGHT + at + 1]
    right = right_ref[rows, at : at + 1]
    return jnp.where(here > 0, left, 0.0), jnp.where(here < last, right, 0.0)


def sources(tangents, grid_rows, observed, slab_columns):
    count, width = tangents[0].shape
    owned = width // LANES
    first = lax.axis_index("obs") * owned
    blocks = jnp.concatenate(
        [t[:, c * LANES : (c + 1) * LANES] for t in tangents for c in range(owned)], axis=0
    )
    doubled = jnp.concatenate([blocks, blocks], axis=1)
    total = None
    for at in range(0, len(observed), 2):
        pair = observed[at : at + 2]
        if len(pair) == 1:
            pair = pair + [tuple(jnp.zeros_like(x) for x in pair[0])]
        high = jnp.concatenate([x[0] for x in pair], axis=0)
        share = pair[0][0].shape[0]
        lane = lane_of((1, LANES))
        ids = jnp.where(lane < share, pair[0][2], pltpu.roll(pair[1][2], share, 1))
        ids = ids.astype(jnp.int32)
        precision = jnp.where(lane < share, pair[0][3], pltpu.roll(pair[1][3], share, 1))
        low = jnp.concatenate([x[1] for x in pair], axis=0)
        misfit = dot(doubled, jnp.concatenate([high, low], axis=1), 1)
        kept = []
        for i, row in enumerate(grid_rows):
            for c in range(owned):
                k = i * owned + c
                scale = jnp.where(ids == row * slab_columns + first + c, precision, 0.0)
                kept.append(misfit[k * count : (k + 1) * count] * scale)
        misfit_high, misfit_low = split(jnp.concatenate(kept, axis=0))
        halves = jnp.concatenate([misfit_high, misfit_low], axis=1)
        both = dot(
            halves,
            jnp.concatenate(
                [
                    jnp.concatenate([high, low], axis=1),
                    jnp.concatenate([high, jnp.zeros_like(low)], axis=1),
                ],
                axis=0,
            ),
        )
        part = both[:, :LANES] + both[:, LANES:]
        total = part if total is None else total + part
    return [
        jnp.concatenate(
            [total[(i * owned + c) * count : (i * owned + c + 1) * count] for c in range(owned)],
            axis=1,
        )
        for i in range(len(tangents))
    ]


def share_rows(ids, precision):
    out = jnp.zeros((PAD, LANES), F32)
    row = row_of(out.shape)

    def wide(x):
        return jnp.concatenate([x, jnp.zeros((1, LANES - x.shape[1]), F32)], axis=1)

    return jnp.where(row == 0, wide(ids), jnp.where(row == 1, wide(precision), out))


def read_share(ref, at, share):
    high, low = split(ref[at : at + share, :])
    return high, low, ref[at + share : at + share + 1, :], ref[at + share + 1 : at + share + 2, :]


def probe_row(turned, r, rows):
    parts, cells, _ = turned.shape
    return jnp.concatenate(
        [turned[c, pl.ds(r, cells // rows, stride=rows), :] for c in range(parts)], axis=1
    )


def edges_kernel(
    probes, velocity, viscosity, friction, weight, ids, precision,
    turned, first, second, grid, owned, staged, staged_ids, staged_precision, small, sems,
):
    count, rows, width = probes.shape
    share = weight.shape[1]
    copies = [
        pltpu.make_async_copy(source, target, sems.at[i])
        for i, (source, target) in enumerate(
            (
                (probes, staged),
                (velocity, grid.at[0]),
                (viscosity, grid.at[1]),
                (friction, grid.at[2]),
                (weight.at[0], owned.at[:share]),
                (ids, staged_ids),
                (precision, staged_precision),
            )
        )
    ]
    for copy in copies:
        copy.start()
    for copy in copies[1:]:
        copy.wait()
    owned[share:, :] = share_rows(staged_ids[...].astype(F32), staged_precision[...])
    half = share // 2
    weights = owned[:share, :].astype(BF16)
    weights = jnp.concatenate([weights[:half], weights[half:]], axis=1)
    even = lax.axis_index("mesh") % 2 == 0
    sides = []
    for out, below in ((first, even), (second, jnp.logical_not(even))):
        near = jnp.where(below, rows - 1, 0)
        beyond = jnp.where(below, rows - 2, 1)
        sides.append((out, near, beyond))
        out[2 * count : 2 * count + half, :] = weights
        small[...] = jnp.zeros_like(small)
        at = 0
        for field, r in ((0, near), (0, beyond), (1, near), (1, beyond), (2, near)):
            value = grid[field, pl.ds(r, 1), :]
            high = value.astype(BF16).astype(F32)
            small[at : at + 1, :] = high
            small[at + 1 : at + 2, :] = value - high
            at += 2
        small[at : at + 1, :LANES] = owned[share : share + 1, :]
        value = owned[share + 1 : share + 2, :]
        high = value.astype(BF16).astype(F32)
        small[at + 1 : at + 2, :LANES] = high
        small[at + 2 : at + 3, :LANES] = value - high
        out[2 * count + half :, :] = small[...].astype(BF16)
    copies[0].wait()
    for c in range(width // LANES):
        lanes = slice(c * LANES, (c + 1) * LANES)
        turned[c] = staged[:, :, lanes].astype(F32).reshape(count * rows, LANES)
    for out, *picked in sides:
        for i, r in enumerate(picked):
            out[i * count : (i + 1) * count, :] = probe_row(turned, r, rows).astype(BF16)


def forced_kernel(omega, grid, owned, forced, sent):
    _, rows, width = grid.shape
    count = omega.shape[1] // rows
    blocks = []
    first = row_of((PAD, width)) == 0
    for r in range(rows):
        block = jnp.concatenate(
            [
                grid[0, r : r + 1, :] * probe_row(omega, r, rows),
                jnp.where(first, grid[1, r : r + 1, :], 0.0),
            ],
            axis=0,
        )
        forced[r] = block
        blocks.append(block)
    sent[: count + PAD, :] = edge_columns(dict(enumerate(blocks)))
    sent[count + PAD :, :] = owned[...]


def shares_of(refs, at, share):
    return [read_share(ref, at, share) for ref in refs]


def inner_kernel(slab_columns, share, forced, grid, from_left, from_right, *rest):
    *observed, out, edge_sources = rest
    rows, height, width = forced.shape
    count = height - PAD
    tangents = []
    inner = range(1, rows - 1)
    for r in inner:
        edges = edges_from(from_left, from_right, slice(0, height), r)
        tangents.append(
            tangent_row(count, forced[r], forced[r - 1], forced[r + 1], *edges, grid[2, r : r + 1, :])
        )
    result = sources(tangents, inner, shares_of(observed, height, share), slab_columns)
    for i, x in enumerate(result):
        out[i * count : (i + 1) * count, :] = x
    edge_sources[...] = edge_columns(dict(zip(inner, result)))


def arrival(first, second, below):
    even = lax.axis_index("mesh") % 2 == 0
    return jnp.where(even if below else jnp.logical_not(even), first[...], second[...])


def received(x, count, share):
    small = x[2 * count + share // 2 :].astype(F32)
    parts = [small[i : i + 1] + small[i + 1 : i + 2] for i in range(0, 10, 2)]
    return parts, small[10:11, :LANES], small[11:12, :LANES] + small[12:13, :LANES]


def far_kernel(count, share, first, second, early, near, sent):
    blocks = []
    here, last = lax.axis_index("mesh"), lax.axis_size("mesh") - 1
    width = first.shape[1]
    top = row_of((PAD, width)) == 0
    at = count + PAD
    for i, inside in enumerate((here > 0, here < last)):
        x = arrival(first, second, i == 1)
        (velocity, _, viscosity, _, _), ids, precision = received(x, count, share)
        block = jnp.concatenate(
            [velocity * x[:count].astype(F32), jnp.where(top, viscosity, 0.0)], axis=0
        )
        block = jnp.where(inside, block, 0.0)
        near[i] = block
        blocks.append(block)
        weight = x[2 * count : 2 * count + share // 2].astype(F32)
        sent[at : at + share // 2, :] = weight[:, :LANES]
        sent[at + share // 2 : at + share, :] = weight[:, LANES:]
        row = row_of((PAD, LANES))
        sent[at + share : at + share + PAD, :] = jnp.where(
            row == 0, ids, jnp.where(row == 1, precision, 0.0)
        )
        at += share + PAD
    sent[: count + PAD, :] = edge_columns(dict(enumerate(blocks)))


def outer_kernel(
    slab_columns, share, forced, near, grid, from_left, from_right, inner_edges, first_in, second_in, *rest
):
    *observed, out, sent, beside = rest
    rows, height, width = forced.shape
    count = height - PAD
    tangents = []
    outer = (0, rows - 1)
    for r in outer:
        edges = edges_from(from_left, from_right, slice(0, height), r)
        above = near[0] if r == 0 else forced[r - 1]
        below = near[1] if r == rows - 1 else forced[r + 1]
        tangents.append(tangent_row(count, forced[r], above, below, *edges, grid[2, r : r + 1, :]))
    first, last = sources(tangents, outer, shares_of(observed, height, share), slab_columns)
    out[:count, :] = first
    out[count:, :] = last
    sent[...] = edge_columns({0: first, rows - 1: last}, inner_edges[...])
    for i in range(2):
        x = arrival(first_in, second_in, i == 1)
        (_, velocity, _, viscosity, friction), _, _ = received(x, count, share)
        far = jnp.concatenate(
            [
                velocity * x[count : 2 * count].astype(F32),
                jnp.broadcast_to(viscosity, (PAD, width)),
            ],
            axis=0,
        )
        own = forced[rows - 1 if i else 0]
        above, below = (own, far) if i else (far, own)
        beside[i * count : (i + 1) * count, :] = forced_row(count, near[i], above, below, 0.0, 0.0, friction)


def halo_kernel(slab_columns, share, rows, near, beside, from_left, from_right, *rest):
    *observed, out = rest
    _, height, width = near.shape
    count = height - PAD
    here, last = lax.axis_index("mesh"), lax.axis_size("mesh") - 1
    for i in range(2):
        edges = edges_from(from_left, from_right, slice(0, height), i)
        tangent = with_edges(count, beside[i * count : (i + 1) * count, :], near[i], *edges)
        at = height + i * (share + PAD)
        (source,) = sources(
            [tangent.astype(BF16)], (0 if i else rows - 1,), shares_of(observed, at, share), slab_columns
        )
        inside = here < last if i else here > 0
        out[i * count : (i + 1) * count, :] = jnp.where(inside, source, 0.0)


def packed(gram):
    half = gram.shape[0] // 2
    top, bottom = gram[:half], gram[half:]
    row, lane = row_of(top.shape), lane_of(top.shape) % (2 * half)
    mixed = jnp.where((lane >= half) & (row >= lane - half), pltpu.roll(top, half, 1), bottom)
    quarter = half // 2
    body = jnp.where(lane_of((quarter, LANES)) < 2 * half, mixed[:quarter], mixed[quarter:])
    diagonal = jnp.sum(jnp.where(row == lane - half, bottom, 0.0), axis=0, keepdims=True)
    return body, diagonal


def unpacked(body, diagonal):
    quarter = body.shape[0]
    half, size = 2 * quarter, 4 * quarter
    lane = lane_of(body.shape)
    turned = pltpu.roll(body, size, 1)
    mixed = jnp.concatenate(
        [jnp.where(lane < size, body, turned), jnp.where(lane < size, turned, body)], axis=0
    )
    row, lane = row_of(mixed.shape), lane_of(mixed.shape)
    top = pltpu.roll(mixed, LANES - half, 1)
    lower = jnp.concatenate(
        [
            jnp.where(row > lane, top, 0.0),
            jnp.where((lane < half) | ((lane < size) & (row < lane - half)), mixed, 0.0),
        ],
        axis=0,
    )
    spread = jnp.concatenate(
        [
            jnp.where(row == lane, top, 0.0),
            jnp.where(row == lane - half, diagonal, 0.0),
        ],
        axis=0,
    )
    square = jnp.concatenate([lower, jnp.zeros((LANES - size, LANES), F32)], axis=0)
    return lower + square.T[:size] + spread


def sketch_row(r, omega, grid, sources, viscs, edges, visc_edges):
    source, above, below = sources
    left, right = shifted(source, *edges)
    gradient = grid[0, r : r + 1, :] * operate_row(
        source, above, below, left, right,
        [*viscs, *shifted(viscs[0], *visc_edges)],
        grid[2, r : r + 1, :],
    )
    return gradient + probe_row(omega, r, grid.shape[1])


def middle_kernel(forced, omega, grid, visc_left, visc_right, inner, out):
    rows, height, width = forced.shape
    count = height - PAD
    none = jnp.zeros((count, width), F32)
    for r in range(1, rows - 1):
        sources = [
            inner[(i - 1) * count : i * count, :] if 0 < i < rows - 1 else none for i in (r, r - 1, r + 1)
        ]
        out[(r - 1) * count : r * count, :] = sketch_row(
            r, omega, grid, sources,
            [forced[i, count : count + 1, :] for i in (r, r - 1, r + 1)],
            (0.0, 0.0),
            edges_from(visc_left, visc_right, slice(count, count + 1), r),
        )


def sketch_kernel(
    cells, forced, near, omega, grid, visc_left, visc_right, from_left, from_right,
    inner, outer, halo, middle, parts, gram,
):
    rows, height, width = forced.shape
    count = height - PAD
    lane = lane_of((count, LANES))
    total = jnp.zeros((2 * count, 2 * count), F32)
    for r in range(rows):
        edges = edges_from(from_left, from_right, slice(0, count), r)
        visc_edges = edges_from(visc_left, visc_right, slice(count, count + 1), r)
        own = forced[r, count : count + 1, :]
        if 0 < r < rows - 1:
            value = middle[(r - 1) * count : r * count, :]
            for beyond, source in ((0, outer[:count, :]), (rows - 1, outer[count:, :])):
                if abs(r - beyond) == 1:
                    face = 0.5 * (own + forced[beyond, count : count + 1, :])
                    value = value - (grid[0, r : r + 1, :] * face) * source
            tiles = [value[:, at : at + LANES] for at in range(0, width, LANES)]
            for at, edge, visc, place in ((0, edges[0], visc_edges[0], 0), (-1, edges[1], visc_edges[1], LANES - 1)):
                lanes = slice(0, LANES) if at == 0 else slice(width - LANES, width)
                face = grid[0, r : r + 1, lanes] * (0.5 * (own[:, lanes] + visc))
                tiles[at] = tiles[at] - jnp.where(lane == place, face * edge, 0.0)
            value = jnp.concatenate(tiles, axis=1)
        else:
            i = min(r, 1)
            mine, beside = (outer[i * count : (i + 1) * count, :], halo[i * count : (i + 1) * count, :])
            next_row = 1 if r == 0 else r - 1
            inside = inner[(next_row - 1) * count : next_row * count, :]
            sources = (mine, inside, beside) if i else (mine, beside, inside)
            viscs = forced[next_row, count : count + 1, :], near[i, count : count + 1, :]
            value = sketch_row(
                r, omega, grid, sources, (own, *(viscs if i else viscs[::-1])), edges, visc_edges
            )
        value = jnp.concatenate(split(value), axis=0)
        parts[r] = value
        total = total + dot(value, value, 1)
    total = total + pltpu.roll(total, count, 1)
    total = (total[:count] + total[count:]) / cells
    body, diagonal = packed(total)
    for i in range(body.shape[0]):
        gram[:, i * LANES : (i + 1) * LANES] = body[i : i + 1, :]
    gram[:, body.shape[0] * LANES :] = diagonal


def factorize(matrix):
    size = matrix.shape[0]
    row = row_of((8, LANES))
    tiles = [matrix[t : t + 8] for t in range(0, size, 8)]
    last = size // 8 - 1

    def whole(x):
        return jnp.broadcast_to(x, (8, LANES))

    def columns_of(q, t):
        return [whole(tiles[q][:, j : j + 1]) for j in range(8 * t, 8 * t + 8)]

    def upper(block):
        return [[whole(block[c][d : d + 1]) if d >= c else None for d in range(8)] for c in range(8)]

    square = upper(columns_of(0, 0))
    columns = {q: columns_of(q, 0) for q in range(1, last + 1)}
    for t in range(last + 1):
        later = range(t + 1, last + 1)
        rows = [whole(tiles[t][c : c + 1]) for c in range(8)]
        block = columns_of(t + 1, t + 1) if t < last else None
        for c in range(8):
            root = lax.rsqrt(square[c][c])
            rows[c] = rows[c] * root
            left = [square[c][d] * root if d > c else None for d in range(8)]
            for d in range(c + 1, 8):
                for e in range(d, 8):
                    square[d][e] = square[d][e] - left[d] * left[e]
                rows[d] = rows[d] - left[d] * rows[c]
            for q in later:
                columns[q][c] = columns[q][c] * root
                for d in range(c + 1, 8):
                    columns[q][d] = columns[q][d] - left[d] * columns[q][c]
        tiles[t] = rows[0]
        for c in range(1, 8):
            tiles[t] = jnp.where(row == c, rows[c], tiles[t])
        if t < last:
            for column in columns[t + 1]:
                block = [block[e] - column * whole(column[e : e + 1]) for e in range(8)]
            square = upper(block)
            for q in later:
                for c in range(8):
                    tiles[q] = tiles[q] - columns[q][c] * rows[c]
            columns = {q: columns_of(q, t + 1) for q in range(t + 2, last + 1)}
    return jnp.concatenate(tiles, axis=0)


def basis_kernel(rank, gram, parts, basis, factor, turned, lower, sems):
    count = factor.shape[0]
    lines = gram.shape[1] // LANES - 1
    row = row_of((lines, LANES))
    body = jnp.zeros((lines, LANES), F32)
    for i in range(lines):
        body = jnp.where(row == i, gram[:, i * LANES : (i + 1) * LANES], body)
    matrix = unpacked(body, gram[:, lines * LANES :])
    row, lane = row_of(matrix.shape), lane_of(matrix.shape)
    matrix = jnp.where(lane == row + count, 1.0, matrix)
    done = factorize(matrix)
    inverse = pltpu.roll(done, count, 1)
    inverse = jnp.where((lane <= row) & (row < rank[0]), inverse, 0.0)
    high = inverse.astype(BF16).astype(F32)
    high, low = (x + pltpu.roll(x, count, 1) for x in (high, inverse - high))
    left = jnp.concatenate([high, low], axis=0).astype(BF16)
    rows = parts.shape[0]
    copies = [pltpu.make_async_copy(lower, factor, sems.at[turned.shape[0]])]
    for c in range(turned.shape[0]):
        lanes = slice(c * LANES, (c + 1) * LANES)
        for r in range(rows):
            part = parts[r, :, lanes]
            value = dot(left, part)
            turned[c, pl.ds(r, count, stride=rows), :] = value[:count] + value[count:]
        copy = pltpu.make_async_copy(turned.at[c], basis.at[:, lanes], sems.at[c])
        copy.start()
        copies.append(copy)
        if c == 0:
            upper = jnp.where((lane < count) & (lane >= row), done, 0.0)
            square = jnp.concatenate([upper, jnp.zeros((LANES - count, LANES), F32)], axis=0)
            lower[...] = square.T[:count, :count]
            copies[0].start()
    for copy in copies:
        copy.wait()


def ring(x, axis, step):
    size = lax.axis_size(axis)
    return lax.ppermute(x, axis, [(i, (i + step) % size) for i in range(size)])


def exchanged(x, odd):
    rows, columns = lax.axis_size("mesh"), lax.axis_size("obs")
    pairs = []
    for i in range(rows):
        partner = i + 1 if i % 2 == odd else i - 1
        for c in range(columns):
            target = partner * columns + c if 0 <= partner < rows else i * columns + (c ^ 1)
            pairs.append((i * columns + c, target))
    return lax.ppermute(x, ("mesh", "obs"), pairs)


def summed(x):
    rows, columns = lax.axis_size("mesh"), lax.axis_size("obs")
    x = x + ring(x, "obs", 1) if columns == 2 else lax.psum(x, "obs")
    if rows & (rows - 1):
        return lax.psum(x, "mesh")
    rounds = [(1 << bit,) for bit in range(rows.bit_length() - 2, 2, -1)]
    rounds += [(1, 3, 2) if rows > 2 else (1,)] if rows > 1 else []
    rounds += [(4,)] if rows > 4 else []
    for offsets in rounds:
        pieces = [
            lax.ppermute(
                x,
                ("mesh", "obs"),
                [
                    (i * columns + c, (i ^ offset) * columns + (c ^ 1))
                    for i in range(rows)
                    for c in range(columns)
                ],
            )
            for offset in offsets
        ]
        for piece in pieces:
            x = x + piece
    return x


def both_sides(x):
    other = ring(x, "obs", 1)
    return other, (other if lax.axis_size("obs") == 2 else ring(x, "obs", -1))


def all_shares(x, sides):
    size = lax.axis_size("obs")
    if size == 2:
        return [x, sides[0]]
    gathered = lax.all_gather(x, "obs")
    here = lax.axis_index("obs")
    return [lax.dynamic_index_in_dim(gathered, (here + i) % size, 0, False) for i in range(size)]


def per_device(probes, velocity, viscosity, friction, obs_block, obs_weight, obs_prec, rank):
    count, rows, width = probes.shape
    share = obs_weight.shape[1]
    mesh_size, obs_size = lax.axis_size("mesh"), lax.axis_size("obs")
    slab_columns = width * obs_size // LANES
    cells = rows * width * mesh_size * obs_size
    height = count + PAD

    payload = (2 * count + share // 2 + 16, width)
    turned = (width // LANES, rows * count, LANES)
    omega, first, second, grid, owned = call(
        edges_kernel,
        [
            (turned, F32),
            (payload, BF16),
            (payload, BF16),
            ((3, rows, width), F32),
            ((share + PAD, LANES), F32),
        ],
        (probes, velocity, viscosity, friction, obs_weight, obs_block, obs_prec),
        [
            pltpu.VMEM(probes.shape, probes.dtype),
            pltpu.VMEM(obs_block.shape, obs_block.dtype),
            pltpu.VMEM(obs_prec.shape, F32),
            pltpu.VMEM((16, width), F32),
            pltpu.SemaphoreType.DMA((7,)),
        ],
        space=pltpu.HBM,
        name="edges",
    )
    arrived = exchanged(first, 0), exchanged(second, 1)

    forced, sent = call(
        forced_kernel,
        [((rows, height, width), F32), ((height + share + PAD, LANES), F32)],
        (omega, grid, owned),
        name="forced",
    )
    sides = both_sides(sent)
    observed = all_shares(sent, sides)
    inner, inner_edges = call(
        functools.partial(inner_kernel, slab_columns, share),
        [(((rows - 2) * count, width), F32), ((count, LANES), F32)],
        (forced, grid, *sides, *observed),
        name="inner",
    )
    (middle,) = call(
        middle_kernel,
        [(((rows - 2) * count, width), F32)],
        (forced, omega, grid, *sides, inner),
        name="middle",
    )
    near, far_sent = call(
        functools.partial(far_kernel, count, share),
        [((2, height, width), F32), ((height + 2 * (share + PAD), LANES), F32)],
        (*arrived, middle),
        name="far",
    )
    far_sides = both_sides(far_sent)
    far_observed = all_shares(far_sent, far_sides)
    outer, source_sent, beside = call(
        functools.partial(outer_kernel, slab_columns, share),
        [((2 * count, width), F32), ((count, LANES), F32), ((2 * count, width), F32)],
        (forced, near, grid, *sides, inner_edges, *arrived, *observed),
        name="outer",
    )
    source_sides = both_sides(source_sent)
    (halo,) = call(
        functools.partial(halo_kernel, slab_columns, share, rows),
        [((2 * count, width), F32)],
        (near, beside, *far_sides, *far_observed),
        name="halo",
    )
    parts, gram = call(
        functools.partial(sketch_kernel, cells),
        [((rows, 2 * count, width), BF16), ((1, 17 * LANES), F32)],
        (forced, near, omega, grid, *sides, *source_sides, inner, outer, halo, middle),
        name="sketch",
    )
    gram = summed(gram)
    basis, factor = pl.pallas_call(
        basis_kernel,
        out_shape=[
            jax.ShapeDtypeStruct((count * rows, width), F32),
            jax.ShapeDtypeStruct((count, count), F32),
        ],
        in_specs=[pl.BlockSpec(memory_space=pltpu.SMEM)] + [pl.BlockSpec(memory_space=pltpu.VMEM)] * 2,
        out_specs=[pl.BlockSpec(memory_space=pl.ANY)] * 2,
        scratch_shapes=[
            pltpu.VMEM(turned, F32),
            pltpu.VMEM((count, count), F32),
            pltpu.SemaphoreType.DMA((width // LANES + 1,)),
        ],
        compiler_params=pltpu.CompilerParams(vmem_limit_bytes=8 * 2**20),
        name="basis",
    )(rank, gram, parts)
    return basis.reshape(count, rows, width), factor


def solution(mesh):
    in_specs = (
        P(None, "mesh", "obs"),
        P("mesh", "obs"),
        P("mesh", "obs"),
        P("mesh", "obs"),
        P("mesh", "obs"),
        P("mesh", "obs", None),
        P("mesh", "obs"),
        P(),
    )
    out_specs = (P(None, "mesh", "obs"), P())
    return jax.shard_map(
        per_device, mesh=mesh, in_specs=in_specs, out_specs=out_specs, check_vma=False
    )
```

```python
import functools

import jax
import jax.numpy as jnp
from jax import lax
from jax.experimental import pallas as pl
from jax.experimental.pallas import tpu as pltpu
from jax.sharding import PartitionSpec as P

LANES = 128
RIGHT = 16
PAD = 8
F32 = jnp.float32
BF16 = jnp.bfloat16


def split(x):
    high = x.astype(BF16)
    return high, (x - high.astype(F32)).astype(BF16)


def lane_of(shape):
    return lax.broadcasted_iota(jnp.int32, shape, 1)


def row_of(shape):
    return lax.broadcasted_iota(jnp.int32, shape, 0)


def dot(a, b, rhs_dim=0):
    return lax.dot_general(
        a, b, (((1,), (rhs_dim,)), ((), ())), preferred_element_type=F32
    )


def call(body, outs, args, scratch=(), flops=0, space=pltpu.VMEM, name=None):
    if space != pltpu.VMEM:
        args = [pltpu.with_memory_space_constraint(x, space) for x in args]
    outs = [jax.ShapeDtypeStruct(shape, kind) for shape, kind in outs]
    return pl.pallas_call(
        body,
        out_shape=outs,
        in_specs=[pl.BlockSpec(memory_space=space)] * len(args),
        scratch_shapes=list(scratch),
        compiler_params=pltpu.CompilerParams(vmem_limit_bytes=8 * 2**20),
        cost_estimate=pl.CostEstimate(
            flops=flops, bytes_accessed=2**20, transcendentals=0
        ),
        name=name,
    )(*args)


def shifted(x, left_edge, right_edge):
    width = x.shape[1]
    lane = lane_of((x.shape[0], LANES))
    left, right = pltpu.roll(x, 1, 1), pltpu.roll(x, width - 1, 1)
    first = jnp.where(lane == 0, left_edge, left[:, :LANES])
    last = jnp.where(lane == LANES - 1, right_edge, right[:, width - LANES :])
    return (
        jnp.concatenate([first, left[:, LANES:]], axis=1),
        jnp.concatenate([right[:, : width - LANES], last], axis=1),
    )


def operate_row(centre, above, below, left, right, visc, friction):
    own, *others = visc
    faces = [0.5 * (own + other) for other in others]
    result = (friction + faces[0] + faces[1] + faces[2] + faces[3]) * centre
    for face, value in zip(faces, (above, below, left, right)):
        result = result - face * value
    return result


def forced_row(count, centre, above, below, left_edge, right_edge, friction):
    left, right = shifted(centre, left_edge, right_edge)
    visc = [x[count : count + 1] for x in (centre, above, below, left, right)]
    values = [x[:count] for x in (centre, above, below, left, right)]
    return operate_row(*values, visc, friction)


def tangent_row(*args):
    return forced_row(*args).astype(BF16)


def with_edges(count, result, centre, left_edge, right_edge):
    width = centre.shape[1]
    lane = lane_of((count, LANES))
    tiles = [result[:, at : at + LANES] for at in range(0, width, LANES)]
    for at, edge, place in ((0, left_edge, 0), (-1, right_edge, LANES - 1)):
        x = centre[:, :LANES] if at == 0 else centre[:, width - LANES :]
        visc = edge[count : count + 1]
        face = 0.5 * (x[count : count + 1] + visc)
        tiles[at] = tiles[at] + jnp.where(lane == place, (0.5 * visc) * x[:count] - face * edge[:count], 0.0)
    return jnp.concatenate(tiles, axis=1)


def edge_columns(rows, out=None):
    for at, x in rows.items():
        height, width = x.shape
        lane = lane_of((height, LANES))
        out = jnp.zeros((height, LANES), F32) if out is None else out
        out = jnp.where(lane == at, x[:, :1], out)
        out = jnp.where(lane == RIGHT + at, x[:, width - 1 :], out)
    return out


def edges_from(left_ref, right_ref, rows, at):
    here, last = lax.axis_index("obs"), lax.axis_size("obs") - 1
    left = left_ref[rows, RIGHT + at : RIGHT + at + 1]
    right = right_ref[rows, at : at + 1]
    return jnp.where(here > 0, left, 0.0), jnp.where(here < last, right, 0.0)


def sources(tangents, grid_rows, observed, slab_columns):
    count, width = tangents[0].shape
    owned = width // LANES
    first = lax.axis_index("obs") * owned
    blocks = jnp.concatenate(
        [t[:, c * LANES : (c + 1) * LANES] for t in tangents for c in range(owned)], axis=0
    )
    doubled = jnp.concatenate([blocks, blocks], axis=1)
    total = None
    for at in range(0, len(observed), 2):
        pair = observed[at : at + 2]
        if len(pair) == 1:
            pair = pair + [tuple(jnp.zeros_like(x) for x in pair[0])]
        high = jnp.concatenate([x[0] for x in pair], axis=0)
        share = pair[0][0].shape[0]
        lane = lane_of((1, LANES))
        ids = jnp.where(lane < share, pair[0][2], pltpu.roll(pair[1][2], share, 1))
        ids = ids.astype(jnp.int32)
        precision = jnp.where(lane < share, pair[0][3], pltpu.roll(pair[1][3], share, 1))
        low = jnp.concatenate([x[1] for x in pair], axis=0)
        misfit = dot(doubled, jnp.concatenate([high, low], axis=1), 1)
        kept = []
        for i, row in enumerate(grid_rows):
            for c in range(owned):
                k = i * owned + c
                scale = jnp.where(ids == row * slab_columns + first + c, precision, 0.0)
                kept.append(misfit[k * count : (k + 1) * count] * scale)
        misfit_high, misfit_low = split(jnp.concatenate(kept, axis=0))
        halves = jnp.concatenate([misfit_high, misfit_low], axis=1)
        both = dot(
            halves,
            jnp.concatenate(
                [
                    jnp.concatenate([high, low], axis=1),
                    jnp.concatenate([high, jnp.zeros_like(low)], axis=1),
                ],
                axis=0,
            ),
        )
        part = both[:, :LANES] + both[:, LANES:]
        total = part if total is None else total + part
    return [
        jnp.concatenate(
            [total[(i * owned + c) * count : (i * owned + c + 1) * count] for c in range(owned)],
            axis=1,
        )
        for i in range(len(tangents))
    ]


def share_rows(ids, precision):
    out = jnp.zeros((PAD, LANES), F32)
    row = row_of(out.shape)

    def wide(x):
        return jnp.concatenate([x, jnp.zeros((1, LANES - x.shape[1]), F32)], axis=1)

    return jnp.where(row == 0, wide(ids), jnp.where(row == 1, wide(precision), out))


def read_share(ref, at, share):
    high, low = split(ref[at : at + share, :])
    return high, low, ref[at + share : at + share + 1, :], ref[at + share + 1 : at + share + 2, :]


def probe_row(turned, r, rows):
    parts, cells, _ = turned.shape
    return jnp.concatenate(
        [turned[c, pl.ds(r, cells // rows, stride=rows), :] for c in range(parts)], axis=1
    )


def edges_kernel(
    probes, velocity, viscosity, friction, weight, ids, precision,
    turned, first, second, grid, owned, staged, staged_ids, staged_precision, small, sems,
):
    count, rows, width = probes.shape
    share = weight.shape[1]
    copies = [
        pltpu.make_async_copy(source, target, sems.at[i])
        for i, (source, target) in enumerate(
            (
                (probes, staged),
                (velocity, grid.at[0]),
                (viscosity, grid.at[1]),
                (friction, grid.at[2]),
                (weight.at[0], owned.at[:share]),
                (ids, staged_ids),
                (precision, staged_precision),
            )
        )
    ]
    for copy in copies:
        copy.start()
    for copy in copies[1:]:
        copy.wait()
    owned[share:, :] = share_rows(staged_ids[...].astype(F32), staged_precision[...])
    half = share // 2
    weights = owned[:share, :].astype(BF16)
    weights = jnp.concatenate([weights[:half], weights[half:]], axis=1)
    even = lax.axis_index("mesh") % 2 == 0
    sides = []
    for out, below in ((first, even), (second, jnp.logical_not(even))):
        near = jnp.where(below, rows - 1, 0)
        beyond = jnp.where(below, rows - 2, 1)
        sides.append((out, near, beyond))
        out[2 * count : 2 * count + half, :] = weights
        small[...] = jnp.zeros_like(small)
        at = 0
        for field, r in ((0, near), (0, beyond), (1, near), (1, beyond), (2, near)):
            value = grid[field, pl.ds(r, 1), :]
            high = value.astype(BF16).astype(F32)
            small[at : at + 1, :] = high
            small[at + 1 : at + 2, :] = value - high
            at += 2
        small[at : at + 1, :LANES] = owned[share : share + 1, :]
        value = owned[share + 1 : share + 2, :]
        high = value.astype(BF16).astype(F32)
        small[at + 1 : at + 2, :LANES] = high
        small[at + 2 : at + 3, :LANES] = value - high
        out[2 * count + half :, :] = small[...].astype(BF16)
    copies[0].wait()
    for c in range(width // LANES):
        lanes = slice(c * LANES, (c + 1) * LANES)
        turned[c] = staged[:, :, lanes].astype(F32).reshape(count * rows, LANES)
    for out, *picked in sides:
        for i, r in enumerate(picked):
            out[i * count : (i + 1) * count, :] = probe_row(turned, r, rows).astype(BF16)


def forced_kernel(omega, grid, owned, forced, sent):
    _, rows, width = grid.shape
    count = omega.shape[1] // rows
    blocks = []
    first = row_of((PAD, width)) == 0
    for r in range(rows):
        block = jnp.concatenate(
            [
                grid[0, r : r + 1, :] * probe_row(omega, r, rows),
                jnp.where(first, grid[1, r : r + 1, :], 0.0),
            ],
            axis=0,
        )
        forced[r] = block
        blocks.append(block)
    sent[: count + PAD, :] = edge_columns(dict(enumerate(blocks)))
    sent[count + PAD :, :] = owned[...]


def shares_of(refs, at, share):
    return [read_share(ref, at, share) for ref in refs]


def inner_kernel(slab_columns, share, forced, grid, from_left, from_right, *rest):
    *observed, out, edge_sources = rest
    rows, height, width = forced.shape
    count = height - PAD
    tangents = []
    inner = range(1, rows - 1)
    for r in inner:
        edges = edges_from(from_left, from_right, slice(0, height), r)
        tangents.append(
            tangent_row(count, forced[r], forced[r - 1], forced[r + 1], *edges, grid[2, r : r + 1, :])
        )
    result = sources(tangents, inner, shares_of(observed, height, share), slab_columns)
    for i, x in enumerate(result):
        out[i * count : (i + 1) * count, :] = x
    edge_sources[...] = edge_columns(dict(zip(inner, result)))


def arrival(first, second, below):
    even = lax.axis_index("mesh") % 2 == 0
    return jnp.where(even if below else jnp.logical_not(even), first[...], second[...])


def received(x, count, share):
    small = x[2 * count + share // 2 :].astype(F32)
    parts = [small[i : i + 1] + small[i + 1 : i + 2] for i in range(0, 10, 2)]
    return parts, small[10:11, :LANES], small[11:12, :LANES] + small[12:13, :LANES]


def far_kernel(count, share, first, second, early, near, sent):
    blocks = []
    here, last = lax.axis_index("mesh"), lax.axis_size("mesh") - 1
    width = first.shape[1]
    top = row_of((PAD, width)) == 0
    at = count + PAD
    for i, inside in enumerate((here > 0, here < last)):
        x = arrival(first, second, i == 1)
        (velocity, _, viscosity, _, _), ids, precision = received(x, count, share)
        block = jnp.concatenate(
            [velocity * x[:count].astype(F32), jnp.where(top, viscosity, 0.0)], axis=0
        )
        block = jnp.where(inside, block, 0.0)
        near[i] = block
        blocks.append(block)
        weight = x[2 * count : 2 * count + share // 2].astype(F32)
        sent[at : at + share // 2, :] = weight[:, :LANES]
        sent[at + share // 2 : at + share, :] = weight[:, LANES:]
        row = row_of((PAD, LANES))
        sent[at + share : at + share + PAD, :] = jnp.where(
            row == 0, ids, jnp.where(row == 1, precision, 0.0)
        )
        at += share + PAD
    sent[: count + PAD, :] = edge_columns(dict(enumerate(blocks)))


def outer_kernel(
    slab_columns, share, forced, near, grid, from_left, from_right, inner_edges, first_in, second_in, *rest
):
    *observed, out, sent, beside = rest
    rows, height, width = forced.shape
    count = height - PAD
    tangents = []
    outer = (0, rows - 1)
    for r in outer:
        edges = edges_from(from_left, from_right, slice(0, height), r)
        above = near[0] if r == 0 else forced[r - 1]
        below = near[1] if r == rows - 1 else forced[r + 1]
        tangents.append(tangent_row(count, forced[r], above, below, *edges, grid[2, r : r + 1, :]))
    first, last = sources(tangents, outer, shares_of(observed, height, share), slab_columns)
    out[:count, :] = first
    out[count:, :] = last
    sent[...] = edge_columns({0: first, rows - 1: last}, inner_edges[...])
    for i in range(2):
        x = arrival(first_in, second_in, i == 1)
        (_, velocity, _, viscosity, friction), _, _ = received(x, count, share)
        far = jnp.concatenate(
            [
                velocity * x[count : 2 * count].astype(F32),
                jnp.broadcast_to(viscosity, (PAD, width)),
            ],
            axis=0,
        )
        own = forced[rows - 1 if i else 0]
        above, below = (own, far) if i else (far, own)
        beside[i * count : (i + 1) * count, :] = forced_row(count, near[i], above, below, 0.0, 0.0, friction)


def halo_kernel(slab_columns, share, rows, near, beside, from_left, from_right, *rest):
    *observed, out = rest
    _, height, width = near.shape
    count = height - PAD
    here, last = lax.axis_index("mesh"), lax.axis_size("mesh") - 1
    for i in range(2):
        edges = edges_from(from_left, from_right, slice(0, height), i)
        tangent = with_edges(count, beside[i * count : (i + 1) * count, :], near[i], *edges)
        at = height + i * (share + PAD)
        (source,) = sources(
            [tangent.astype(BF16)], (0 if i else rows - 1,), shares_of(observed, at, share), slab_columns
        )
        inside = here < last if i else here > 0
        out[i * count : (i + 1) * count, :] = jnp.where(inside, source, 0.0)


def packed(gram):
    half = gram.shape[0] // 2
    top, bottom = gram[:half], gram[half:]
    row, lane = row_of(top.shape), lane_of(top.shape) % (2 * half)
    mixed = jnp.where((lane >= half) & (row >= lane - half), pltpu.roll(top, half, 1), bottom)
    quarter = half // 2
    body = jnp.where(lane_of((quarter, LANES)) < 2 * half, mixed[:quarter], mixed[quarter:])
    diagonal = jnp.sum(jnp.where(row == lane - half, bottom, 0.0), axis=0, keepdims=True)
    return body, diagonal


def unpacked(body, diagonal):
    quarter = body.shape[0]
    half, size = 2 * quarter, 4 * quarter
    lane = lane_of(body.shape)
    turned = pltpu.roll(body, size, 1)
    mixed = jnp.concatenate(
        [jnp.where(lane < size, body, turned), jnp.where(lane < size, turned, body)], axis=0
    )
    row, lane = row_of(mixed.shape), lane_of(mixed.shape)
    top = pltpu.roll(mixed, LANES - half, 1)
    lower = jnp.concatenate(
        [
            jnp.where(row > lane, top, 0.0),
            jnp.where((lane < half) | ((lane < size) & (row < lane - half)), mixed, 0.0),
        ],
        axis=0,
    )
    spread = jnp.concatenate(
        [
            jnp.where(row == lane, top, 0.0),
            jnp.where(row == lane - half, diagonal, 0.0),
        ],
        axis=0,
    )
    square = jnp.concatenate([lower, jnp.zeros((LANES - size, LANES), F32)], axis=0)
    return lower + square.T[:size] + spread


def sketch_row(r, omega, grid, sources, viscs, edges, visc_edges):
    source, above, below = sources
    left, right = shifted(source, *edges)
    gradient = grid[0, r : r + 1, :] * operate_row(
        source, above, below, left, right,
        [*viscs, *shifted(viscs[0], *visc_edges)],
        grid[2, r : r + 1, :],
    )
    return gradient + probe_row(omega, r, grid.shape[1])


def middle_kernel(forced, omega, grid, visc_left, visc_right, inner, out):
    rows, height, width = forced.shape
    count = height - PAD
    none = jnp.zeros((count, width), F32)
    for r in range(1, rows - 1):
        sources = [
            inner[(i - 1) * count : i * count, :] if 0 < i < rows - 1 else none for i in (r, r - 1, r + 1)
        ]
        out[(r - 1) * count : r * count, :] = sketch_row(
            r, omega, grid, sources,
            [forced[i, count : count + 1, :] for i in (r, r - 1, r + 1)],
            (0.0, 0.0),
            edges_from(visc_left, visc_right, slice(count, count + 1), r),
        )


def sketch_kernel(
    cells, forced, near, omega, grid, visc_left, visc_right, from_left, from_right,
    inner, outer, halo, middle, parts, gram,
):
    rows, height, width = forced.shape
    count = height - PAD
    lane = lane_of((count, LANES))
    total = jnp.zeros((2 * count, 2 * count), F32)
    for r in range(rows):
        edges = edges_from(from_left, from_right, slice(0, count), r)
        visc_edges = edges_from(visc_left, visc_right, slice(count, count + 1), r)
        own = forced[r, count : count + 1, :]
        if 0 < r < rows - 1:
            value = middle[(r - 1) * count : r * count, :]
            for beyond, source in ((0, outer[:count, :]), (rows - 1, outer[count:, :])):
                if abs(r - beyond) == 1:
                    face = 0.5 * (own + forced[beyond, count : count + 1, :])
                    value = value - (grid[0, r : r + 1, :] * face) * source
            tiles = [value[:, at : at + LANES] for at in range(0, width, LANES)]
            for at, edge, visc, place in ((0, edges[0], visc_edges[0], 0), (-1, edges[1], visc_edges[1], LANES - 1)):
                lanes = slice(0, LANES) if at == 0 else slice(width - LANES, width)
                face = grid[0, r : r + 1, lanes] * (0.5 * (own[:, lanes] + visc))
                tiles[at] = tiles[at] - jnp.where(lane == place, face * edge, 0.0)
            value = jnp.concatenate(tiles, axis=1)
        else:
            i = min(r, 1)
            mine, beside = (outer[i * count : (i + 1) * count, :], halo[i * count : (i + 1) * count, :])
            next_row = 1 if r == 0 else r - 1
            inside = inner[(next_row - 1) * count : next_row * count, :]
            sources = (mine, inside, beside) if i else (mine, beside, inside)
            viscs = forced[next_row, count : count + 1, :], near[i, count : count + 1, :]
            value = sketch_row(
                r, omega, grid, sources, (own, *(viscs if i else viscs[::-1])), edges, visc_edges
            )
        value = jnp.concatenate(split(value), axis=0)
        parts[r] = value
        total = total + dot(value, value, 1)
    total = total + pltpu.roll(total, count, 1)
    total = (total[:count] + total[count:]) / cells
    body, diagonal = packed(total)
    for i in range(body.shape[0]):
        gram[:, i * LANES : (i + 1) * LANES] = body[i : i + 1, :]
    gram[:, body.shape[0] * LANES :] = diagonal


def factorize(matrix, take):
    size = matrix.shape[0]
    row = row_of((8, LANES))
    tiles = [matrix[t : t + 8] for t in range(0, size, 8)]
    last = size // 8 - 1

    def whole(x):
        return jnp.broadcast_to(x, (8, LANES))

    def columns_of(q, t):
        return [whole(tiles[q][:, j : j + 1]) for j in range(8 * t, 8 * t + 8)]

    def upper(block):
        return [[whole(block[c][d : d + 1]) if d >= c else None for d in range(8)] for c in range(8)]

    square = upper(columns_of(0, 0))
    columns = {q: columns_of(q, 0) for q in range(1, last + 1)}
    for t in range(last + 1):
        later = range(t + 1, last + 1)
        rows = [whole(tiles[t][c : c + 1]) for c in range(8)]
        block = columns_of(t + 1, t + 1) if t < last else None
        for c in range(8):
            root = lax.rsqrt(square[c][c])
            rows[c] = rows[c] * root
            left = [square[c][d] * root if d > c else None for d in range(8)]
            for d in range(c + 1, 8):
                for e in range(d, 8):
                    square[d][e] = square[d][e] - left[d] * left[e]
                rows[d] = rows[d] - left[d] * rows[c]
            for q in later:
                columns[q][c] = columns[q][c] * root
                for d in range(c + 1, 8):
                    columns[q][d] = columns[q][d] - left[d] * columns[q][c]
        tiles[t] = rows[0]
        for c in range(1, 8):
            tiles[t] = jnp.where(row == c, rows[c], tiles[t])
        if t < last:
            for column in columns[t + 1]:
                block = [block[e] - column * whole(column[e : e + 1]) for e in range(8)]
            square = upper(block)
            for q in later:
                for c in range(8):
                    tiles[q] = tiles[q] - columns[q][c] * rows[c]
            columns = {q: columns_of(q, t + 1) for q in range(t + 2, last + 1)}
        if t in (last // 2, last):
            first = 0 if t < last else t // 2 + 1
            take(8 * first, jnp.concatenate(tiles[first : t + 1], axis=0))


def basis_kernel(rank, gram, parts, basis, factor, turned, lower, sems):
    count = factor.shape[0]
    lines = gram.shape[1] // LANES - 1
    row = row_of((lines, LANES))
    body = jnp.zeros((lines, LANES), F32)
    for i in range(lines):
        body = jnp.where(row == i, gram[:, i * LANES : (i + 1) * LANES], body)
    matrix = unpacked(body, gram[:, lines * LANES :])
    row, lane = row_of(matrix.shape), lane_of(matrix.shape)
    matrix = jnp.where(lane == row + count, 1.0, matrix)
    rows = parts.shape[0]
    copies = []
    finals = []

    def take(at, done):
        finals.append(done)
        height = done.shape[0]
        for copy in copies:
            copy.start()
        row, lane = row_of(done.shape) + at, lane_of(done.shape)
        inverse = pltpu.roll(done, count, 1)
        inverse = jnp.where((lane <= row) & (row < rank[0]), inverse, 0.0)
        high = inverse.astype(BF16).astype(F32)
        high, low = (x + pltpu.roll(x, count, 1) for x in (high, inverse - high))
        left = jnp.concatenate([high, low], axis=0).astype(BF16)
        for c in range(turned.shape[0]):
            lanes = slice(c * LANES, (c + 1) * LANES)
            for r in range(rows):
                value = dot(left, parts[r, :, lanes])
                turned[c, pl.ds(at * rows + r, height, stride=rows), :] = value[:height] + value[height:]
            cells = slice(at * rows, (at + height) * rows)
            copies.append(
                pltpu.make_async_copy(turned.at[c, cells], basis.at[cells, lanes], sems.at[len(copies)])
            )
            if at:
                copies[-1].start()

    factorize(matrix, take)
    upper = jnp.where((lane < count) & (lane >= row), jnp.concatenate(finals, axis=0), 0.0)
    square = jnp.concatenate([upper, jnp.zeros((LANES - count, LANES), F32)], axis=0)
    lower[...] = square.T[:count, :count]
    copies.append(pltpu.make_async_copy(lower, factor, sems.at[len(copies)]))
    copies[-1].start()
    for copy in copies:
        copy.wait()


def ring(x, axis, step):
    size = lax.axis_size(axis)
    return lax.ppermute(x, axis, [(i, (i + step) % size) for i in range(size)])


def exchanged(x, odd):
    rows, columns = lax.axis_size("mesh"), lax.axis_size("obs")
    pairs = []
    for i in range(rows):
        partner = i + 1 if i % 2 == odd else i - 1
        for c in range(columns):
            target = partner * columns + c if 0 <= partner < rows else i * columns + (c ^ 1)
            pairs.append((i * columns + c, target))
    return lax.ppermute(x, ("mesh", "obs"), pairs)


def summed(x):
    rows, columns = lax.axis_size("mesh"), lax.axis_size("obs")
    x = x + ring(x, "obs", 1) if columns == 2 else lax.psum(x, "obs")
    if rows & (rows - 1):
        return lax.psum(x, "mesh")
    rounds = [(1 << bit,) for bit in range(rows.bit_length() - 2, 2, -1)]
    rounds += [(1, 3, 2) if rows > 2 else (1,)] if rows > 1 else []
    rounds += [(4,)] if rows > 4 else []
    for offsets in rounds:
        pieces = [
            lax.ppermute(
                x,
                ("mesh", "obs"),
                [
                    (i * columns + c, (i ^ offset) * columns + (c ^ 1))
                    for i in range(rows)
                    for c in range(columns)
                ],
            )
            for offset in offsets
        ]
        for piece in pieces:
            x = x + piece
    return x


def both_sides(x):
    other = ring(x, "obs", 1)
    return other, (other if lax.axis_size("obs") == 2 else ring(x, "obs", -1))


def all_shares(x, sides):
    size = lax.axis_size("obs")
    if size == 2:
        return [x, sides[0]]
    gathered = lax.all_gather(x, "obs")
    here = lax.axis_index("obs")
    return [lax.dynamic_index_in_dim(gathered, (here + i) % size, 0, False) for i in range(size)]


def per_device(probes, velocity, viscosity, friction, obs_block, obs_weight, obs_prec, rank):
    count, rows, width = probes.shape
    share = obs_weight.shape[1]
    mesh_size, obs_size = lax.axis_size("mesh"), lax.axis_size("obs")
    slab_columns = width * obs_size // LANES
    cells = rows * width * mesh_size * obs_size
    height = count + PAD

    payload = (2 * count + share // 2 + 16, width)
    turned = (width // LANES, rows * count, LANES)
    omega, first, second, grid, owned = call(
        edges_kernel,
        [
            (turned, F32),
            (payload, BF16),
            (payload, BF16),
            ((3, rows, width), F32),
            ((share + PAD, LANES), F32),
        ],
        (probes, velocity, viscosity, friction, obs_weight, obs_block, obs_prec),
        [
            pltpu.VMEM(probes.shape, probes.dtype),
            pltpu.VMEM(obs_block.shape, obs_block.dtype),
            pltpu.VMEM(obs_prec.shape, F32),
            pltpu.VMEM((16, width), F32),
            pltpu.SemaphoreType.DMA((7,)),
        ],
        space=pltpu.HBM,
        name="edges",
    )
    arrived = exchanged(first, 0), exchanged(second, 1)

    forced, sent = call(
        forced_kernel,
        [((rows, height, width), F32), ((height + share + PAD, LANES), F32)],
        (omega, grid, owned),
        name="forced",
    )
    sides = both_sides(sent)
    observed = all_shares(sent, sides)
    inner, inner_edges = call(
        functools.partial(inner_kernel, slab_columns, share),
        [(((rows - 2) * count, width), F32), ((count, LANES), F32)],
        (forced, grid, *sides, *observed),
        name="inner",
    )
    (middle,) = call(
        middle_kernel,
        [(((rows - 2) * count, width), F32)],
        (forced, omega, grid, *sides, inner),
        name="middle",
    )
    near, far_sent = call(
        functools.partial(far_kernel, count, share),
        [((2, height, width), F32), ((height + 2 * (share + PAD), LANES), F32)],
        (*arrived, middle),
        name="far",
    )
    far_sides = both_sides(far_sent)
    far_observed = all_shares(far_sent, far_sides)
    outer, source_sent, beside = call(
        functools.partial(outer_kernel, slab_columns, share),
        [((2 * count, width), F32), ((count, LANES), F32), ((2 * count, width), F32)],
        (forced, near, grid, *sides, inner_edges, *arrived, *observed),
        name="outer",
    )
    source_sides = both_sides(source_sent)
    (halo,) = call(
        functools.partial(halo_kernel, slab_columns, share, rows),
        [((2 * count, width), F32)],
        (near, beside, *far_sides, *far_observed),
        name="halo",
    )
    parts, gram = call(
        functools.partial(sketch_kernel, cells),
        [((rows, 2 * count, width), BF16), ((1, 17 * LANES), F32)],
        (forced, near, omega, grid, *sides, *source_sides, inner, outer, halo, middle),
        name="sketch",
    )
    gram = summed(gram)
    basis, factor = pl.pallas_call(
        basis_kernel,
        out_shape=[
            jax.ShapeDtypeStruct((count * rows, width), F32),
            jax.ShapeDtypeStruct((count, count), F32),
        ],
        in_specs=[pl.BlockSpec(memory_space=pltpu.SMEM)] + [pl.BlockSpec(memory_space=pltpu.VMEM)] * 2,
        out_specs=[pl.BlockSpec(memory_space=pl.ANY)] * 2,
        scratch_shapes=[
            pltpu.VMEM(turned, F32),
            pltpu.VMEM((count, count), F32),
            pltpu.SemaphoreType.DMA((2 * width // LANES + 1,)),
        ],
        compiler_params=pltpu.CompilerParams(vmem_limit_bytes=8 * 2**20),
        name="basis",
    )(rank, gram, parts)
    return basis.reshape(count, rows, width), factor


def solution(mesh):
    in_specs = (
        P(None, "mesh", "obs"),
        P("mesh", "obs"),
        P("mesh", "obs"),
        P("mesh", "obs"),
        P("mesh", "obs"),
        P("mesh", "obs", None),
        P("mesh", "obs"),
        P(),
    )
    out_specs = (P(None, "mesh", "obs"), P())
    return jax.shard_map(
        per_device, mesh=mesh, in_specs=in_specs, out_specs=out_specs, check_vma=False
    )
```

```python
import functools

import jax
import jax.numpy as jnp
from jax import lax
from jax.experimental import pallas as pl
from jax.experimental.pallas import tpu as pltpu
from jax.sharding import PartitionSpec as P

LANES = 128
RIGHT = 16
PAD = 8
F32 = jnp.float32
BF16 = jnp.bfloat16


def split(x):
    high = x.astype(BF16)
    return high, (x - high.astype(F32)).astype(BF16)


def lane_of(shape):
    return lax.broadcasted_iota(jnp.int32, shape, 1)


def row_of(shape):
    return lax.broadcasted_iota(jnp.int32, shape, 0)


def dot(a, b, rhs_dim=0):
    return lax.dot_general(
        a, b, (((1,), (rhs_dim,)), ((), ())), preferred_element_type=F32
    )


def call(body, outs, args, scratch=(), flops=0, space=pltpu.VMEM, name=None):
    if space != pltpu.VMEM:
        args = [pltpu.with_memory_space_constraint(x, space) for x in args]
    outs = [jax.ShapeDtypeStruct(shape, kind) for shape, kind in outs]
    return pl.pallas_call(
        body,
        out_shape=outs,
        in_specs=[pl.BlockSpec(memory_space=space)] * len(args),
        scratch_shapes=list(scratch),
        compiler_params=pltpu.CompilerParams(vmem_limit_bytes=8 * 2**20),
        cost_estimate=pl.CostEstimate(
            flops=flops, bytes_accessed=2**20, transcendentals=0
        ),
        name=name,
    )(*args)


def shifted(x, left_edge, right_edge):
    width = x.shape[1]
    lane = lane_of((x.shape[0], LANES))
    left, right = pltpu.roll(x, 1, 1), pltpu.roll(x, width - 1, 1)
    first = jnp.where(lane == 0, left_edge, left[:, :LANES])
    last = jnp.where(lane == LANES - 1, right_edge, right[:, width - LANES :])
    return (
        jnp.concatenate([first, left[:, LANES:]], axis=1),
        jnp.concatenate([right[:, : width - LANES], last], axis=1),
    )


def operate_row(centre, above, below, left, right, visc, friction):
    own, *others = visc
    faces = [0.5 * (own + other) for other in others]
    result = (friction + faces[0] + faces[1] + faces[2] + faces[3]) * centre
    for face, value in zip(faces, (above, below, left, right)):
        result = result - face * value
    return result


def forced_row(count, centre, above, below, left_edge, right_edge, friction):
    left, right = shifted(centre, left_edge, right_edge)
    visc = [x[count : count + 1] for x in (centre, above, below, left, right)]
    values = [x[:count] for x in (centre, above, below, left, right)]
    return operate_row(*values, visc, friction)


def tangent_row(*args):
    return forced_row(*args).astype(BF16)


def with_edges(count, result, centre, left_edge, right_edge):
    width = centre.shape[1]
    lane = lane_of((count, LANES))
    tiles = [result[:, at : at + LANES] for at in range(0, width, LANES)]
    for at, edge, place in ((0, left_edge, 0), (-1, right_edge, LANES - 1)):
        x = centre[:, :LANES] if at == 0 else centre[:, width - LANES :]
        visc = edge[count : count + 1]
        face = 0.5 * (x[count : count + 1] + visc)
        tiles[at] = tiles[at] + jnp.where(lane == place, (0.5 * visc) * x[:count] - face * edge[:count], 0.0)
    return jnp.concatenate(tiles, axis=1)


def edge_columns(rows, out=None):
    for at, x in rows.items():
        height, width = x.shape
        lane = lane_of((height, LANES))
        out = jnp.zeros((height, LANES), F32) if out is None else out
        out = jnp.where(lane == at, x[:, :1], out)
        out = jnp.where(lane == RIGHT + at, x[:, width - 1 :], out)
    return out


def edges_from(left_ref, right_ref, rows, at):
    here, last = lax.axis_index("obs"), lax.axis_size("obs") - 1
    left = left_ref[rows, RIGHT + at : RIGHT + at + 1]
    right = right_ref[rows, at : at + 1]
    return jnp.where(here > 0, left, 0.0), jnp.where(here < last, right, 0.0)


def sources(tangents, grid_rows, observed, slab_columns):
    count, width = tangents[0].shape
    owned = width // LANES
    first = lax.axis_index("obs") * owned
    blocks = jnp.concatenate(
        [t[:, c * LANES : (c + 1) * LANES] for t in tangents for c in range(owned)], axis=0
    )
    doubled = jnp.concatenate([blocks, blocks], axis=1)
    total = None
    for at in range(0, len(observed), 2):
        pair = observed[at : at + 2]
        if len(pair) == 1:
            pair = pair + [tuple(jnp.zeros_like(x) for x in pair[0])]
        high = jnp.concatenate([x[0] for x in pair], axis=0)
        share = pair[0][0].shape[0]
        lane = lane_of((1, LANES))
        ids = jnp.where(lane < share, pair[0][2], pltpu.roll(pair[1][2], share, 1))
        ids = ids.astype(jnp.int32)
        precision = jnp.where(lane < share, pair[0][3], pltpu.roll(pair[1][3], share, 1))
        low = jnp.concatenate([x[1] for x in pair], axis=0)
        misfit = dot(doubled, jnp.concatenate([high, low], axis=1), 1)
        kept = []
        for i, row in enumerate(grid_rows):
            for c in range(owned):
                k = i * owned + c
                scale = jnp.where(ids == row * slab_columns + first + c, precision, 0.0)
                kept.append(misfit[k * count : (k + 1) * count] * scale)
        misfit_high, misfit_low = split(jnp.concatenate(kept, axis=0))
        halves = jnp.concatenate([misfit_high, misfit_low], axis=1)
        both = dot(
            halves,
            jnp.concatenate(
                [
                    jnp.concatenate([high, low], axis=1),
                    jnp.concatenate([high, jnp.zeros_like(low)], axis=1),
                ],
                axis=0,
            ),
        )
        part = both[:, :LANES] + both[:, LANES:]
        total = part if total is None else total + part
    return [
        jnp.concatenate(
            [total[(i * owned + c) * count : (i * owned + c + 1) * count] for c in range(owned)],
            axis=1,
        )
        for i in range(len(tangents))
    ]


def share_rows(ids, precision):
    out = jnp.zeros((PAD, LANES), F32)
    row = row_of(out.shape)

    def wide(x):
        return jnp.concatenate([x, jnp.zeros((1, LANES - x.shape[1]), F32)], axis=1)

    return jnp.where(row == 0, wide(ids), jnp.where(row == 1, wide(precision), out))


def read_share(ref, at, share):
    high, low = split(ref[at : at + share, :])
    return high, low, ref[at + share : at + share + 1, :], ref[at + share + 1 : at + share + 2, :]


def probe_row(turned, r, rows):
    parts, cells, _ = turned.shape
    return jnp.concatenate(
        [turned[c, pl.ds(r, cells // rows, stride=rows), :] for c in range(parts)], axis=1
    )


def edges_kernel(
    probes, velocity, viscosity, friction, weight, ids, precision,
    turned, first, second, grid, owned, staged, staged_ids, staged_precision, small, sems,
):
    count, rows, width = probes.shape
    share = weight.shape[1]
    copies = [
        pltpu.make_async_copy(source, target, sems.at[i])
        for i, (source, target) in enumerate(
            (
                (probes, staged),
                (velocity, grid.at[0]),
                (viscosity, grid.at[1]),
                (friction, grid.at[2]),
                (weight.at[0], owned.at[:share]),
                (ids, staged_ids),
                (precision, staged_precision),
            )
        )
    ]
    for copy in copies:
        copy.start()
    for copy in copies[1:]:
        copy.wait()
    owned[share:, :] = share_rows(staged_ids[...].astype(F32), staged_precision[...])
    half = share // 2
    weights = owned[:share, :].astype(BF16)
    weights = jnp.concatenate([weights[:half], weights[half:]], axis=1)
    even = lax.axis_index("mesh") % 2 == 0
    sides = []
    for out, below in ((first, even), (second, jnp.logical_not(even))):
        near = jnp.where(below, rows - 1, 0)
        beyond = jnp.where(below, rows - 2, 1)
        sides.append((out, near, beyond))
        out[2 * count : 2 * count + half, :] = weights
        small[...] = jnp.zeros_like(small)
        at = 0
        for field, r in ((0, near), (0, beyond), (1, near), (1, beyond), (2, near)):
            value = grid[field, pl.ds(r, 1), :]
            high = value.astype(BF16).astype(F32)
            small[at : at + 1, :] = high
            small[at + 1 : at + 2, :] = value - high
            at += 2
        small[at : at + 1, :LANES] = owned[share : share + 1, :]
        value = owned[share + 1 : share + 2, :]
        high = value.astype(BF16).astype(F32)
        small[at + 1 : at + 2, :LANES] = high
        small[at + 2 : at + 3, :LANES] = value - high
        out[2 * count + half :, :] = small[...].astype(BF16)
    copies[0].wait()
    for c in range(width // LANES):
        lanes = slice(c * LANES, (c + 1) * LANES)
        turned[c] = staged[:, :, lanes].astype(F32).reshape(count * rows, LANES)
    for out, *picked in sides:
        for i, r in enumerate(picked):
            out[i * count : (i + 1) * count, :] = probe_row(turned, r, rows).astype(BF16)


def forced_kernel(omega, grid, owned, forced, sent):
    _, rows, width = grid.shape
    count = omega.shape[1] // rows
    blocks = []
    first = row_of((PAD, width)) == 0
    for r in range(rows):
        block = jnp.concatenate(
            [
                grid[0, r : r + 1, :] * probe_row(omega, r, rows),
                jnp.where(first, grid[1, r : r + 1, :], 0.0),
            ],
            axis=0,
        )
        forced[r] = block
        blocks.append(block)
    sent[: count + PAD, :] = edge_columns(dict(enumerate(blocks)))
    sent[count + PAD :, :] = owned[...]


def shares_of(refs, at, share):
    return [read_share(ref, at, share) for ref in refs]


def inner_kernel(slab_columns, share, forced, grid, from_left, from_right, *rest):
    *observed, out, edge_sources = rest
    rows, height, width = forced.shape
    count = height - PAD
    tangents = []
    inner = range(1, rows - 1)
    for r in inner:
        edges = edges_from(from_left, from_right, slice(0, height), r)
        tangents.append(
            tangent_row(count, forced[r], forced[r - 1], forced[r + 1], *edges, grid[2, r : r + 1, :])
        )
    result = sources(tangents, inner, shares_of(observed, height, share), slab_columns)
    for i, x in enumerate(result):
        out[i * count : (i + 1) * count, :] = x
    edge_sources[...] = edge_columns(dict(zip(inner, result)))


def arrival(first, second, below):
    even = lax.axis_index("mesh") % 2 == 0
    return jnp.where(even if below else jnp.logical_not(even), first[...], second[...])


def received(x, count, share):
    small = x[2 * count + share // 2 :].astype(F32)
    parts = [small[i : i + 1] + small[i + 1 : i + 2] for i in range(0, 10, 2)]
    return parts, small[10:11, :LANES], small[11:12, :LANES] + small[12:13, :LANES]


def far_kernel(count, share, first, second, early, near, sent):
    blocks = []
    here, last = lax.axis_index("mesh"), lax.axis_size("mesh") - 1
    width = first.shape[1]
    top = row_of((PAD, width)) == 0
    at = count + PAD
    for i, inside in enumerate((here > 0, here < last)):
        x = arrival(first, second, i == 1)
        (velocity, _, viscosity, _, _), ids, precision = received(x, count, share)
        block = jnp.concatenate(
            [velocity * x[:count].astype(F32), jnp.where(top, viscosity, 0.0)], axis=0
        )
        block = jnp.where(inside, block, 0.0)
        near[i] = block
        blocks.append(block)
        weight = x[2 * count : 2 * count + share // 2].astype(F32)
        sent[at : at + share // 2, :] = weight[:, :LANES]
        sent[at + share // 2 : at + share, :] = weight[:, LANES:]
        row = row_of((PAD, LANES))
        sent[at + share : at + share + PAD, :] = jnp.where(
            row == 0, ids, jnp.where(row == 1, precision, 0.0)
        )
        at += share + PAD
    sent[: count + PAD, :] = edge_columns(dict(enumerate(blocks)))


def outer_kernel(
    slab_columns, share, forced, near, grid, from_left, from_right, inner_edges, first_in, second_in, *rest
):
    *observed, out, sent, beside = rest
    rows, height, width = forced.shape
    count = height - PAD
    tangents = []
    outer = (0, rows - 1)
    for r in outer:
        edges = edges_from(from_left, from_right, slice(0, height), r)
        above = near[0] if r == 0 else forced[r - 1]
        below = near[1] if r == rows - 1 else forced[r + 1]
        tangents.append(tangent_row(count, forced[r], above, below, *edges, grid[2, r : r + 1, :]))
    first, last = sources(tangents, outer, shares_of(observed, height, share), slab_columns)
    out[:count, :] = first
    out[count:, :] = last
    sent[...] = edge_columns({0: first, rows - 1: last}, inner_edges[...])
    for i in range(2):
        x = arrival(first_in, second_in, i == 1)
        (_, velocity, _, viscosity, friction), _, _ = received(x, count, share)
        far = jnp.concatenate(
            [
                velocity * x[count : 2 * count].astype(F32),
                jnp.broadcast_to(viscosity, (PAD, width)),
            ],
            axis=0,
        )
        own = forced[rows - 1 if i else 0]
        above, below = (own, far) if i else (far, own)
        beside[i * count : (i + 1) * count, :] = forced_row(count, near[i], above, below, 0.0, 0.0, friction)


def halo_kernel(slab_columns, share, rows, near, beside, from_left, from_right, *rest):
    *observed, out = rest
    _, height, width = near.shape
    count = height - PAD
    here, last = lax.axis_index("mesh"), lax.axis_size("mesh") - 1
    for i in range(2):
        edges = edges_from(from_left, from_right, slice(0, height), i)
        tangent = with_edges(count, beside[i * count : (i + 1) * count, :], near[i], *edges)
        at = height + i * (share + PAD)
        (source,) = sources(
            [tangent.astype(BF16)], (0 if i else rows - 1,), shares_of(observed, at, share), slab_columns
        )
        inside = here < last if i else here > 0
        out[i * count : (i + 1) * count, :] = jnp.where(inside, source, 0.0)


def packed(gram):
    half = gram.shape[0] // 2
    top, bottom = gram[:half], gram[half:]
    row, lane = row_of(top.shape), lane_of(top.shape) % (2 * half)
    mixed = jnp.where((lane >= half) & (row >= lane - half), pltpu.roll(top, half, 1), bottom)
    quarter = half // 2
    body = jnp.where(lane_of((quarter, LANES)) < 2 * half, mixed[:quarter], mixed[quarter:])
    diagonal = jnp.sum(jnp.where(row == lane - half, bottom, 0.0), axis=0, keepdims=True)
    return body, diagonal


def unpacked(body, diagonal):
    quarter = body.shape[0]
    half, size = 2 * quarter, 4 * quarter
    lane = lane_of(body.shape)
    turned = pltpu.roll(body, size, 1)
    mixed = jnp.concatenate(
        [jnp.where(lane < size, body, turned), jnp.where(lane < size, turned, body)], axis=0
    )
    row, lane = row_of(mixed.shape), lane_of(mixed.shape)
    top = pltpu.roll(mixed, LANES - half, 1)
    lower = jnp.concatenate(
        [
            jnp.where(row > lane, top, 0.0),
            jnp.where((lane < half) | ((lane < size) & (row < lane - half)), mixed, 0.0),
        ],
        axis=0,
    )
    spread = jnp.concatenate(
        [
            jnp.where(row == lane, top, 0.0),
            jnp.where(row == lane - half, diagonal, 0.0),
        ],
        axis=0,
    )
    square = jnp.concatenate([lower, jnp.zeros((LANES - size, LANES), F32)], axis=0)
    return lower + square.T[:size] + spread


def sketch_row(r, omega, grid, sources, viscs, edges, visc_edges):
    source, above, below = sources
    left, right = shifted(source, *edges)
    gradient = grid[0, r : r + 1, :] * operate_row(
        source, above, below, left, right,
        [*viscs, *shifted(viscs[0], *visc_edges)],
        grid[2, r : r + 1, :],
    )
    return gradient + probe_row(omega, r, grid.shape[1])


def middle_kernel(forced, omega, grid, visc_left, visc_right, inner, out):
    rows, height, width = forced.shape
    count = height - PAD
    none = jnp.zeros((count, width), F32)
    for r in range(1, rows - 1):
        sources = [
            inner[(i - 1) * count : i * count, :] if 0 < i < rows - 1 else none for i in (r, r - 1, r + 1)
        ]
        out[(r - 1) * count : r * count, :] = sketch_row(
            r, omega, grid, sources,
            [forced[i, count : count + 1, :] for i in (r, r - 1, r + 1)],
            (0.0, 0.0),
            edges_from(visc_left, visc_right, slice(count, count + 1), r),
        )


def sketch_kernel(
    cells, forced, near, omega, grid, visc_left, visc_right, from_left, from_right,
    inner, outer, halo, middle, parts, gram,
):
    rows, height, width = forced.shape
    count = height - PAD
    lane = lane_of((count, LANES))
    total = jnp.zeros((2 * count, 2 * count), F32)
    for r in range(rows):
        edges = edges_from(from_left, from_right, slice(0, count), r)
        visc_edges = edges_from(visc_left, visc_right, slice(count, count + 1), r)
        own = forced[r, count : count + 1, :]
        if 0 < r < rows - 1:
            value = middle[(r - 1) * count : r * count, :]
            for beyond, source in ((0, outer[:count, :]), (rows - 1, outer[count:, :])):
                if abs(r - beyond) == 1:
                    face = 0.5 * (own + forced[beyond, count : count + 1, :])
                    value = value - (grid[0, r : r + 1, :] * face) * source
            tiles = [value[:, at : at + LANES] for at in range(0, width, LANES)]
            for at, edge, visc, place in ((0, edges[0], visc_edges[0], 0), (-1, edges[1], visc_edges[1], LANES - 1)):
                lanes = slice(0, LANES) if at == 0 else slice(width - LANES, width)
                face = grid[0, r : r + 1, lanes] * (0.5 * (own[:, lanes] + visc))
                tiles[at] = tiles[at] - jnp.where(lane == place, face * edge, 0.0)
            value = jnp.concatenate(tiles, axis=1)
        else:
            i = min(r, 1)
            mine, beside = (outer[i * count : (i + 1) * count, :], halo[i * count : (i + 1) * count, :])
            next_row = 1 if r == 0 else r - 1
            inside = inner[(next_row - 1) * count : next_row * count, :]
            sources = (mine, inside, beside) if i else (mine, beside, inside)
            viscs = forced[next_row, count : count + 1, :], near[i, count : count + 1, :]
            value = sketch_row(
                r, omega, grid, sources, (own, *(viscs if i else viscs[::-1])), edges, visc_edges
            )
        value = jnp.concatenate(split(value), axis=0)
        parts[r] = value
        total = total + dot(value, value, 1)
    total = total + pltpu.roll(total, count, 1)
    total = (total[:count] + total[count:]) / cells
    body, diagonal = packed(total)
    for i in range(body.shape[0]):
        gram[:, i * LANES : (i + 1) * LANES] = body[i : i + 1, :]
    gram[:, body.shape[0] * LANES :] = diagonal


def factorize(matrix):
    size = matrix.shape[0]
    row = row_of((8, LANES))
    tiles = [matrix[t : t + 8] for t in range(0, size, 8)]
    last = size // 8 - 1

    def whole(x):
        return jnp.broadcast_to(x, (8, LANES))

    def columns_of(q, t):
        return [whole(tiles[q][:, j : j + 1]) for j in range(8 * t, 8 * t + 8)]

    def upper(block):
        return [[whole(block[c][d : d + 1]) if d >= c else None for d in range(8)] for c in range(8)]

    square = upper(columns_of(0, 0))
    columns = {q: columns_of(q, 0) for q in range(1, last + 1)}
    for t in range(last + 1):
        later = range(t + 1, last + 1)
        rows = [whole(tiles[t][c : c + 1]) for c in range(8)]
        block = columns_of(t + 1, t + 1) if t < last else None
        for c in range(8):
            root = lax.rsqrt(square[c][c])
            rows[c] = rows[c] * root
            left = [square[c][d] * root if d > c else None for d in range(8)]
            for d in range(c + 1, 8):
                for e in range(d, 8):
                    square[d][e] = square[d][e] - left[d] * left[e]
                rows[d] = rows[d] - left[d] * rows[c]
            for q in later:
                columns[q][c] = columns[q][c] * root
                for d in range(c + 1, 8):
                    columns[q][d] = columns[q][d] - left[d] * columns[q][c]
        tiles[t] = rows[0]
        for c in range(1, 8):
            tiles[t] = jnp.where(row == c, rows[c], tiles[t])
        if t < last:
            for column in columns[t + 1]:
                block = [block[e] - column * whole(column[e : e + 1]) for e in range(8)]
            square = upper(block)
            for q in later:
                for c in range(8):
                    tiles[q] = tiles[q] - columns[q][c] * rows[c]
            columns = {q: columns_of(q, t + 1) for q in range(t + 2, last + 1)}
    return jnp.concatenate(tiles, axis=0)


def basis_kernel(rank, gram, parts, basis, factor, turned, lower, sems):
    count = factor.shape[0]
    lines = gram.shape[1] // LANES - 1
    row = row_of((lines, LANES))
    body = jnp.zeros((lines, LANES), F32)
    for i in range(lines):
        body = jnp.where(row == i, gram[:, i * LANES : (i + 1) * LANES], body)
    matrix = unpacked(body, gram[:, lines * LANES :])
    row, lane = row_of(matrix.shape), lane_of(matrix.shape)
    matrix = jnp.where(lane == row + count, 1.0, matrix)
    done = factorize(matrix)
    inverse = pltpu.roll(done, count, 1)
    inverse = jnp.where((lane <= row) & (row < rank[0]), inverse, 0.0)
    high = inverse.astype(BF16).astype(F32)
    high, low = (x + pltpu.roll(x, count, 1) for x in (high, inverse - high))
    left = jnp.concatenate([high, low], axis=0).astype(BF16)
    rows = parts.shape[0]
    copies = [pltpu.make_async_copy(lower, factor, sems.at[turned.shape[0]])]
    for c in range(turned.shape[0]):
        lanes = slice(c * LANES, (c + 1) * LANES)
        for r in range(rows):
            part = parts[r, :, lanes]
            value = dot(left, part)
            turned[c, pl.ds(r, count, stride=rows), :] = value[:count] + value[count:]
        copy = pltpu.make_async_copy(turned.at[c], basis.at[:, lanes], sems.at[c])
        copy.start()
        copies.append(copy)
        if c == 0:
            upper = jnp.where((lane < count) & (lane >= row), done, 0.0)
            square = jnp.concatenate([upper, jnp.zeros((LANES - count, LANES), F32)], axis=0)
            lower[...] = square.T[:count, :count]
            copies[0].start()
    for copy in copies:
        copy.wait()


def ring(x, axis, step):
    size = lax.axis_size(axis)
    return lax.ppermute(x, axis, [(i, (i + step) % size) for i in range(size)])


def exchanged(x, odd):
    rows, columns = lax.axis_size("mesh"), lax.axis_size("obs")
    pairs = []
    for i in range(rows):
        partner = i + 1 if i % 2 == odd else i - 1
        for c in range(columns):
            target = partner * columns + c if 0 <= partner < rows else i * columns + (c ^ 1)
            pairs.append((i * columns + c, target))
    return lax.ppermute(x, ("mesh", "obs"), pairs)


def summed(x):
    rows, columns = lax.axis_size("mesh"), lax.axis_size("obs")
    x = x + ring(x, "obs", 1) if columns == 2 else lax.psum(x, "obs")
    if rows & (rows - 1):
        return lax.psum(x, "mesh")
    rounds = [(4,)] if rows > 4 else []
    rounds += [(1, 3, 2) if rows > 2 else (1,)] if rows > 1 else []
    rounds += [(1 << bit,) for bit in range(3, rows.bit_length() - 1)]
    for offsets in rounds:
        pieces = [
            lax.ppermute(
                x,
                ("mesh", "obs"),
                [
                    (i * columns + c, (i ^ offset) * columns + (c ^ 1))
                    for i in range(rows)
                    for c in range(columns)
                ],
            )
            for offset in offsets
        ]
        for piece in pieces:
            x = x + piece
    return x


def both_sides(x):
    other = ring(x, "obs", 1)
    return other, (other if lax.axis_size("obs") == 2 else ring(x, "obs", -1))


def all_shares(x, sides):
    size = lax.axis_size("obs")
    if size == 2:
        return [x, sides[0]]
    gathered = lax.all_gather(x, "obs")
    here = lax.axis_index("obs")
    return [lax.dynamic_index_in_dim(gathered, (here + i) % size, 0, False) for i in range(size)]


def per_device(probes, velocity, viscosity, friction, obs_block, obs_weight, obs_prec, rank):
    count, rows, width = probes.shape
    share = obs_weight.shape[1]
    mesh_size, obs_size = lax.axis_size("mesh"), lax.axis_size("obs")
    slab_columns = width * obs_size // LANES
    cells = rows * width * mesh_size * obs_size
    height = count + PAD

    payload = (2 * count + share // 2 + 16, width)
    turned = (width // LANES, rows * count, LANES)
    omega, first, second, grid, owned = call(
        edges_kernel,
        [
            (turned, F32),
            (payload, BF16),
            (payload, BF16),
            ((3, rows, width), F32),
            ((share + PAD, LANES), F32),
        ],
        (probes, velocity, viscosity, friction, obs_weight, obs_block, obs_prec),
        [
            pltpu.VMEM(probes.shape, probes.dtype),
            pltpu.VMEM(obs_block.shape, obs_block.dtype),
            pltpu.VMEM(obs_prec.shape, F32),
            pltpu.VMEM((16, width), F32),
            pltpu.SemaphoreType.DMA((7,)),
        ],
        space=pltpu.HBM,
        name="edges",
    )
    arrived = exchanged(first, 0), exchanged(second, 1)

    forced, sent = call(
        forced_kernel,
        [((rows, height, width), F32), ((height + share + PAD, LANES), F32)],
        (omega, grid, owned),
        name="forced",
    )
    sides = both_sides(sent)
    observed = all_shares(sent, sides)
    inner, inner_edges = call(
        functools.partial(inner_kernel, slab_columns, share),
        [(((rows - 2) * count, width), F32), ((count, LANES), F32)],
        (forced, grid, *sides, *observed),
        name="inner",
    )
    (middle,) = call(
        middle_kernel,
        [(((rows - 2) * count, width), F32)],
        (forced, omega, grid, *sides, inner),
        name="middle",
    )
    near, far_sent = call(
        functools.partial(far_kernel, count, share),
        [((2, height, width), F32), ((height + 2 * (share + PAD), LANES), F32)],
        (*arrived, middle),
        name="far",
    )
    far_sides = both_sides(far_sent)
    far_observed = all_shares(far_sent, far_sides)
    outer, source_sent, beside = call(
        functools.partial(outer_kernel, slab_columns, share),
        [((2 * count, width), F32), ((count, LANES), F32), ((2 * count, width), F32)],
        (forced, near, grid, *sides, inner_edges, *arrived, *observed),
        name="outer",
    )
    source_sides = both_sides(source_sent)
    (halo,) = call(
        functools.partial(halo_kernel, slab_columns, share, rows),
        [((2 * count, width), F32)],
        (near, beside, *far_sides, *far_observed),
        name="halo",
    )
    parts, gram = call(
        functools.partial(sketch_kernel, cells),
        [((rows, 2 * count, width), BF16), ((1, 17 * LANES), F32)],
        (forced, near, omega, grid, *sides, *source_sides, inner, outer, halo, middle),
        name="sketch",
    )
    gram = summed(gram)
    basis, factor = pl.pallas_call(
        basis_kernel,
        out_shape=[
            jax.ShapeDtypeStruct((count * rows, width), F32),
            jax.ShapeDtypeStruct((count, count), F32),
        ],
        in_specs=[pl.BlockSpec(memory_space=pltpu.SMEM)] + [pl.BlockSpec(memory_space=pltpu.VMEM)] * 2,
        out_specs=[pl.BlockSpec(memory_space=pl.ANY)] * 2,
        scratch_shapes=[
            pltpu.VMEM(turned, F32),
            pltpu.VMEM((count, count), F32),
            pltpu.SemaphoreType.DMA((width // LANES + 1,)),
        ],
        compiler_params=pltpu.CompilerParams(vmem_limit_bytes=8 * 2**20),
        name="basis",
    )(rank, gram, parts)
    return basis.reshape(count, rows, width), factor


def solution(mesh):
    in_specs = (
        P(None, "mesh", "obs"),
        P("mesh", "obs"),
        P("mesh", "obs"),
        P("mesh", "obs"),
        P("mesh", "obs"),
        P("mesh", "obs", None),
        P("mesh", "obs"),
        P(),
    )
    out_specs = (P(None, "mesh", "obs"), P())
    return jax.shard_map(
        per_device, mesh=mesh, in_specs=in_specs, out_specs=out_specs, check_vma=False
    )
```
